32 devices in a mesh: dp: 8 (over z, x), tensor: 4 (over y, core).
Axes of the slice: x: 2, y: 2, z: 4, core: 2. Of those that a mesh axis runs over, the one named last changes fastest.
Arguments:
- tokens: bfloat16 [9216, 2048], P('dp'), may hold values from -6 to 6
- gain_attn: bfloat16 [2048], P('dp'), may hold values from 0.5 to 1.5
- w_query: bfloat16 [2048, 2048], P('dp', 'tensor'), may hold values from -0.125 to 0.125
- w_key: bfloat16 [2048, 256], P('dp', 'tensor'), may hold values from -0.125 to 0.125
- w_value: bfloat16 [2048, 256], P('dp', 'tensor'), may hold values from -0.125 to 0.125
- w_out: bfloat16 [2048, 2048], P('tensor', 'dp'), may hold values from -1 to 1
- gain_mlp: bfloat16 [2048], P('dp'), may hold values from 0.5 to 1.5
- w_gate: bfloat16 [2048, 5632], P('dp', 'tensor'), may hold values from -0.125 to 0.125
- w_up: bfloat16 [2048, 5632], P('dp', 'tensor'), may hold values from -0.125 to 0.125
- w_down: bfloat16 [5632, 2048], P('tensor', 'dp'), may hold values from -0.078125 to 0.078125
- lengths: int32 [8, 4], P('dp'), may hold values from 1 to 1024, 1152 in all within a row
- cotangent: bfloat16 [9216, 2048], P('dp'), may hold values from -6 to 6
Outputs:
- output: bfloat16 [9216, 2048], P('dp')
- grad_tokens: float32 [9216, 2048], P('dp')
- grad_w_query: float32 [2048, 2048], P('dp', 'tensor')
- grad_w_key: float32 [2048, 256], P('dp', 'tensor')
- grad_w_value: float32 [2048, 256], P('dp', 'tensor')
- grad_w_out: float32 [2048, 2048], P('tensor', 'dp')
- grad_w_gate: float32 [2048, 5632], P('dp', 'tensor')
- grad_w_up: float32 [2048, 5632], P('dp', 'tensor')
- grad_w_down: float32 [5632, 2048], P('tensor', 'dp')
- grad_gain_attn: float32 [2048], P('dp')
- grad_gain_mlp: float32 [2048], P('dp')
The draws below stay inside these ranges and needn't reach their ends.
Inputs may be any that keep to these rules, and one draw needn't show every extreme that they name: Row r lists the lengths of the sequences of data index r, laid one after another in its 1152 tokens; each row sums to 1152 and holds one sequence of 1024.
All inputs are finite; a program needn't handle non-finite values.
Results may differ from the reference program's by a relative error of at most 0.013.
Values may be sent and summed in bfloat16 or wider, within the bound.
A program may use at most 256 MiB of HBM per device.

```python
import math
import jax
import jax.numpy as jnp
import numpy as np
from jax import lax

D = 2048
H = 32
KV = 4
HD = 64
FF = 5632
SEQS = 4
MAXLEN = 1024
TOK_DEV = 1152
TOKENS = 9216
N_DP = 8


def strengthened(entries, rng, source, target, parts, factor):
    owner, partner = [(jnp.arange(entries.shape[dim]) // (entries.shape[dim] // parts)).reshape([-1 if axis == dim else 1 for axis in range(entries.ndim)]) for dim in (source, target)]
    chosen = jax.random.permutation(rng, parts)[partner]
    strong = (owner == chosen) | (owner == (partner + parts // 2) % parts)
    return jnp.where(strong, factor * entries, entries)


def level_of(rng, shape, cuts, smallest, largest):
    level, own = 1.0, jax.random.fold_in(rng, 6)
    for dim, shards_of in cuts:
        draws = jnp.exp(jax.random.uniform(jax.random.fold_in(own, dim), (shards_of,), jnp.float32, smallest / len(cuts), largest / len(cuts)))
        level = level * jnp.repeat(draws, shape[dim] // shards_of).reshape([-1 if axis == dim else 1 for axis in range(len(shape))])
    return level


def profile(count, total, bound, lean):
    loads = [(1 << 20) // math.isqrt(rank ** lean) + 1 for rank in range(2, count + 1)]
    rest, given = total - bound - (count - 1), [1] * (count - 1)
    while rest > 0:
        candidates = [i for i in range(count - 1) if given[i] < bound]
        pool, remaining = sum([loads[i] for i in candidates]), rest
        for i in candidates:
            extra = min(bound - given[i], max(1, remaining * loads[i] // pool), rest)
            given[i] = given[i] + extra
            rest = rest - extra
    return np.array([bound] + given)


def uneven(stream_key, number_of, total, reach, skew):
    if number_of == 2:
        one = jax.random.randint(stream_key, (), max(1, total - reach), min(reach, total - 1) + 1)
        return jnp.stack([one, total - one])
    tallies = jnp.asarray(profile(number_of, total, reach, skew), jnp.int32)
    couples = (number_of - 1) // 2
    source_of, taker = tallies[1:1 + 2 * couples:2], tallies[2:2 + 2 * couples:2]
    room = jnp.minimum(source_of - 1, reach - taker)
    passed = jax.random.randint(jax.random.fold_in(stream_key, 1), (couples,), 0, 1 << 20) % (room + 1)
    tallies = tallies.at[1:1 + 2 * couples:2].set(source_of - passed).at[2:2 + 2 * couples:2].set(taker + passed)
    return tallies[jax.random.permutation(jax.random.fold_in(stream_key, 2), number_of)]


def normal_values(own_key, dims, width, reach, cuts=(), kind=jnp.bfloat16):
    level = level_of(own_key, dims, cuts, -0.22, 0.18) if cuts else 1.0
    values = jax.random.normal(own_key, dims, jnp.float32) * width * level
    return jnp.minimum(jnp.maximum(values, -reach), reach).astype(kind)


def bell_draw_with(own_key, shape, spread, most, shards, heavy, kind=jnp.bfloat16):
    entries = spread * jax.random.normal(own_key, shape, jnp.float32)
    if shards:
        entries = entries * level_of(own_key, shape, shards, -0.22, 0.18)
    return jnp.clip(strengthened(entries, jax.random.fold_in(own_key, 3), *heavy), -most, most).astype(kind)


def setup_inputs(seed: int = 0) -> dict:
    streams_of = jax.random.split(jax.random.key(seed), 13)
    tokens = bell_draw_with(streams_of[0], (TOKENS, D), 1.0, 6.0, ((0, 8),), (0, 1, 8, 2.0))
    gain_attn = jnp.clip(1.0 + 0.1 * jax.random.normal(streams_of[1], (D,), jnp.float32), 0.5, 1.5).astype(jnp.bfloat16)
    w_query = normal_values(streams_of[2], (D, H * HD), D ** -0.5, 0.125, ((0, 8), (1, 4)))
    w_key = normal_values(streams_of[3], (D, KV * HD), D ** -0.5, 0.125, ((0, 8), (1, 4)))
    w_value = normal_values(streams_of[4], (D, KV * HD), D ** -0.5, 0.125, ((0, 8), (1, 4)))
    w_out = normal_values(streams_of[5], (H * HD, D), (H * HD // 64) ** -0.5, 1.0, ((0, 4), (1, 8)))
    gain_mlp = jnp.clip(1.0 + 0.1 * jax.random.normal(streams_of[6], (D,), jnp.float32), 0.5, 1.5).astype(jnp.bfloat16)
    w_gate = normal_values(streams_of[7], (D, FF), D ** -0.5, 0.125, ((0, 8), (1, 4)))
    w_up = normal_values(streams_of[8], (D, FF), D ** -0.5, 0.125, ((0, 8), (1, 4)))
    w_down = normal_values(streams_of[9], (FF, D), FF ** -0.5, 0.078125, ((0, 4), (1, 8)))
    lengths = jax.vmap(lambda own: uneven(own, SEQS, TOK_DEV, MAXLEN, 2))(jax.random.split(streams_of[10], N_DP)).reshape((N_DP, SEQS)).astype(jnp.int32)
    cotangent = bell_draw_with(streams_of[11], (TOKENS, D), 1.0, 6.0, ((0, 8),), (0, 1, 8, 2.0))
    return {"tokens": tokens, "gain_attn": gain_attn, "w_query": w_query, "w_key": w_key, "w_value": w_value, "w_out": w_out, "gain_mlp": gain_mlp, "w_gate": w_gate, "w_up": w_up, "w_down": w_down, "lengths": lengths, "cotangent": cotangent}


@jax.custom_vjp
def low(v):
    return lax.optimization_barrier(v.astype(jnp.bfloat16)).astype(jnp.float32)

@jax.custom_vjp
def low_back(v):
    return v

def low_keep(v):
    return (low(v), None)

def low_pass(kept, grad):
    return (grad,)

def back_keep(v):
    return (v, None)

def back_low(kept, grad):
    return (low(grad),)
low.defvjp(low_keep, low_pass)
low_back.defvjp(back_keep, back_low)
norm_eps = 1e-05
rope_base = 10000.0

def exact_dot(left, right):
    return jnp.dot(left, right, precision=lax.Precision.HIGHEST, preferred_element_type=jnp.float32)

def rms_norm(values, gain):
    inverse = lax.rsqrt(lax.optimization_barrier(jnp.mean(values * values, axis=-1, keepdims=True)) + norm_eps)
    return values * inverse * gain

def rotary(values, cosine_table, sine_table):
    half_size = values.shape[-1] // 2
    first_half = values[..., :half_size]
    second_half = values[..., half_size:]
    return jnp.concatenate([first_half * cosine_table - second_half * sine_table, second_half * cosine_table + first_half * sine_table], axis=-1)

def layout(lengths_row, tok_count):
    seq_ends = jnp.cumsum(lengths_row, dtype=jnp.int32)
    seq_starts = seq_ends - lengths_row
    places = jnp.arange(tok_count, dtype=jnp.int32)
    segment = lax.optimization_barrier(jnp.sum((places[:, None] >= seq_ends[None, :]).astype(jnp.int32), axis=1, dtype=jnp.int32))
    chosen = segment[:, None] == jnp.arange(lengths_row.shape[0], dtype=jnp.int32)[None, :]
    position = places - lax.optimization_barrier(jnp.sum(jnp.where(chosen, seq_starts[None, :], 0), axis=1, dtype=jnp.int32))
    return (segment, position)

def rope_tables(position, head_size):
    freqs = rope_base ** (-jnp.arange(head_size // 2, dtype=jnp.float32) * 2.0 / head_size)
    angles = position.astype(jnp.float32)[:, None] * freqs[None, :]
    return (jnp.cos(angles), jnp.sin(angles))

def forward(tokens, gain_attn, w_query, w_key, w_value, w_out, gain_mlp, w_gate, w_up, w_down, segment, cosine_table, sine_table):
    score_scale = HD ** (-0.5)
    group_size = H // KV
    normed = low(rms_norm(tokens, gain_attn))
    query_lin = low_back(exact_dot(normed, w_query)).reshape(N_DP, TOK_DEV, H, HD)
    key_lin = low_back(exact_dot(normed, w_key)).reshape(N_DP, TOK_DEV, KV, HD)
    value_all = low(low_back(exact_dot(normed, w_value))).reshape(N_DP, TOK_DEV, KV, HD)
    queries = low(rotary(query_lin, cosine_table, sine_table))
    key_rot = low(rotary(key_lin, cosine_table, sine_table))

    def attend(packed):
        query_pack, key_pack, value_pack, segment_pack = packed
        places = jnp.arange(TOK_DEV, dtype=jnp.int32)
        allowed = (segment_pack[:, None] == segment_pack[None, :]) & (places[None, :] <= places[:, None])
        key_rep = jnp.repeat(key_pack, group_size, axis=1)
        value_rep = jnp.repeat(value_pack, group_size, axis=1)
        scores = low_back(jnp.einsum('qhd,khd->hqk', query_pack, key_rep, precision=lax.Precision.HIGHEST) * score_scale)
        scores = jnp.where(allowed[None], scores, -1e+30)
        attn_probs = low(jax.nn.softmax(scores, axis=-1))
        return jnp.einsum('hqk,khd->qhd', attn_probs, value_rep, precision=lax.Precision.HIGHEST)
    attended = lax.map(jax.checkpoint(attend), (queries, key_rot, value_all, segment))
    attn_out = low(low_back(attended.reshape(TOKENS, H * HD)))
    hidden = tokens + low_back(exact_dot(attn_out, w_out))
    normed_mlp = low(rms_norm(hidden, gain_mlp))
    gate_proj = low_back(exact_dot(normed_mlp, w_gate))
    up_proj = low_back(exact_dot(normed_mlp, w_up))
    inner = low(jax.nn.silu(gate_proj) * up_proj)
    return hidden + low_back(exact_dot(inner, w_down))

def reference(tokens, gain_attn, w_query, w_key, w_value, w_out, gain_mlp, w_gate, w_up, w_down, lengths, cotangent):

    def layout_row(lengths_row):
        return layout(lengths_row, TOK_DEV)
    segment, position = jax.vmap(layout_row)(lengths)
    cosine_table, sine_table = rope_tables(position.reshape(-1), HD)
    cosine_table = cosine_table.reshape(N_DP, TOK_DEV, 1, HD // 2)
    sine_table = sine_table.reshape(N_DP, TOK_DEV, 1, HD // 2)
    floats = tuple((array.astype(jnp.float32) for array in (tokens, gain_attn, w_query, w_key, w_value, w_out, gain_mlp, w_gate, w_up, w_down)))

    def apply(*arrays):
        return forward(*arrays, segment, cosine_table, sine_table)
    result, pull = jax.vjp(apply, *floats)
    grads = pull(cotangent.astype(jnp.float32))
    return (result.astype(jnp.bfloat16), grads[0], grads[2], grads[3], grads[4], grads[5], grads[7], grads[8], grads[9], grads[1], grads[6])
```

```python
import functools

import jax
import jax.numpy as jnp
from jax import lax
from jax.experimental import pallas as pl
from jax.experimental.pallas import tpu as pltpu
from jax.sharding import PartitionSpec as P

HD = 64
QB = 128


def swap_halves(z):
    lane = lax.broadcasted_iota(jnp.int32, z.shape, 1)
    return jnp.where(lane % HD < HD // 2, pltpu.roll(z, 128 - HD // 2, 1), pltpu.roll(z, HD // 2, 1))


def nt(a, b):
    return lax.dot_general(a, b, (((1,), (1,)), ((), ())), preferred_element_type=jnp.float32)


def attn_fwd_kernel(qkv_ref, cs_ref, sn_ref, start_ref, q_ref, kv_ref, ob_ref, lse_ref, ka, kb, va, vb):
    tok = qkv_ref.shape[0]
    width = q_ref.shape[1]
    pairs = width // 128
    lane = lax.broadcasted_iota(jnp.int32, (tok, 128), 1)
    cs = cs_ref[...]
    sn = sn_ref[...]
    kv = qkv_ref[:, width:]
    krot = kv * cs + swap_halves(kv) * sn
    kvr = jnp.where(lane < HD, krot, kv).astype(jnp.bfloat16)
    kv_ref[...] = kvr
    kvf = kvr.astype(jnp.float32)
    rolled = pltpu.roll(kvf, HD, 1)
    ka[...] = jnp.where(lane < HD, kvf, 0.0).astype(jnp.bfloat16)
    kb[...] = jnp.where(lane < HD, 0.0, rolled).astype(jnp.bfloat16)
    va[...] = jnp.where(lane < HD, rolled, 0.0).astype(jnp.bfloat16)
    vb[...] = jnp.where(lane < HD, 0.0, kvf).astype(jnp.bfloat16)
    for i in range(tok // QB):
        rows = pl.ds(i * QB, QB)
        kp = (i + 1) * QB
        qs = []
        for p in range(pairs):
            z = qkv_ref[rows, p * 128:(p + 1) * 128]
            r = (z * cs_ref[rows, :] + swap_halves(z) * sn_ref[rows, :]).astype(jnp.bfloat16)
            r = (r.astype(jnp.float32) * 0.125).astype(jnp.bfloat16)
            q_ref[rows, p * 128:(p + 1) * 128] = r
            qs.append(r)
        qe = jnp.concatenate(qs, axis=0)
        col = lax.broadcasted_iota(jnp.int32, (QB, kp), 1)
        row = lax.broadcasted_iota(jnp.int32, (QB, kp), 0) + i * QB
        seen = (col <= row) & (col >= start_ref[rows, :])
        bias = jnp.where(seen, 0.0, -1e30)
        total = 0.0
        lse_tile = jnp.zeros((QB, 128), jnp.float32)
        lane_b = lax.broadcasted_iota(jnp.int32, (QB, 128), 1)
        for odd, (k2, v2) in enumerate(((ka, va), (kb, vb))):
            s = nt(qe, k2[:kp, :]).reshape(pairs, QB, kp) + bias[None]
            m = jnp.max(s, axis=-1, keepdims=True)
            e = jnp.exp(s - m)
            l = jnp.sum(e, axis=-1, keepdims=True)
            o = jnp.dot(e.astype(jnp.bfloat16).reshape(pairs * QB, kp), v2[:kp, :], preferred_element_type=jnp.float32)
            total = total + o.reshape(pairs, QB, 128) / l
            lse = m + jnp.log(l)
            for p in range(pairs):
                lse_tile = jnp.where(lane_b == 2 * p + odd, lse[p], lse_tile)
        for p in range(pairs):
            ob_ref[rows, p * 128:(p + 1) * 128] = total[p].astype(jnp.bfloat16)
        lse_ref[:, i * QB:(i + 1) * QB] = jnp.transpose(lse_tile)[: 2 * pairs]


def attn_fwd(qkv, cs, sn, start):
    tok, width = qkv.shape[0], qkv.shape[1] - 128
    heads = width // HD
    vm = pl.BlockSpec(memory_space=pltpu.VMEM)
    flops = 8 * tok * tok * width
    return pl.pallas_call(
        attn_fwd_kernel,
        out_shape=(
            jax.ShapeDtypeStruct((tok, width), jnp.bfloat16),
            jax.ShapeDtypeStruct((tok, 128), jnp.bfloat16),
            jax.ShapeDtypeStruct((tok, width), jnp.bfloat16),
            jax.ShapeDtypeStruct((heads, tok), jnp.float32),
        ),
        in_specs=[vm] * 4,
        out_specs=(vm,) * 4,
        scratch_shapes=[pltpu.VMEM((tok, 128), jnp.bfloat16)] * 4,
        compiler_params=pltpu.CompilerParams(vmem_limit_bytes=48 * 2**20),
        cost_estimate=pl.CostEstimate(flops=flops, bytes_accessed=tok * width * 12, transcendentals=heads * tok * tok // 2),
    )(qkv, cs, sn, start)


def attn_bwd_kernel(q_ref, kv_ref, dob_ref, lse_ref, cs_ref, sn_ref, start_ref, out_ref, ka, kb, va, vb, dk, dv):
    tok, width = q_ref.shape
    pairs = width // 128
    lane = lax.broadcasted_iota(jnp.int32, (tok, 128), 1)
    kvf = kv_ref[...].astype(jnp.float32)
    rolled = pltpu.roll(kvf, HD, 1)
    ka[...] = jnp.where(lane < HD, kvf, 0.0).astype(jnp.bfloat16)
    kb[...] = jnp.where(lane < HD, 0.0, rolled).astype(jnp.bfloat16)
    va[...] = jnp.where(lane < HD, rolled, 0.0).astype(jnp.bfloat16)
    vb[...] = jnp.where(lane < HD, 0.0, kvf).astype(jnp.bfloat16)
    dk[...] = jnp.zeros_like(dk)
    dv[...] = jnp.zeros_like(dv)
    for i in range(tok // QB):
        rows = pl.ds(i * QB, QB)
        kp = (i + 1) * QB
        qe = jnp.concatenate([q_ref[rows, p * 128:(p + 1) * 128] for p in range(pairs)], axis=0)
        de = jnp.concatenate([dob_ref[rows, p * 128:(p + 1) * 128] for p in range(pairs)], axis=0)
        key = lax.broadcasted_iota(jnp.int32, (kp, QB), 0)
        query = lax.broadcasted_iota(jnp.int32, (kp, QB), 1) + i * QB
        seen = (key <= query) & (key >= start_ref[:, i * QB:(i + 1) * QB])
        bias = jnp.where(seen, 0.0, -1e30)
        bias = jnp.concatenate([bias] * pairs, axis=1)
        dq = 0.0
        parts = []
        for odd, (k2, v2) in enumerate(((ka, va), (kb, vb))):
            lse = jnp.concatenate([lse_ref[2 * p + odd:2 * p + odd + 1, i * QB:(i + 1) * QB] for p in range(pairs)], axis=1)
            s = nt(k2[:kp, :], qe)
            pt = jnp.exp(s + bias - lse)
            dp = nt(v2[:kp, :], de)
            delta = jnp.sum(pt * dp, axis=0, keepdims=True)
            ds = (pt * (dp - delta)).astype(jnp.bfloat16)
            dvo = jnp.dot(pt.astype(jnp.bfloat16), de, preferred_element_type=jnp.float32)
            dko = jnp.dot(ds, qe, preferred_element_type=jnp.float32)
            parts.append((dko, dvo))
            dq = dq + lax.dot_general(ds, k2[:kp, :], (((0,), (0,)), ((), ())), preferred_element_type=jnp.float32)
        lk = lane[:kp]
        dk[:kp, :] += jnp.where(lk < HD, parts[0][0], parts[1][0])
        dv[:kp, :] += jnp.where(lk < HD, parts[0][1], parts[1][1])
        cs = cs_ref[rows, :]
        sn = sn_ref[rows, :]
        for p in range(pairs):
            y = dq[p * QB:(p + 1) * QB] * 0.125
            out_ref[rows, p * 128:(p + 1) * 128] = (y * cs - swap_halves(y) * sn).astype(jnp.bfloat16)
    dkf = dk[...]
    dkf = dkf + pltpu.roll(dkf, HD, 1)
    dkf = dkf * cs_ref[...] - swap_halves(dkf) * sn_ref[...]
    dvf = dv[...]
    dvf = dvf + pltpu.roll(dvf, HD, 1)
    out_ref[:, width:] = jnp.where(lane < HD, dkf, dvf).astype(jnp.bfloat16)


def attn_bwd(q, kv, dob, lse, cs, sn, start_row):
    tok, width = q.shape
    heads = width // HD
    vm = pl.BlockSpec(memory_space=pltpu.VMEM)
    return pl.pallas_call(
        attn_bwd_kernel,
        out_shape=jax.ShapeDtypeStruct((tok, width + 128), jnp.bfloat16),
        in_specs=[vm] * 7,
        out_specs=vm,
        scratch_shapes=[pltpu.VMEM((tok, 128), jnp.bfloat16)] * 4 + [pltpu.VMEM((tok, 128), jnp.float32)] * 2,
        compiler_params=pltpu.CompilerParams(vmem_limit_bytes=48 * 2**20),
        cost_estimate=pl.CostEstimate(flops=20 * tok * tok * width, bytes_accessed=tok * width * 8, transcendentals=heads * tok * tok // 2),
    )(q, kv, dob, lse, cs, sn, start_row)


norm_eps = 1e-05
rope_base = 10000.0
bf16 = jnp.bfloat16
f32 = jnp.float32


def mm(a, b):
    return jnp.dot(a, b, preferred_element_type=f32)


def mm_nt(a, b):
    return lax.dot_general(a, b, (((1,), (1,)), ((), ())), preferred_element_type=f32)


def mm_tn(a, b):
    return lax.dot_general(a, b, (((0,), (0,)), ((), ())), preferred_element_type=f32)


def prep_kernel(q_ref, k_ref, v_ref, o_ref, d_ref, g1_ref, g2_ref, qkv_ref, ot_ref, dt_ref):
    rows, cols = q_ref.shape
    qkv_ref[:rows, :cols] = q_ref[...]
    qkv_ref[:rows, cols:] = jnp.concatenate([k_ref[...], v_ref[...]], axis=1)
    qkv_ref[rows:, :] = jnp.zeros((16, qkv_ref.shape[1]), bf16)
    gains = jnp.concatenate([g1_ref[...], g2_ref[...]], axis=1).astype(f32)
    qkv_ref[rows:, : 2 * rows] = jnp.broadcast_to(gains, (16, 2 * rows)).astype(bf16)
    ot_ref[...] = jnp.transpose(o_ref[...].astype(f32)).astype(bf16)
    dt_ref[...] = jnp.transpose(d_ref[...].astype(f32)).astype(bf16)


def prep(w_query, w_key, w_value, w_out, w_down, gain_attn, gain_mlp):
    rows, cols = w_query.shape
    vm = pl.BlockSpec(memory_space=pltpu.VMEM)
    return pl.pallas_call(
        prep_kernel,
        out_shape=(
            jax.ShapeDtypeStruct((rows + 16, cols + 128), bf16),
            jax.ShapeDtypeStruct(w_out.shape[::-1], bf16),
            jax.ShapeDtypeStruct(w_down.shape[::-1], bf16),
        ),
        in_specs=[vm] * 7,
        out_specs=(vm,) * 3,
        compiler_params=pltpu.CompilerParams(vmem_limit_bytes=32 * 2**20),
    )(w_query, w_key, w_value, w_out, w_down, gain_attn.reshape(1, -1), gain_mlp.reshape(1, -1))


def norm_back(grad_normed, scaled, inverse, gain):
    grad_gain = jnp.sum(grad_normed * scaled, axis=0)
    grad_scaled = grad_normed * gain.astype(f32)
    mixing = jnp.mean(grad_scaled * scaled, axis=-1, keepdims=True)
    return (inverse * (grad_scaled - scaled * mixing), grad_gain)


def per_device(
    n_dp,
    tokens,
    gain_attn,
    w_query,
    w_key,
    w_value,
    w_out,
    gain_mlp,
    w_gate,
    w_up,
    w_down,
    lengths,
    cotangent,
):
    tok, width = tokens.shape
    line = n_dp // 2
    block = width // n_dp
    quarter = tok // 4
    cols = w_query.shape[1]
    dp = lax.axis_index("dp")
    x = dp % 2
    t = lax.axis_index("tensor")
    c, y = t % 2, t // 2
    mine = (2 * c + y) * quarter
    line_groups = [list(range(0, n_dp, 2)), list(range(1, n_dp, 2))]
    pair = [(i, i ^ 1) for i in range(n_dp)]
    core_perm = [(i, i ^ 1) for i in range(4)]
    y_perm = [(i, i ^ 2) for i in range(4)]

    def along_line(a):
        return lax.all_gather(a, "dp", axis=0, tiled=True, axis_index_groups=line_groups)

    def gather(shard):
        rows = shard.shape[0]
        own = along_line(shard)
        other = lax.ppermute(own, "dp", pair)
        whole = jnp.zeros((line, 2, rows, shard.shape[1]), bf16)
        whole = lax.dynamic_update_slice(whole, own.reshape(line, 1, rows, -1), (0, x, 0, 0))
        whole = lax.dynamic_update_slice(whole, other.reshape(line, 1, rows, -1), (0, 1 - x, 0, 0))
        return whole.reshape(n_dp, rows, -1)

    def dp_reduce(left, right):
        grad = mm_tn(left, right).astype(bf16).reshape(line, 2, block, -1)
        send = lax.dynamic_slice_in_dim(grad, 1 - x, 1, 1).reshape(line * block, -1)
        recv = lax.ppermute(send, "dp", pair)
        keep = lax.dynamic_slice_in_dim(grad, x, 1, 1).reshape(line * block, -1)
        keep = (keep.astype(f32) + recv.astype(f32)).astype(bf16)
        return lax.psum_scatter(
            keep, "dp", scatter_dimension=0, tiled=True, axis_index_groups=line_groups
        ).astype(f32)

    def rows_of(a, first, count):
        return lax.dynamic_slice_in_dim(a, first * quarter, count * quarter, 0)

    def tp_reduce(left, right):
        send = mm_nt(rows_of(left, 2 * (1 - c), 2), right).astype(bf16)
        recv = lax.ppermute(send, "tensor", core_perm)
        keep = mm_nt(rows_of(left, 2 * c, 2), right) + recv.astype(f32)
        recv = lax.ppermute(rows_of(keep, 1 - y, 1).astype(bf16), "tensor", y_perm)
        return rows_of(keep, y, 1) + recv.astype(f32)

    def tp_gather(own, dtype=bf16):
        near = lax.ppermute(own, "tensor", core_perm)
        far = lax.ppermute(own, "tensor", y_perm)
        diagonal = lax.ppermute(far, "tensor", core_perm)
        whole = jnp.zeros((tok, own.shape[1]), dtype)
        for i, j, part in ((0, 0, own), (1, 0, near), (0, 1, far), (1, 1, diagonal)):
            place = (2 * (c ^ i) + (y ^ j)) * quarter
            whole = lax.dynamic_update_slice(whole, part.astype(dtype), (place, 0))
        return whole

    p_qkv, p_out, p_down = prep(w_query, w_key, w_value, w_out, w_down, gain_attn, gain_mlp)
    w_qkv = gather(p_qkv)
    gain_one = w_qkv[:, block, :block].reshape(-1)
    gain_two = w_qkv[:, block, block : 2 * block].reshape(-1)
    w_qkv = w_qkv[:, :block].reshape(width, -1)
    w_out_t = gather(p_out).reshape(width, -1)
    w_g = gather(w_gate).reshape(width, -1)
    w_u = gather(w_up).reshape(width, -1)
    w_down_t = gather(p_down).reshape(width, -1)

    ends = jnp.cumsum(lengths[0], dtype=jnp.int32)
    starts = ends - lengths[0]
    places = jnp.arange(tok, dtype=jnp.int32)
    inside = (places[:, None] >= starts[None, :]) & (places[:, None] < ends[None, :])
    start = jnp.sum(jnp.where(inside, starts[None, :], 0), axis=1, dtype=jnp.int32)
    freqs = rope_base ** (-jnp.arange(HD // 2, dtype=f32) * 2.0 / HD)
    angles = (places - start).astype(f32)[:, None] * freqs[None, :]
    cosine, sine = jnp.cos(angles), jnp.sin(angles)
    cs = jnp.concatenate([cosine] * 4, axis=1)
    sn = jnp.concatenate([-sine, sine, -sine, sine], axis=1)

    token_f = tokens.astype(f32)
    inverse_one = lax.rsqrt(jnp.mean(token_f * token_f, axis=-1, keepdims=True) + norm_eps)
    normed_one = (token_f * inverse_one * gain_one.astype(f32)).astype(bf16)
    qkv = mm(normed_one, w_qkv)
    q, kv, attn_b, lse = attn_fwd(qkv, cs, sn, start[:, None])
    token_q = lax.dynamic_slice_in_dim(tokens, mine, quarter, 0).astype(f32)
    hidden = token_q + tp_reduce(attn_b, w_out_t)
    inverse_two = lax.rsqrt(jnp.mean(hidden * hidden, axis=-1, keepdims=True) + norm_eps)
    scaled_two = hidden * inverse_two
    normed_two = tp_gather((scaled_two * gain_two.astype(f32)).astype(bf16))
    gate = mm(normed_two, w_g)
    up = mm(normed_two, w_u)
    sig = jax.nn.sigmoid(gate)
    inner = (gate * sig * up).astype(bf16)
    grad_inner = mm(cotangent, w_down_t)
    grad_gate = (grad_inner * up * sig * (1.0 + gate * (1.0 - sig))).astype(bf16)
    grad_up = (grad_inner * gate * sig).astype(bf16)
    shard_down = dp_reduce(cotangent, inner).T
    out_q = hidden + tp_reduce(inner, w_down_t)
    output = tp_gather(out_q.astype(bf16))
    grad_gu = jnp.concatenate([grad_gate, grad_up], axis=1)
    grad_normed_two = tp_reduce(grad_gu, jnp.concatenate([w_g, w_u], axis=1))
    shard_gate = dp_reduce(normed_two, grad_gate)
    shard_up = dp_reduce(normed_two, grad_up)
    grad_scaled, gain_grad_two = norm_back(grad_normed_two, scaled_two, inverse_two, gain_two)
    cot_q = lax.dynamic_slice_in_dim(cotangent, mine, quarter, 0).astype(f32)
    grad_hidden = cot_q + grad_scaled
    grad_attn = tp_gather(grad_hidden.astype(bf16))
    grad_heads = mm(grad_attn, w_out_t).astype(bf16)
    grad_qkv = attn_bwd(q, kv, grad_heads, lse, cs, sn, start[None, :])
    shard_out = dp_reduce(grad_attn, attn_b).T
    grad_normed_one = tp_reduce(grad_qkv, w_qkv)
    shard_qkv = dp_reduce(normed_one, grad_qkv)
    inverse_q = lax.rsqrt(jnp.mean(token_q * token_q, axis=-1, keepdims=True) + norm_eps)
    grad_scaled, gain_grad_one = norm_back(grad_normed_one, token_q * inverse_q, inverse_q, gain_one)
    grad_tokens = tp_gather((grad_hidden + grad_scaled).astype(bf16), f32)
    gain_grads = jnp.stack([gain_grad_one, gain_grad_two])
    for perm in (core_perm, y_perm):
        gain_grads = gain_grads + lax.ppermute(gain_grads, "tensor", perm)
    step = 1
    while step < n_dp:
        gain_grads = gain_grads + lax.ppermute(gain_grads, "dp", [(i, i ^ step) for i in range(n_dp)])
        step *= 2
    gain_grads = lax.dynamic_slice_in_dim(gain_grads, dp * block, block, 1)
    return (
        output,
        grad_tokens,
        shard_qkv[:, :cols],
        shard_qkv[:, cols : cols + HD],
        shard_qkv[:, cols + HD :],
        shard_out,
        shard_gate,
        shard_up,
        shard_down,
        gain_grads[0],
        gain_grads[1],
    )


def solution(mesh):
    placed = (
        P("dp", None),
        P("dp"),
        P("dp", "tensor"),
        P("dp", "tensor"),
        P("dp", "tensor"),
        P("tensor", "dp"),
        P("dp"),
        P("dp", "tensor"),
        P("dp", "tensor"),
        P("tensor", "dp"),
        P("dp", None),
        P("dp", None),
    )
    return jax.shard_map(
        functools.partial(per_device, mesh.shape["dp"]),
        mesh=mesh,
        in_specs=placed,
        out_specs=(
            P("dp", None),
            P("dp", None),
            P("dp", "tensor"),
            P("dp", "tensor"),
            P("dp", "tensor"),
            P("tensor", "dp"),
            P("dp", "tensor"),
            P("dp", "tensor"),
            P("tensor", "dp"),
            P("dp"),
            P("dp"),
        ),
        check_vma=False,
    )
```

```python
import functools

import jax
import jax.numpy as jnp
from jax import lax
from jax.experimental import pallas as pl
from jax.experimental.pallas import tpu as pltpu
from jax.sharding import PartitionSpec as P

HD = 64
QB = 128


def swap_halves(z):
    lane = lax.broadcasted_iota(jnp.int32, z.shape, 1)
    return jnp.where(lane % HD < HD // 2, pltpu.roll(z, 128 - HD // 2, 1), pltpu.roll(z, HD // 2, 1))


def nt(a, b):
    return lax.dot_general(a, b, (((1,), (1,)), ((), ())), preferred_element_type=jnp.float32)


def attn_forward(qkv_ref, cs_ref, sn_ref, start_ref, q_ref, kv_ref, ob_ref, lse_ref, ka, kb, va, vb, between=()):
    tok = qkv_ref.shape[0]
    width = q_ref.shape[1]
    pairs = width // 128
    lane = lax.broadcasted_iota(jnp.int32, (tok, 128), 1)
    cs = cs_ref[...]
    sn = sn_ref[...]
    kv = qkv_ref[:, width:]
    krot = kv * cs + swap_halves(kv) * sn
    kvr = jnp.where(lane < HD, krot, kv).astype(jnp.bfloat16)
    kv_ref[...] = kvr
    kvf = kvr.astype(jnp.float32)
    rolled = pltpu.roll(kvf, HD, 1)
    ka[...] = jnp.where(lane < HD, kvf, 0.0).astype(jnp.bfloat16)
    kb[...] = jnp.where(lane < HD, 0.0, rolled).astype(jnp.bfloat16)
    va[...] = jnp.where(lane < HD, rolled, 0.0).astype(jnp.bfloat16)
    vb[...] = jnp.where(lane < HD, 0.0, kvf).astype(jnp.bfloat16)
    for i in range(tok // QB):
        rows = pl.ds(i * QB, QB)
        kp = (i + 1) * QB
        qs = []
        for p in range(pairs):
            z = qkv_ref[rows, p * 128:(p + 1) * 128]
            r = (z * cs_ref[rows, :] + swap_halves(z) * sn_ref[rows, :]).astype(jnp.bfloat16)
            r = (r.astype(jnp.float32) * 0.125).astype(jnp.bfloat16)
            q_ref[rows, p * 128:(p + 1) * 128] = r
            qs.append(r)
        qe = jnp.concatenate(qs, axis=0)
        col = lax.broadcasted_iota(jnp.int32, (QB, kp), 1)
        row = lax.broadcasted_iota(jnp.int32, (QB, kp), 0) + i * QB
        seen = (col <= row) & (col >= start_ref[rows, :])
        bias = jnp.where(seen, 0.0, -1e30)
        total = 0.0
        lse_tile = jnp.zeros((QB, 128), jnp.float32)
        lane_b = lax.broadcasted_iota(jnp.int32, (QB, 128), 1)
        for odd, (k2, v2) in enumerate(((ka, va), (kb, vb))):
            s = nt(qe, k2[:kp, :]).reshape(pairs, QB, kp) + bias[None]
            m = jnp.max(s, axis=-1, keepdims=True)
            e = jnp.exp(s - m)
            l = jnp.sum(e, axis=-1, keepdims=True)
            o = jnp.dot(e.astype(jnp.bfloat16).reshape(pairs * QB, kp), v2[:kp, :], preferred_element_type=jnp.float32)
            total = total + o.reshape(pairs, QB, 128) / l
            lse = m + jnp.log(l)
            for p in range(pairs):
                lse_tile = jnp.where(lane_b == 2 * p + odd, lse[p], lse_tile)
        for p in range(pairs):
            ob_ref[rows, p * 128:(p + 1) * 128] = total[p].astype(jnp.bfloat16)
        lse_ref[:, i * QB:(i + 1) * QB] = jnp.transpose(lse_tile)[: 2 * pairs]
        if i in between:
            between[i]()


def attn_bwd_kernel(q_ref, kv_ref, dob_ref, lse_ref, cs_ref, sn_ref, start_ref, out_ref, ka, kb, va, vb, dk, dv):
    tok, width = q_ref.shape
    pairs = width // 128
    lane = lax.broadcasted_iota(jnp.int32, (tok, 128), 1)
    kvf = kv_ref[...].astype(jnp.float32)
    rolled = pltpu.roll(kvf, HD, 1)
    ka[...] = jnp.where(lane < HD, kvf, 0.0).astype(jnp.bfloat16)
    kb[...] = jnp.where(lane < HD, 0.0, rolled).astype(jnp.bfloat16)
    va[...] = jnp.where(lane < HD, rolled, 0.0).astype(jnp.bfloat16)
    vb[...] = jnp.where(lane < HD, 0.0, kvf).astype(jnp.bfloat16)
    dk[...] = jnp.zeros_like(dk)
    dv[...] = jnp.zeros_like(dv)
    for i in range(tok // QB):
        rows = pl.ds(i * QB, QB)
        kp = (i + 1) * QB
        qe = jnp.concatenate([q_ref[rows, p * 128:(p + 1) * 128] for p in range(pairs)], axis=0)
        de = jnp.concatenate([dob_ref[rows, p * 128:(p + 1) * 128] for p in range(pairs)], axis=0)
        key = lax.broadcasted_iota(jnp.int32, (kp, QB), 0)
        query = lax.broadcasted_iota(jnp.int32, (kp, QB), 1) + i * QB
        seen = (key <= query) & (key >= start_ref[:, i * QB:(i + 1) * QB])
        bias = jnp.where(seen, 0.0, -1e30)
        bias = jnp.concatenate([bias] * pairs, axis=1)
        dq = 0.0
        parts = []
        for odd, (k2, v2) in enumerate(((ka, va), (kb, vb))):
            lse = jnp.concatenate([lse_ref[2 * p + odd:2 * p + odd + 1, i * QB:(i + 1) * QB] for p in range(pairs)], axis=1)
            s = nt(k2[:kp, :], qe)
            pt = jnp.exp(s + bias - lse)
            dp = nt(v2[:kp, :], de)
            delta = jnp.sum(pt * dp, axis=0, keepdims=True)
            ds = (pt * (dp - delta)).astype(jnp.bfloat16)
            dvo = jnp.dot(pt.astype(jnp.bfloat16), de, preferred_element_type=jnp.float32)
            dko = jnp.dot(ds, qe, preferred_element_type=jnp.float32)
            parts.append((dko, dvo))
            dq = dq + lax.dot_general(ds, k2[:kp, :], (((0,), (0,)), ((), ())), preferred_element_type=jnp.float32)
        lk = lane[:kp]
        dk[:kp, :] += jnp.where(lk < HD, parts[0][0], parts[1][0])
        dv[:kp, :] += jnp.where(lk < HD, parts[0][1], parts[1][1])
        cs = cs_ref[rows, :]
        sn = sn_ref[rows, :]
        for p in range(pairs):
            y = dq[p * QB:(p + 1) * QB] * 0.125
            out_ref[rows, p * 128:(p + 1) * 128] = (y * cs - swap_halves(y) * sn).astype(jnp.bfloat16)
    dkf = dk[...]
    dkf = dkf + pltpu.roll(dkf, HD, 1)
    dkf = dkf * cs_ref[...] - swap_halves(dkf) * sn_ref[...]
    dvf = dv[...]
    dvf = dvf + pltpu.roll(dvf, HD, 1)
    out_ref[:, width:] = jnp.where(lane < HD, dkf, dvf).astype(jnp.bfloat16)


def attn_bwd(q, kv, dob, lse, cs, sn, start_row):
    tok, width = q.shape
    heads = width // HD
    vm = pl.BlockSpec(memory_space=pltpu.VMEM)
    return pl.pallas_call(
        attn_bwd_kernel,
        out_shape=jax.ShapeDtypeStruct((tok, width + 128), jnp.bfloat16),
        in_specs=[vm] * 7,
        out_specs=vm,
        scratch_shapes=[pltpu.VMEM((tok, 128), jnp.bfloat16)] * 4 + [pltpu.VMEM((tok, 128), jnp.float32)] * 2,
        compiler_params=pltpu.CompilerParams(vmem_limit_bytes=48 * 2**20),
        cost_estimate=pl.CostEstimate(flops=20 * tok * tok * width, bytes_accessed=tok * width * 8, transcendentals=heads * tok * tok // 2),
    )(q, kv, dob, lse, cs, sn, start_row)


norm_eps = 1e-05
rope_base = 10000.0
bf16 = jnp.bfloat16
f32 = jnp.float32


def mm(a, b):
    return jnp.dot(a, b, preferred_element_type=f32)


def mm_nt(a, b):
    return lax.dot_general(a, b, (((1,), (1,)), ((), ())), preferred_element_type=f32)


def mm_tn(a, b):
    return lax.dot_general(a, b, (((0,), (0,)), ((), ())), preferred_element_type=f32)


MESH = pl.DeviceIdType.MESH


def ring_place(n, index):
    odd = index % 2
    return (1 - odd) * (index // 2) + odd * (n - 1 - index // 2)


def ring_index(n, place):
    place = (place + 2 * n) % n
    far = place // (n // 2)
    return (1 - far) * 2 * place + far * (2 * (n - 1 - place) + 1)


class Gather:
    def __init__(self, n, chains, send, recv):
        self.n, self.chains, self.send_sem, self.recv_sem = n, chains, send, recv
        self.index = lax.axis_index("dp")
        self.place = ring_place(n, self.index)
        self.up = ring_index(n, self.place + 1)
        self.down = ring_index(n, self.place - 1)
        self.sent, self.events = [], []

    def copy(self, chain, step, way):
        first, whole, *rows = self.chains[chain]
        rows = pl.ds(*rows[way])
        origin = ring_index(self.n, self.place - step if way == 0 else self.place + step)
        place = whole.at[origin, rows]
        return pltpu.make_async_remote_copy(
            src_ref=first.at[rows] if step == 0 else place,
            dst_ref=place,
            send_sem=self.send_sem.at[chain, way, step],
            recv_sem=self.recv_sem.at[chain, way, step],
            device_id={"dp": self.up if way == 0 else self.down},
            device_id_type=MESH,
        )

    def start(self, chain, step):
        for way in (0, 1):
            self.copy(chain, step, way).start()
        self.sent.append((chain, step))

    def order(self, chains):
        self.events += [(chain, step) for step in range(self.n - 1) for chain in chains]

    def pass_on(self, count=1):
        for _ in range(min(count, len(self.events))):
            chain, step = self.events.pop(0)
            for way in (0, 1):
                self.copy(chain, step, way).wait_recv()
            if step + 1 < self.n - 1:
                self.start(chain, step + 1)

    def finish(self):
        for chain, step in self.sent:
            for way in (0, 1):
                self.copy(chain, step, way).wait_send()


def forward_kernel(
    n,
    s_qkv, s_out, s_gate, s_up, s_down, tokens, cs_ref, sn_ref, start_ref,
    w_qkv, w_out, w_gate, w_up, w_down, n1_out, q_ref, kv_ref, ob_ref, lse_ref, hid_ref, n2_out, gate_out, up_out,
    v_qkv, v_out, n1, n2, qkv, ka, kb, va, vb, part, near, keep, far_part, far, own_n2, weight, stage,
    ring_send, ring_recv, tp_send, tp_recv, local,
):
    tok, width = n1.shape
    block = width // n
    quarter = tok // 4
    sub = quarter // 2
    index = lax.axis_index("dp")
    t = lax.axis_index("tensor")
    c, y = t % 2, t // 2
    mate = y * 2 + (1 - c)
    across = (1 - y) * 2 + c
    h = block // 2
    chains = [
        (s_qkv, v_qkv, (0, h + 16), (h + 16, h)),
        (s_out, v_out, (0, s_out.shape[0] // 2), (s_out.shape[0] // 2, s_out.shape[0] // 2)),
        (s_gate, w_gate, (0, h), (h, h)),
        (s_up, w_up, (0, h), (h, h)),
        (s_down, w_down, (0, h // 2), (h, h // 2)),
        (s_down, w_down, (h // 2, h // 2), (h + h // 2, h // 2)),
    ]
    ring = Gather(n, chains, ring_send, ring_recv)
    barrier = pltpu.get_barrier_semaphore()
    for device in ({"dp": ring.up}, {"dp": ring.down}, {"tensor": mate}, {"tensor": across}):
        pl.semaphore_signal(barrier, inc=1, device_id=device, device_id_type=MESH)

    used = []

    def copy(source, target):
        made = pltpu.make_async_copy(source, target, local.at[len(used)])
        made.start()
        used.append(made)
        return made

    whole = copy(tokens, n2)
    pairs = ((s_qkv, v_qkv), (s_out, v_out), (s_gate, w_gate), (s_up, w_up), (s_down, w_down))
    own = [copy(source, target.at[index]) for source, target in pairs]
    pl.semaphore_wait(barrier, 4)
    ring.start(0, 0)
    ring.start(1, 0)
    ring.order([0, 1])
    whole.wait()
    ring.pass_on(2 * (n - 1) - 2)
    ring.start(2, 0)
    ring.pass_on(1)
    ring.start(3, 0)
    ring.pass_on(1)
    ring.order([2, 3])
    own[0].wait()
    own[1].wait()

    gain_one = v_qkv[:, block : block + 16, :block]
    gain_two = v_qkv[:, block : block + 16, block : 2 * block]
    gains = [[g[i, :1].astype(f32) for i in range(n)] for g in (gain_one, gain_two)]
    gain_one, gain_two = (jnp.concatenate(g, axis=1) for g in gains)
    steps = 4
    rows_each = tok // steps
    for i in range(steps):
        rows = pl.ds(i * rows_each, rows_each)
        z = n2[rows, :].astype(f32)
        inverse = lax.rsqrt(jnp.mean(z * z, axis=-1, keepdims=True) + norm_eps)
        n1[rows, :] = (z * inverse * gain_one).astype(bf16)
        qkv[rows, :] = mm(n1[rows, :], v_qkv[:, :block].reshape(width, qkv.shape[1]))
    saved = [copy(n1, n1_out), copy(v_qkv, w_qkv), copy(v_out, w_out)]
    ring.pass_on()
    attn_forward(qkv, cs_ref, sn_ref, start_ref, q_ref, kv_ref, ob_ref, lse_ref, ka, kb, va, vb, {4: ring.pass_on, 8: ring.pass_on})

    def remote(k, source, target, device):
        made = pltpu.make_async_remote_copy(
            src_ref=source, dst_ref=target, send_sem=tp_send.at[k], recv_sem=tp_recv.at[k],
            device_id={"tensor": device}, device_id_type=MESH,
        )
        made.start()
        return made

    def projected(first):
        rows = pl.ds(pl.multiple_of(first, 16), sub)
        return jnp.concatenate([mm(ob_ref[rows, :], v_out[j]) for j in range(n)], axis=1)

    pieces = [((1 - y) * quarter + i * sub) for i in (0, 1)] + [(y * quarter + i * sub) for i in (0, 1)]
    tp = []
    for i, first in enumerate(pieces):
        part[i * sub : (i + 1) * sub, :] = projected((1 - c) * 2 * quarter + first).astype(bf16)
        tp.append(remote(i, part.at[pl.ds(i * sub, sub)], near.at[pl.ds(i * sub, sub)], mate))
    for i, first in enumerate(pieces):
        mine = projected(c * 2 * quarter + first)
        tp[i].wait_recv()
        total = mine + near[i * sub : (i + 1) * sub, :].astype(f32)
        if i < 2:
            far_part[i * sub : (i + 1) * sub, :] = total.astype(bf16)
            tp.append(remote(4 + i, far_part.at[pl.ds(i * sub, sub)], far.at[pl.ds(i * sub, sub)], across))
        else:
            keep[(i - 2) * sub : (i - 1) * sub, :] = total
    ring.pass_on(2)

    first_row = (2 * c + y) * quarter
    token_rows = copy(tokens.at[pl.ds(pl.multiple_of(first_row, 16), quarter)], own_n2)
    token_rows.wait()
    sent = []
    for i in (0, 1):
        rows = pl.ds(i * sub, sub)
        tp[4 + i].wait_recv()
        hidden = own_n2[rows, :].astype(f32) + keep[rows, :] + far[rows, :].astype(f32)
        hid_ref[rows, :] = hidden
        inverse = lax.rsqrt(jnp.mean(hidden * hidden, axis=-1, keepdims=True) + norm_eps)
        place = pl.ds(pl.multiple_of(first_row + i * sub, 16), sub)
        n2[place, :] = (hidden * inverse * gain_two).astype(bf16)
        sent.append(remote(6 + i, n2.at[place], n2.at[place], across))
        sent.append(remote(8 + i, n2.at[place], n2.at[place], mate))
        ring.pass_on()
    ring.pass_on()
    other_row = (2 * c + 1 - y) * quarter
    for i in (0, 1):
        sent[2 * i].wait_recv()
        place = pl.ds(pl.multiple_of(other_row + i * sub, 16), sub)
        sent.append(remote(10 + i, n2.at[place], n2.at[place], mate))
        ring.pass_on()
    for made in (sent[1], sent[3], sent[4], sent[5]):
        made.wait_recv()
    saved.append(copy(n2, n2_out))
    ring.pass_on(len(ring.events) - 2)
    ring.start(4, 0)
    ring.pass_on(1)
    ring.start(5, 0)
    ring.pass_on(1)
    ring.order([4, 5])
    own[2].wait()
    own[3].wait()

    for source, target in ((w_gate, gate_out), (w_up, up_out)):
        copy(source, weight).wait()
        units = weight.shape[2]
        writes = []
        for j, first in enumerate(range(0, units, 256)):
            wide = min(256, units - first)
            if j >= 2:
                writes[j - 2].wait()
            stage[j % 2, :, :wide] = mm(n2[...], weight[:, :, first : first + wide].reshape(width, wide))
            writes.append(copy(stage.at[j % 2, :, pl.ds(0, wide)], target.at[:, pl.ds(first, wide)]))
            ring.pass_on()
        writes[-2].wait()
        writes[-1].wait()
    ring.pass_on(len(ring.events))
    for made in tp + sent:
        made.wait_send()
    ring.finish()
    own[4].wait()
    for made in saved:
        made.wait()


def forward(n, s_qkv, s_out, s_gate, s_up, s_down, tokens, cs, sn, start):
    tok, width = tokens.shape
    heads = s_qkv.shape[1] - 128
    units = s_gate.shape[1]
    quarter = tok // 4
    vm = pl.BlockSpec(memory_space=pltpu.VMEM)
    anywhere = pl.BlockSpec(memory_space=pl.ANY)
    shards = (s_qkv, s_out, s_gate, s_up, s_down)
    return pl.pallas_call(
        functools.partial(forward_kernel, n),
        out_shape=tuple(jax.ShapeDtypeStruct((n,) + s.shape, bf16) for s in shards)
        + (
            jax.ShapeDtypeStruct((tok, width), bf16),
            jax.ShapeDtypeStruct((tok, heads), bf16),
            jax.ShapeDtypeStruct((tok, 128), bf16),
            jax.ShapeDtypeStruct((tok, heads), bf16),
            jax.ShapeDtypeStruct((heads // HD, tok), f32),
            jax.ShapeDtypeStruct((quarter, width), f32),
            jax.ShapeDtypeStruct((tok, width), bf16),
            jax.ShapeDtypeStruct((tok, units), f32),
            jax.ShapeDtypeStruct((tok, units), f32),
        ),
        in_specs=[anywhere] * 6 + [vm] * 3,
        out_specs=(anywhere,) * 6 + (vm,) * 5 + (anywhere,) * 3,
        scratch_shapes=[
            pltpu.VMEM((n,) + s_qkv.shape, bf16),
            pltpu.VMEM((n,) + s_out.shape, bf16),
            pltpu.VMEM((tok, width), bf16),
            pltpu.VMEM((tok, width), bf16),
            pltpu.VMEM((tok, heads + 128), f32),
            pltpu.VMEM((tok, 128), bf16),
            pltpu.VMEM((tok, 128), bf16),
            pltpu.VMEM((tok, 128), bf16),
            pltpu.VMEM((tok, 128), bf16),
            pltpu.VMEM((2 * quarter, width), bf16),
            pltpu.VMEM((2 * quarter, width), bf16),
            pltpu.VMEM((quarter, width), f32),
            pltpu.VMEM((quarter, width), bf16),
            pltpu.VMEM((quarter, width), bf16),
            pltpu.VMEM((quarter, width), bf16),
            pltpu.VMEM((n,) + s_gate.shape, bf16),
            pltpu.VMEM((2, tok, 256), f32),
            pltpu.SemaphoreType.DMA((6, 2, n - 1)),
            pltpu.SemaphoreType.DMA((6, 2, n - 1)),
            pltpu.SemaphoreType.DMA((12,)),
            pltpu.SemaphoreType.DMA((12,)),
            pltpu.SemaphoreType.DMA((32,)),
        ],
        compiler_params=pltpu.CompilerParams(collective_id=1, has_side_effects=True, vmem_limit_bytes=62 * 2**20),
    )(*shards, tokens, cs, sn, start)


def prep_kernel(q_ref, k_ref, v_ref, d_ref, g1_ref, g2_ref, qkv_ref, dt_ref):
    rows, cols = q_ref.shape
    qkv_ref[:rows, :cols] = q_ref[...]
    qkv_ref[:rows, cols:] = jnp.concatenate([k_ref[...], v_ref[...]], axis=1)
    qkv_ref[rows:, :] = jnp.zeros((16, qkv_ref.shape[1]), bf16)
    gains = jnp.concatenate([g1_ref[...], g2_ref[...]], axis=1).astype(f32)
    qkv_ref[rows:, : 2 * rows] = jnp.broadcast_to(gains, (16, 2 * rows)).astype(bf16)
    dt_ref[...] = jnp.transpose(d_ref[...].astype(f32)).astype(bf16)


def prep(w_query, w_key, w_value, w_down, gain_attn, gain_mlp):
    rows, cols = w_query.shape
    vm = pl.BlockSpec(memory_space=pltpu.VMEM)
    return pl.pallas_call(
        prep_kernel,
        out_shape=(
            jax.ShapeDtypeStruct((rows + 16, cols + 128), bf16),
            jax.ShapeDtypeStruct(w_down.shape[::-1], bf16),
        ),
        in_specs=[vm] * 6,
        out_specs=(vm,) * 2,
        compiler_params=pltpu.CompilerParams(vmem_limit_bytes=32 * 2**20),
    )(w_query, w_key, w_value, w_down, gain_attn.reshape(1, -1), gain_mlp.reshape(1, -1))


def norm_back(grad_normed, scaled, inverse, gain):
    grad_gain = jnp.sum(grad_normed * scaled, axis=0)
    grad_scaled = grad_normed * gain.astype(f32)
    mixing = jnp.mean(grad_scaled * scaled, axis=-1, keepdims=True)
    return (inverse * (grad_scaled - scaled * mixing), grad_gain)


def per_device(
    n_dp,
    tokens,
    gain_attn,
    w_query,
    w_key,
    w_value,
    w_out,
    gain_mlp,
    w_gate,
    w_up,
    w_down,
    lengths,
    cotangent,
):
    tok, width = tokens.shape
    line = n_dp // 2
    block = width // n_dp
    quarter = tok // 4
    cols = w_query.shape[1]
    dp = lax.axis_index("dp")
    x = dp % 2
    t = lax.axis_index("tensor")
    c, y = t % 2, t // 2
    mine = (2 * c + y) * quarter
    line_groups = [list(range(0, n_dp, 2)), list(range(1, n_dp, 2))]
    pair = [(i, i ^ 1) for i in range(n_dp)]
    core_perm = [(i, i ^ 1) for i in range(4)]
    y_perm = [(i, i ^ 2) for i in range(4)]

    def dp_reduce(left, right):
        grad = mm_tn(left, right).astype(bf16).reshape(line, 2, block, -1)
        send = lax.dynamic_slice_in_dim(grad, 1 - x, 1, 1).reshape(line * block, -1)
        recv = lax.ppermute(send, "dp", pair)
        keep = lax.dynamic_slice_in_dim(grad, x, 1, 1).reshape(line * block, -1)
        keep = (keep.astype(f32) + recv.astype(f32)).astype(bf16)
        return lax.psum_scatter(
            keep, "dp", scatter_dimension=0, tiled=True, axis_index_groups=line_groups
        ).astype(f32)

    def rows_of(a, first, count):
        return lax.dynamic_slice_in_dim(a, first * quarter, count * quarter, 0)

    def tp_reduce(left, right):
        send = mm_nt(rows_of(left, 2 * (1 - c), 2), right).astype(bf16)
        recv = lax.ppermute(send, "tensor", core_perm)
        keep = mm_nt(rows_of(left, 2 * c, 2), right) + recv.astype(f32)
        recv = lax.ppermute(rows_of(keep, 1 - y, 1).astype(bf16), "tensor", y_perm)
        return rows_of(keep, y, 1) + recv.astype(f32)

    def tp_gather(own, dtype=bf16):
        near = lax.ppermute(own, "tensor", core_perm)
        far = lax.ppermute(own, "tensor", y_perm)
        diagonal = lax.ppermute(far, "tensor", core_perm)
        whole = jnp.zeros((tok, own.shape[1]), dtype)
        for i, j, part in ((0, 0, own), (1, 0, near), (0, 1, far), (1, 1, diagonal)):
            place = (2 * (c ^ i) + (y ^ j)) * quarter
            whole = lax.dynamic_update_slice(whole, part.astype(dtype), (place, 0))
        return whole

    ends = jnp.cumsum(lengths[0], dtype=jnp.int32)
    starts = ends - lengths[0]
    places = jnp.arange(tok, dtype=jnp.int32)
    inside = (places[:, None] >= starts[None, :]) & (places[:, None] < ends[None, :])
    start = jnp.sum(jnp.where(inside, starts[None, :], 0), axis=1, dtype=jnp.int32)
    freqs = rope_base ** (-jnp.arange(HD // 2, dtype=f32) * 2.0 / HD)
    angles = (places - start).astype(f32)[:, None] * freqs[None, :]
    cosine, sine = jnp.cos(angles), jnp.sin(angles)
    cs = jnp.concatenate([cosine] * 4, axis=1)
    sn = jnp.concatenate([-sine, sine, -sine, sine], axis=1)

    p_qkv, p_down = prep(w_query, w_key, w_value, w_down, gain_attn, gain_mlp)
    w_qkv, w_out_all, w_g, w_u, w_down_t, normed_one, q, kv, attn_b, lse, hidden, normed_two, gate, up = forward(
        n_dp, p_qkv, w_out, w_gate, w_up, p_down, tokens, cs, sn, start[:, None]
    )
    gain_one = w_qkv[:, block, :block].reshape(-1)
    gain_two = w_qkv[:, block, block : 2 * block].reshape(-1)
    w_qkv = w_qkv[:, :block].reshape(width, -1)
    w_out_t = w_out_all.transpose(0, 2, 1).reshape(width, -1)
    w_g = w_g.reshape(width, -1)
    w_u = w_u.reshape(width, -1)
    w_down_t = w_down_t.reshape(width, -1)
    token_q = lax.dynamic_slice_in_dim(tokens, mine, quarter, 0).astype(f32)
    inverse_two = lax.rsqrt(jnp.mean(hidden * hidden, axis=-1, keepdims=True) + norm_eps)
    scaled_two = hidden * inverse_two
    sig = jax.nn.sigmoid(gate)
    inner = (gate * sig * up).astype(bf16)
    grad_inner = mm(cotangent, w_down_t)
    grad_gate = (grad_inner * up * sig * (1.0 + gate * (1.0 - sig))).astype(bf16)
    grad_up = (grad_inner * gate * sig).astype(bf16)
    shard_down = dp_reduce(cotangent, inner).T
    out_q = hidden + tp_reduce(inner, w_down_t)
    output = tp_gather(out_q.astype(bf16))
    grad_gu = jnp.concatenate([grad_gate, grad_up], axis=1)
    grad_normed_two = tp_reduce(grad_gu, jnp.concatenate([w_g, w_u], axis=1))
    shard_gate = dp_reduce(normed_two, grad_gate)
    shard_up = dp_reduce(normed_two, grad_up)
    grad_scaled, gain_grad_two = norm_back(grad_normed_two, scaled_two, inverse_two, gain_two)
    cot_q = lax.dynamic_slice_in_dim(cotangent, mine, quarter, 0).astype(f32)
    grad_hidden = cot_q + grad_scaled
    grad_attn = tp_gather(grad_hidden.astype(bf16))
    grad_heads = mm(grad_attn, w_out_t).astype(bf16)
    grad_qkv = attn_bwd(q, kv, grad_heads, lse, cs, sn, start[None, :])
    shard_out = dp_reduce(grad_attn, attn_b).T
    grad_normed_one = tp_reduce(grad_qkv, w_qkv)
    shard_qkv = dp_reduce(normed_one, grad_qkv)
    inverse_q = lax.rsqrt(jnp.mean(token_q * token_q, axis=-1, keepdims=True) + norm_eps)
    grad_scaled, gain_grad_one = norm_back(grad_normed_one, token_q * inverse_q, inverse_q, gain_one)
    grad_tokens = tp_gather((grad_hidden + grad_scaled).astype(bf16), f32)
    gain_grads = jnp.stack([gain_grad_one, gain_grad_two])
    for perm in (core_perm, y_perm):
        gain_grads = gain_grads + lax.ppermute(gain_grads, "tensor", perm)
    step = 1
    while step < n_dp:
        gain_grads = gain_grads + lax.ppermute(gain_grads, "dp", [(i, i ^ step) for i in range(n_dp)])
        step *= 2
    gain_grads = lax.dynamic_slice_in_dim(gain_grads, dp * block, block, 1)
    return (
        output,
        grad_tokens,
        shard_qkv[:, :cols],
        shard_qkv[:, cols : cols + HD],
        shard_qkv[:, cols + HD :],
        shard_out,
        shard_gate,
        shard_up,
        shard_down,
        gain_grads[0],
        gain_grads[1],
    )


def solution(mesh):
    placed = (
        P("dp", None),
        P("dp"),
        P("dp", "tensor"),
        P("dp", "tensor"),
        P("dp", "tensor"),
        P("tensor", "dp"),
        P("dp"),
        P("dp", "tensor"),
        P("dp", "tensor"),
        P("tensor", "dp"),
        P("dp", None),
        P("dp", None),
    )
    return jax.shard_map(
        functools.partial(per_device, mesh.shape["dp"]),
        mesh=mesh,
        in_specs=placed,
        out_specs=(
            P("dp", None),
            P("dp", None),
            P("dp", "tensor"),
            P("dp", "tensor"),
            P("dp", "tensor"),
            P("tensor", "dp"),
            P("dp", "tensor"),
            P("dp", "tensor"),
            P("tensor", "dp"),
            P("dp"),
            P("dp"),
        ),
        check_vma=False,
    )
```

```python
import functools

import jax
import jax.numpy as jnp
from jax import lax
from jax.experimental import pallas as pl
from jax.experimental.pallas import tpu as pltpu
from jax.sharding import PartitionSpec as P

HD = 64
QB = 128


def swap_halves(z):
    lane = lax.broadcasted_iota(jnp.int32, z.shape, 1)
    return jnp.where(lane % HD < HD // 2, pltpu.roll(z, 128 - HD // 2, 1), pltpu.roll(z, HD // 2, 1))


def nt(a, b):
    return lax.dot_general(a, b, (((1,), (1,)), ((), ())), preferred_element_type=jnp.float32)


def attn_forward(qkv_ref, cs_ref, sn_ref, start_ref, q_ref, kv_ref, ob_ref, lse_ref, ka, kb, va, vb, between=()):
    tok = qkv_ref.shape[0]
    width = q_ref.shape[1]
    pairs = width // 128
    lane = lax.broadcasted_iota(jnp.int32, (tok, 128), 1)
    cs = cs_ref[...]
    sn = sn_ref[...]
    kv = qkv_ref[:, width:]
    krot = kv * cs + swap_halves(kv) * sn
    kvr = jnp.where(lane < HD, krot, kv).astype(jnp.bfloat16)
    kv_ref[...] = kvr
    kvf = kvr.astype(jnp.float32)
    rolled = pltpu.roll(kvf, HD, 1)
    ka[...] = jnp.where(lane < HD, kvf, 0.0).astype(jnp.bfloat16)
    kb[...] = jnp.where(lane < HD, 0.0, rolled).astype(jnp.bfloat16)
    va[...] = jnp.where(lane < HD, rolled, 0.0).astype(jnp.bfloat16)
    vb[...] = jnp.where(lane < HD, 0.0, kvf).astype(jnp.bfloat16)
    for i in range(tok // QB):
        rows = pl.ds(i * QB, QB)
        kp = (i + 1) * QB
        qs = []
        for p in range(pairs):
            z = qkv_ref[rows, p * 128:(p + 1) * 128]
            r = (z * cs_ref[rows, :] + swap_halves(z) * sn_ref[rows, :]).astype(jnp.bfloat16)
            r = (r.astype(jnp.float32) * 0.125).astype(jnp.bfloat16)
            q_ref[rows, p * 128:(p + 1) * 128] = r
            qs.append(r)
        qe = jnp.concatenate(qs, axis=0)
        col = lax.broadcasted_iota(jnp.int32, (QB, kp), 1)
        row = lax.broadcasted_iota(jnp.int32, (QB, kp), 0) + i * QB
        seen = (col <= row) & (col >= start_ref[rows, :])
        bias = jnp.where(seen, 0.0, -1e30)
        total = 0.0
        lse_tile = jnp.zeros((QB, 128), jnp.float32)
        lane_b = lax.broadcasted_iota(jnp.int32, (QB, 128), 1)
        for odd, (k2, v2) in enumerate(((ka, va), (kb, vb))):
            s = nt(qe, k2[:kp, :]).reshape(pairs, QB, kp) + bias[None]
            m = jnp.max(s, axis=-1, keepdims=True)
            e = jnp.exp(s - m)
            l = jnp.sum(e, axis=-1, keepdims=True)
            o = jnp.dot(e.astype(jnp.bfloat16).reshape(pairs * QB, kp), v2[:kp, :], preferred_element_type=jnp.float32)
            total = total + o.reshape(pairs, QB, 128) / l
            lse = m + jnp.log(l)
            for p in range(pairs):
                lse_tile = jnp.where(lane_b == 2 * p + odd, lse[p], lse_tile)
        for p in range(pairs):
            ob_ref[rows, p * 128:(p + 1) * 128] = total[p].astype(jnp.bfloat16)
        lse_ref[:, i * QB:(i + 1) * QB] = jnp.transpose(lse_tile)[: 2 * pairs]
        if i in between:
            between[i]()


def attn_backward(q_ref, kv_ref, dob_ref, lse_ref, cs_ref, sn_ref, start_ref, out_ref, ka, kb, va, vb, dk, dv, between=()):
    tok, width = q_ref.shape
    pairs = width // 128
    lane = lax.broadcasted_iota(jnp.int32, (tok, 128), 1)
    kvf = kv_ref[...].astype(jnp.float32)
    rolled = pltpu.roll(kvf, HD, 1)
    ka[...] = jnp.where(lane < HD, kvf, 0.0).astype(jnp.bfloat16)
    kb[...] = jnp.where(lane < HD, 0.0, rolled).astype(jnp.bfloat16)
    va[...] = jnp.where(lane < HD, rolled, 0.0).astype(jnp.bfloat16)
    vb[...] = jnp.where(lane < HD, 0.0, kvf).astype(jnp.bfloat16)
    dk[...] = jnp.zeros_like(dk)
    dv[...] = jnp.zeros_like(dv)
    for i in range(tok // QB):
        rows = pl.ds(i * QB, QB)
        kp = (i + 1) * QB
        qe = jnp.concatenate([q_ref[rows, p * 128:(p + 1) * 128] for p in range(pairs)], axis=0)
        de = jnp.concatenate([dob_ref[rows, p * 128:(p + 1) * 128] for p in range(pairs)], axis=0)
        key = lax.broadcasted_iota(jnp.int32, (kp, QB), 0)
        query = lax.broadcasted_iota(jnp.int32, (kp, QB), 1) + i * QB
        seen = (key <= query) & (key >= start_ref[:, i * QB:(i + 1) * QB])
        bias = jnp.where(seen, 0.0, -1e30)
        bias = jnp.concatenate([bias] * pairs, axis=1)
        dq = 0.0
        parts = []
        for odd, (k2, v2) in enumerate(((ka, va), (kb, vb))):
            lse = jnp.concatenate([lse_ref[2 * p + odd:2 * p + odd + 1, i * QB:(i + 1) * QB] for p in range(pairs)], axis=1)
            s = nt(k2[:kp, :], qe)
            pt = jnp.exp(s + bias - lse)
            dp = nt(v2[:kp, :], de)
            delta = jnp.sum(pt * dp, axis=0, keepdims=True)
            ds = (pt * (dp - delta)).astype(jnp.bfloat16)
            dvo = jnp.dot(pt.astype(jnp.bfloat16), de, preferred_element_type=jnp.float32)
            dko = jnp.dot(ds, qe, preferred_element_type=jnp.float32)
            parts.append((dko, dvo))
            dq = dq + lax.dot_general(ds, k2[:kp, :], (((0,), (0,)), ((), ())), preferred_element_type=jnp.float32)
        lk = lane[:kp]
        dk[:kp, :] += jnp.where(lk < HD, parts[0][0], parts[1][0])
        dv[:kp, :] += jnp.where(lk < HD, parts[0][1], parts[1][1])
        cs = cs_ref[rows, :]
        sn = sn_ref[rows, :]
        for p in range(pairs):
            y = dq[p * QB:(p + 1) * QB] * 0.125
            out_ref[rows, p * 128:(p + 1) * 128] = (y * cs - swap_halves(y) * sn).astype(jnp.bfloat16)
        if i in between:
            between[i]()
    dkf = dk[...]
    dkf = dkf + pltpu.roll(dkf, HD, 1)
    dkf = dkf * cs_ref[...] - swap_halves(dkf) * sn_ref[...]
    dvf = dv[...]
    dvf = dvf + pltpu.roll(dvf, HD, 1)
    out_ref[:, width:] = jnp.where(lane < HD, dkf, dvf).astype(jnp.bfloat16)


norm_eps = 1e-05
rope_base = 10000.0
bf16 = jnp.bfloat16
f32 = jnp.float32


def mm(a, b):
    return jnp.dot(a, b, preferred_element_type=f32)


def mm_nt(a, b):
    return lax.dot_general(a, b, (((1,), (1,)), ((), ())), preferred_element_type=f32)


def mm_tn(a, b):
    return lax.dot_general(a, b, (((0,), (0,)), ((), ())), preferred_element_type=f32)


MESH = pl.DeviceIdType.MESH


def ring_place(n, index):
    odd = index % 2
    return (1 - odd) * (index // 2) + odd * (n - 1 - index // 2)


def ring_index(n, place):
    place = (place + 2 * n) % n
    far = place // (n // 2)
    return (1 - far) * 2 * place + far * (2 * (n - 1 - place) + 1)


class Gather:
    def __init__(self, n, chains, send, recv):
        self.n, self.chains, self.send_sem, self.recv_sem = n, chains, send, recv
        self.index = lax.axis_index("dp")
        self.place = ring_place(n, self.index)
        self.up = ring_index(n, self.place + 1)
        self.down = ring_index(n, self.place - 1)
        self.sent, self.events = [], []

    def copy(self, chain, step, way):
        first, whole, *rows = self.chains[chain]
        rows = pl.ds(*rows[way])
        origin = ring_index(self.n, self.place - step if way == 0 else self.place + step)
        place = whole.at[origin, rows]
        return pltpu.make_async_remote_copy(
            src_ref=first.at[rows] if step == 0 else place,
            dst_ref=place,
            send_sem=self.send_sem.at[chain, way, step],
            recv_sem=self.recv_sem.at[chain, way, step],
            device_id={"dp": self.up if way == 0 else self.down},
            device_id_type=MESH,
        )

    def start(self, chain, step):
        for way in (0, 1):
            self.copy(chain, step, way).start()
        self.sent.append((chain, step))

    def order(self, chains):
        self.events += [(chain, step) for step in range(self.n - 1) for chain in chains]

    def pass_on(self, count=1):
        for _ in range(min(count, len(self.events))):
            chain, step = self.events.pop(0)
            for way in (0, 1):
                self.copy(chain, step, way).wait_recv()
            if step + 1 < self.n - 1:
                self.start(chain, step + 1)

    def finish(self):
        for chain, step in self.sent:
            for way in (0, 1):
                self.copy(chain, step, way).wait_send()


def forward_kernel(
    n,
    s_qkv, s_out, s_gate, s_up, s_down, tokens, cotangent, cs_ref, sn_ref, start_ref,
    w_qkv, w_out, w_gate, w_up, w_down, n1_out, q_ref, kv_ref, ob_ref, lse_ref, hid_ref, n2_out, to_gate_out, to_up_out, inner_out, grad_down,
    v_qkv, v_out, n1, n2, qkv, ka, kb, va, vb, part, near, keep, far_part, far, own_n2, weight, stage, inner, grads,
    ring_send, ring_recv, tp_send, tp_recv, local,
):
    tok, width = n1.shape
    block = width // n
    quarter = tok // 4
    sub = quarter // 2
    index = lax.axis_index("dp")
    t = lax.axis_index("tensor")
    c, y = t % 2, t // 2
    mate = y * 2 + (1 - c)
    across = (1 - y) * 2 + c
    h = block // 2
    chains = [
        (s_qkv, v_qkv, (0, h + 16), (h + 16, h)),
        (s_out, v_out, (0, s_out.shape[0] // 2), (s_out.shape[0] // 2, s_out.shape[0] // 2)),
        (s_gate, w_gate, (0, h), (h, h)),
        (s_up, w_up, (0, h), (h, h)),
        (s_down, w_down, (0, h // 2), (h, h // 2)),
        (s_down, w_down, (h // 2, h // 2), (h + h // 2, h // 2)),
    ]
    ring = Gather(n, chains, ring_send, ring_recv)
    barrier = pltpu.get_barrier_semaphore()
    for device in ({"dp": ring.up}, {"dp": ring.down}, {"tensor": mate}, {"tensor": across}):
        pl.semaphore_signal(barrier, inc=1, device_id=device, device_id_type=MESH)

    used = []

    def copy(source, target):
        made = pltpu.make_async_copy(source, target, local.at[len(used)])
        made.start()
        used.append(made)
        return made

    whole = copy(tokens, n2)
    pairs = ((s_qkv, v_qkv), (s_out, v_out), (s_gate, w_gate), (s_up, w_up), (s_down, w_down))
    own = [copy(source, target.at[index]) for source, target in pairs]
    pl.semaphore_wait(barrier, 4)
    ring.start(0, 0)
    ring.start(1, 0)
    ring.order([0, 1])
    whole.wait()
    ring.pass_on(2 * (n - 1) - 2)
    ring.start(2, 0)
    ring.pass_on(1)
    ring.start(3, 0)
    ring.pass_on(1)
    ring.order([2, 3])
    own[0].wait()
    own[1].wait()

    gain_one = v_qkv[:, block : block + 16, :block]
    gain_two = v_qkv[:, block : block + 16, block : 2 * block]
    gains = [[g[i, :1].astype(f32) for i in range(n)] for g in (gain_one, gain_two)]
    gain_one, gain_two = (jnp.concatenate(g, axis=1) for g in gains)
    steps = 4
    rows_each = tok // steps
    for i in range(steps):
        rows = pl.ds(i * rows_each, rows_each)
        z = n2[rows, :].astype(f32)
        inverse = lax.rsqrt(jnp.mean(z * z, axis=-1, keepdims=True) + norm_eps)
        n1[rows, :] = (z * inverse * gain_one).astype(bf16)
        qkv[rows, :] = mm(n1[rows, :], v_qkv[:, :block].reshape(width, qkv.shape[1]))
    saved = [copy(n1, n1_out), copy(v_qkv, w_qkv), copy(v_out, w_out)]
    ring.pass_on()
    attn_forward(qkv, cs_ref, sn_ref, start_ref, q_ref, kv_ref, ob_ref, lse_ref, ka, kb, va, vb, {4: ring.pass_on, 8: ring.pass_on})

    def remote(k, source, target, device):
        made = pltpu.make_async_remote_copy(
            src_ref=source, dst_ref=target, send_sem=tp_send.at[k], recv_sem=tp_recv.at[k],
            device_id={"tensor": device}, device_id_type=MESH,
        )
        made.start()
        return made

    def projected(first):
        rows = pl.ds(pl.multiple_of(first, 16), sub)
        return jnp.concatenate([mm(ob_ref[rows, :], v_out[j]) for j in range(n)], axis=1)

    pieces = [((1 - y) * quarter + i * sub) for i in (0, 1)] + [(y * quarter + i * sub) for i in (0, 1)]
    tp = []
    for i, first in enumerate(pieces):
        part[i * sub : (i + 1) * sub, :] = projected((1 - c) * 2 * quarter + first).astype(bf16)
        tp.append(remote(i, part.at[pl.ds(i * sub, sub)], near.at[pl.ds(i * sub, sub)], mate))
    for i, first in enumerate(pieces):
        mine = projected(c * 2 * quarter + first)
        tp[i].wait_recv()
        total = mine + near[i * sub : (i + 1) * sub, :].astype(f32)
        if i < 2:
            far_part[i * sub : (i + 1) * sub, :] = total.astype(bf16)
            tp.append(remote(4 + i, far_part.at[pl.ds(i * sub, sub)], far.at[pl.ds(i * sub, sub)], across))
        else:
            keep[(i - 2) * sub : (i - 1) * sub, :] = total
    ring.pass_on(2)

    first_row = (2 * c + y) * quarter
    token_rows = copy(tokens.at[pl.ds(pl.multiple_of(first_row, 16), quarter)], own_n2)
    token_rows.wait()
    sent = []
    for i in (0, 1):
        rows = pl.ds(i * sub, sub)
        tp[4 + i].wait_recv()
        hidden = own_n2[rows, :].astype(f32) + keep[rows, :] + far[rows, :].astype(f32)
        hid_ref[rows, :] = hidden
        inverse = lax.rsqrt(jnp.mean(hidden * hidden, axis=-1, keepdims=True) + norm_eps)
        place = pl.ds(pl.multiple_of(first_row + i * sub, 16), sub)
        n2[place, :] = (hidden * inverse * gain_two).astype(bf16)
        sent.append(remote(6 + i, n2.at[place], n2.at[place], across))
        sent.append(remote(8 + i, n2.at[place], n2.at[place], mate))
        ring.pass_on()
    ring.pass_on()
    other_row = (2 * c + 1 - y) * quarter
    for i in (0, 1):
        sent[2 * i].wait_recv()
        place = pl.ds(pl.multiple_of(other_row + i * sub, 16), sub)
        sent.append(remote(10 + i, n2.at[place], n2.at[place], mate))
        ring.pass_on()
    for made in (sent[1], sent[3], sent[4], sent[5]):
        made.wait_recv()
    saved.append(copy(n2, n2_out))
    ring.pass_on(len(ring.events) - 2)
    ring.start(4, 0)
    ring.pass_on(1)
    ring.start(5, 0)
    ring.pass_on(1)
    ring.order([4, 5])
    own[2].wait()
    own[3].wait()

    units = inner.shape[1]
    firsts = list(range(0, units, 256))

    def load(j):
        wide = min(256, units - firsts[j])
        return [
            copy(source.at[:, :, pl.ds(firsts[j], wide)], weight.at[j % 2, k, :, :, pl.ds(0, wide)])
            for k, source in enumerate((w_gate, w_up))
        ]

    loads = {0: load(0)}
    writes = []
    for j, first in enumerate(firsts):
        wide = min(256, units - first)
        if j + 1 < len(firsts):
            loads[j + 1] = load(j + 1)
        for made in loads[j]:
            made.wait()
        gate, up = (mm(n2[...], weight[j % 2, k, :, :, :wide].reshape(width, wide)) for k in (0, 1))
        sig = jax.nn.sigmoid(gate)
        silu = gate * sig
        inner[:, first : first + wide] = (silu * up).astype(bf16)
        if j >= 2:
            for made in writes[j - 2]:
                made.wait()
        stage[j % 2, 0, :, :wide] = (up * (sig * (1.0 + gate * (1.0 - sig)))).astype(bf16)
        stage[j % 2, 1, :, :wide] = silu.astype(bf16)
        writes.append(
            [
                copy(stage.at[j % 2, k, :, pl.ds(0, wide)], target.at[:, pl.ds(first, wide)])
                for k, target in enumerate((to_gate_out, to_up_out))
            ]
        )
        ring.pass_on()
    for made in writes[-2] + writes[-1]:
        made.wait()
    saved.append(copy(inner, inner_out))
    saved[3].wait()
    for made in sent:
        made.wait_send()
    copy(cotangent, n2).wait()
    per = 256 // block
    writes = []
    for j in range(width // 256):
        if j >= 2:
            writes[j - 2].wait()
        grad = mm_tn(n2[:, j * 256 : (j + 1) * 256], inner[...]).astype(bf16)
        grads[j % 2] = grad.reshape(per, block, units)
        writes.append(copy(grads.at[j % 2], grad_down.at[pl.ds(j * per, per)]))
        ring.pass_on()
    writes[-2].wait()
    writes[-1].wait()
    ring.pass_on(len(ring.events))
    for made in tp:
        made.wait_send()
    ring.finish()
    own[4].wait()
    for i, made in enumerate(saved):
        if i != 3:
            made.wait()


def forward(n, s_qkv, s_out, s_gate, s_up, s_down, tokens, cotangent, cs, sn, start):
    tok, width = tokens.shape
    heads = s_qkv.shape[1] - 128
    units = s_gate.shape[1]
    quarter = tok // 4
    vm = pl.BlockSpec(memory_space=pltpu.VMEM)
    anywhere = pl.BlockSpec(memory_space=pl.ANY)
    shards = (s_qkv, s_out, s_gate, s_up, s_down)
    return pl.pallas_call(
        functools.partial(forward_kernel, n),
        out_shape=tuple(jax.ShapeDtypeStruct((n,) + s.shape, bf16) for s in shards)
        + (
            jax.ShapeDtypeStruct((tok, width), bf16),
            jax.ShapeDtypeStruct((tok, heads), bf16),
            jax.ShapeDtypeStruct((tok, 128), bf16),
            jax.ShapeDtypeStruct((tok, heads), bf16),
            jax.ShapeDtypeStruct((heads // HD, tok), f32),
            jax.ShapeDtypeStruct((quarter, width), f32),
            jax.ShapeDtypeStruct((tok, width), bf16),
            jax.ShapeDtypeStruct((tok, units), bf16),
            jax.ShapeDtypeStruct((tok, units), bf16),
            jax.ShapeDtypeStruct((tok, units), bf16),
            jax.ShapeDtypeStruct((n, width // n, units), bf16),
        ),
        in_specs=[anywhere] * 7 + [vm] * 3,
        out_specs=(anywhere,) * 6 + (vm,) * 5 + (anywhere,) * 5,
        scratch_shapes=[
            pltpu.VMEM((n,) + s_qkv.shape, bf16),
            pltpu.VMEM((n,) + s_out.shape, bf16),
            pltpu.VMEM((tok, width), bf16),
            pltpu.VMEM((tok, width), bf16),
            pltpu.VMEM((tok, heads + 128), f32),
            pltpu.VMEM((tok, 128), bf16),
            pltpu.VMEM((tok, 128), bf16),
            pltpu.VMEM((tok, 128), bf16),
            pltpu.VMEM((tok, 128), bf16),
            pltpu.VMEM((2 * quarter, width), bf16),
            pltpu.VMEM((2 * quarter, width), bf16),
            pltpu.VMEM((quarter, width), f32),
            pltpu.VMEM((quarter, width), bf16),
            pltpu.VMEM((quarter, width), bf16),
            pltpu.VMEM((quarter, width), bf16),
            pltpu.VMEM((2, 2, n, width // n, 256), bf16),
            pltpu.VMEM((2, 2, tok, 256), bf16),
            pltpu.VMEM((tok, units), bf16),
            pltpu.VMEM((2, 256 * n // width, width // n, units), bf16),
            pltpu.SemaphoreType.DMA((6, 2, n - 1)),
            pltpu.SemaphoreType.DMA((6, 2, n - 1)),
            pltpu.SemaphoreType.DMA((12,)),
            pltpu.SemaphoreType.DMA((12,)),
            pltpu.SemaphoreType.DMA((64,)),
        ],
        compiler_params=pltpu.CompilerParams(collective_id=1, has_side_effects=True, vmem_limit_bytes=62 * 2**20),
    )(*shards, tokens, cotangent, cs, sn, start)


class Later:
    def __init__(self, make):
        self.make = make

    def start(self):
        self.make().start()

    def wait(self):
        self.make().wait()

    def wait_send(self):
        self.make().wait_send()

    def wait_recv(self):
        self.make().wait_recv()


class Reduce:
    def __init__(self, n, chains, pools, send, recv, slot_sem, term_sem):
        self.n, self.chains, self.pools = n, chains, pools
        self.send_sem, self.recv_sem = send, recv
        self.slot_sem, self.term_sem = slot_sem, term_sem
        self.place = ring_place(n, lax.axis_index("dp"))
        self.up = ring_index(n, self.place + 1)
        self.down = ring_index(n, self.place - 1)
        self.origin = [
            [ring_index(n, self.place - 1 - step), ring_index(n, self.place + 1 + step)] for step in range(n)
        ]
        self.events, self.waiting, self.used = [], [], [0] * len(pools)
        self.busy = [{} for _ in pools]
        self.ready = None

    def send(self, chain, step, way, source):
        return Later(
            lambda: pltpu.make_async_remote_copy(
                src_ref=source(),
                dst_ref=self.landing(chain, step, way),
                send_sem=self.send_sem.at[chain, way, step],
                recv_sem=self.recv_sem.at[chain, way, step],
                device_id={"dp": self.up if way == 0 else self.down},
                device_id_type=MESH,
            )
        )

    def landing(self, chain, step, way):
        slots, rows = self.chains[chain][1], self.chains[chain][2 + way]
        return slots().at[step, way, pl.ds(0, rows[1])]

    def term(self, chain, step, way):
        rows = pl.ds(*self.chains[chain][2 + way])
        return self.chains[chain][0].at[self.origin[step][way], rows]

    def start(self, chain):
        for way in (0, 1):
            made = self.send(chain, 0, way, functools.partial(self.term, chain, 0, way))
            made.start()
            self.waiting.append(made)

    def order(self, chains):
        self.events += [(chain, step) for step in range(self.n - 1) for chain in chains]
        self.fetch()

    def fetch(self):
        if self.ready is not None or not self.events:
            return
        chain, step = self.events[0]
        pool = self.chains[chain][4]
        arrived, terms = self.pools[pool]
        slot = self.used[pool] % arrived.shape[0]
        self.used[pool] += 1
        for made in self.busy[pool].pop(slot, ()):
            made.wait_send()
        copies = []
        for way in (0, 1):
            count = self.chains[chain][2 + way][1]
            copies.append(
                Later(
                    lambda way=way, count=count: pltpu.make_async_copy(
                        self.term(chain, step + 1, way),
                        terms.at[slot, way, pl.ds(0, count)],
                        self.term_sem.at[pool, slot, way],
                    )
                )
            )
            copies[-1].start()
        self.ready = (slot, copies)

    def held(self, pool, slot, way, rows):
        return self.pools[pool][0].at[slot, way, pl.ds(0, rows)]

    def pass_on(self, count=1):
        for _ in range(min(count, len(self.events))):
            chain, step = self.events.pop(0)
            pool, result = self.chains[chain][4:]
            arrived, terms = self.pools[pool]
            slot, copies = self.ready
            self.ready = None
            loads = []
            for way in (0, 1):
                rows = self.chains[chain][2 + way][1]
                self.send(chain, step, way, functools.partial(self.landing, chain, step, way)).wait_recv()
                loads.append(
                    pltpu.make_async_copy(
                        self.landing(chain, step, way),
                        arrived.at[slot, way, pl.ds(0, rows)],
                        self.slot_sem.at[pool, slot, way],
                    )
                )
                loads[-1].start()
            sent = []
            for way in (0, 1):
                rows = self.chains[chain][2 + way][1]
                loads[way].wait()
                copies[way].wait()
                total = arrived[slot, way, :rows].astype(f32) + terms[slot, way, :rows].astype(f32)
                if step + 1 < self.n - 1:
                    arrived[slot, way, :rows] = total.astype(bf16)
                    place = functools.partial(self.held, pool, slot, way, rows)
                    sent.append(self.send(chain, step + 1, way, place))
                    sent[-1].start()
                else:
                    result(way, total)
            self.busy[pool][slot] = sent
            self.fetch()

    def finish(self):
        for busy in self.busy:
            for sent in busy.values():
                for made in sent:
                    made.wait_send()
        for made in self.waiting:
            made.wait_send()


def backward_kernel(
    n,
    g_hbm, n2_hbm, n1_hbm, x_hbm, to_gate, to_up, inner_hbm, grad_down,
    w_qkv, w_out, w_gate, w_up, w_down, q_hbm, kv_hbm, ob_hbm, hid_ref, lse_ref, cs_ref, sn_ref, start_ref,
    output, grad_x, r_down, r_gate, r_up, r_out, r_qkv,
    grad_gate, grad_up, grad_out, grad_qkv, l_down, l_gate, l_up, l_out, l_qkv,
    tile, part, near, far_part, far, keep, dh, gh, rows_in, own_rows, dqkv, stage, stage_o, fin, fin_o, fin_q,
    pool_a, pool_b, pool_c, pool_d, pool_e, pool_f, gain_rows, gain_in, gain_tile,
    ring_send, ring_recv, slot_sem, term_sem, tp_send, tp_recv, credit, local,
):
    tok, width = dh.shape
    block = width // n
    per = 256 // block
    chunks = width // 256
    units = w_gate.shape[2]
    heads = ob_hbm.shape[1]
    quarter = tok // 4
    sub = quarter // 2
    h = block // 2
    ho = heads // 2
    t = lax.axis_index("tensor")
    c, y = t % 2, t // 2
    mate = y * 2 + (1 - c)
    across = (1 - y) * 2 + c
    first_row = (2 * c + y) * quarter
    other_row = (2 * c + 1 - y) * quarter
    count = [0, 0]

    def rows_at(first, rows):
        return pl.ds(pl.multiple_of(first, 16), rows)

    own_rows_at = rows_at(first_row, quarter)
    own_subs = [rows_at(first_row + i * sub, sub) for i in (0, 1)]
    other_subs = [rows_at(other_row + i * sub, sub) for i in (0, 1)]
    sent_half = rows_at((1 - c) * 2 * quarter, 2 * quarter)
    sent_quarter, kept_quarter = rows_at((1 - y) * quarter, quarter), rows_at(y * quarter, quarter)
    sent_tile, kept_tile = (rows_at((2 * c + at) * quarter, quarter) for at in (1 - y, y))

    def now(place):
        return place() if callable(place) else place

    def copy(source, target):
        k = count[0]
        count[0] += 1
        made = Later(lambda: pltpu.make_async_copy(now(source), now(target), local.at[k]))
        made.start()
        return made

    def remote(source, target, device):
        k = count[1]
        count[1] += 1
        return Later(
            lambda: pltpu.make_async_remote_copy(
                src_ref=now(source), dst_ref=now(target), send_sem=tp_send.at[k], recv_sem=tp_recv.at[k],
                device_id={"tensor": device}, device_id_type=MESH,
            )
        )

    def to(result, buffer, writes, firsts):
        def write(way, total):
            if len(writes) >= 2:
                writes[-2].wait()
            rows = total.shape[0]
            slot = len(writes) % 2
            buffer[slot, :rows] = total
            source = lambda: buffer.at[slot, pl.ds(0, rows)]
            writes.append(copy(source, lambda: result.at[pl.ds(firsts[way], rows)]))

        return write

    written = [[], [], []]
    ends = [
        to(r_down, fin, written[0], (0, h)),
        to(r_down, fin, written[0], (h // 2, h + h // 2)),
        to(r_gate, fin, written[0], (0, h)),
        to(r_up, fin, written[0], (0, h)),
        to(r_out, fin_o, written[1], (0, ho)),
        to(r_qkv, fin_q, written[2], (0, h + 16)),
    ]
    chains = [
        (grad_down, lambda: l_down.at[0], (0, h // 2), (h, h // 2), 0, ends[0]),
        (grad_down, lambda: l_down.at[1], (h // 2, h // 2), (h + h // 2, h // 2), 0, ends[1]),
        (grad_gate, lambda: l_gate, (0, h), (h, h), 0, ends[2]),
        (grad_up, lambda: l_up, (0, h), (h, h), 0, ends[3]),
        (grad_out, lambda: l_out, (0, ho), (ho, ho), 1, ends[4]),
        (grad_qkv, lambda: l_qkv, (0, h + 16), (h + 16, h), 2, ends[5]),
    ]
    pools = [(pool_a, pool_b), (pool_c, pool_d), (pool_e, pool_f)]
    ring = Reduce(n, chains, pools, ring_send, ring_recv, slot_sem, term_sem)
    barrier = pltpu.get_barrier_semaphore()
    for device in ({"dp": ring.up}, {"dp": ring.down}, {"tensor": mate}, {"tensor": across}):
        pl.semaphore_signal(barrier, inc=1, device_id=device, device_id_type=MESH)
    gain_load = copy(w_qkv.at[:, pl.ds(block, 16)], gain_tile)
    pl.semaphore_wait(barrier, 4)
    ring.start(0)
    ring.start(1)
    ring.order([0, 1])
    gain_load.wait()
    gains = [
        jnp.concatenate([gain_tile[i, :1, k * block : (k + 1) * block].astype(f32) for i in range(n)], axis=1)
        for k in (0, 1)
    ]

    class Sum:
        def __init__(self, at_once=True):
            self.near, self.far, self.at_once = [], [], at_once

        def put(self, j, value):
            tile[j % 2] = value
            part[j] = tile[j % 2, sent_half, :].astype(bf16)
            self.near.append(remote(lambda: part.at[j], lambda: near.at[j], mate))
            self.near[j].start()
            if j > 0:
                self.absorb(j - 1)
            if j == chunks - 1:
                self.absorb(j)

        def absorb(self, j):
            self.near[j].wait_recv()

            far_part[j] = (tile[j % 2, sent_tile, :] + near[j, sent_quarter, :].astype(f32)).astype(bf16)
            keep[:, j * 256 : (j + 1) * 256] = tile[j % 2, kept_tile, :] + near[j, kept_quarter, :].astype(f32)
            self.far.append(remote(lambda: far_part.at[j], lambda: far.at[j], across))
            if self.at_once:
                self.far[j].start()

        def send_far(self):
            for made in self.far:
                made.start()

        def finish(self):
            for j in range(chunks):
                self.far[j].wait_recv()
                keep[:, j * 256 : (j + 1) * 256] += far[j].astype(f32)
            for made in self.near + self.far:
                made.wait_send()

    class Spread:
        def __init__(self, whole):
            self.whole, self.far, self.near, self.last = whole, [], [], []

        def put(self, i, source):
            place = lambda: self.whole.at[own_subs[i]]
            self.far.append(remote(source, place, across))
            self.far[i].start()
            self.near.append(remote(source, place, mate))
            self.near[i].start()

        def forward(self):
            for i in (0, 1):
                self.far[i].wait_recv()
                place = lambda i=i: self.whole.at[other_subs[i]]
                self.last.append(remote(place, place, mate))
                self.last[i].start()

        def arrive_near(self):
            for made in self.near:
                made.wait_recv()

        def arrive(self):
            for made in self.last:
                made.wait_recv()

        def close(self):
            for made in self.far + self.near + self.last:
                made.wait_send()

    def through_norm(values, gain, base, put):
        gain_grad = 0.0
        for i in (0, 1):
            rows = slice(i * sub, (i + 1) * sub)
            z = values[rows, :].astype(f32)
            inverse = lax.rsqrt(jnp.mean(z * z, axis=-1, keepdims=True) + norm_eps)
            scaled = z * inverse
            grad = keep[rows, :]
            gain_grad = gain_grad + jnp.sum(grad * scaled, axis=0, keepdims=True)
            grad = grad * gain
            grad = inverse * (grad - scaled * jnp.mean(grad * scaled, axis=-1, keepdims=True))
            put(i, rows, base[rows, :].astype(f32) + grad)
        return gain_grad

    def weight_grads(target, left, right):
        writes = []
        cols = right.shape[1]
        for j in range(chunks):
            if j >= 2:
                writes[j - 2].wait()
            grad = mm_tn(left[:, j * 256 : (j + 1) * 256], right[...]).astype(bf16)
            stage[j % 2, :, :, :cols] = grad.reshape(per, block, cols)
            writes.append(copy(stage.at[j % 2, :, :, pl.ds(0, cols)], target.at[pl.ds(j * per, per), pl.ds(0, block)]))
            yield j
        writes[-2].wait()
        writes[-1].wait()

    hid_sum, out_sum, x_sum = Sum(), Sum(False), Sum()
    spread, result, last = Spread(dh), Spread(output), Spread(grad_x)
    gain_rows[...] = jnp.zeros_like(gain_rows)

    def feed_forward(acts, dg, du, weight, wtile):
        loads = [copy(g_hbm, acts), copy(to_gate, dg), copy(to_up, du)]
        firsts = list(range(0, units, 256))

        def tile_load(j):
            wide = min(256, units - firsts[j])
            return copy(w_down.at[:, :, pl.ds(firsts[j], wide)], wtile.at[j % 2, :, :, pl.ds(0, wide)])

        def block_load(j, *sources):
            return [copy(s.at[pl.ds(j * per, per)], weight.at[j % 2, k]) for k, s in enumerate(sources)]

        tiles = [tile_load(0)]
        for made in loads:
            made.wait()
        for j, first in enumerate(firsts):
            wide = min(256, units - first)
            if j + 1 < len(firsts):
                tiles.append(tile_load(j + 1))
            tiles[j].wait()
            grad = mm(acts[...], wtile[j % 2, :, :, :wide].reshape(width, wide))
            cols = slice(first, first + wide)
            dg[:, cols] = (grad * dg[:, cols].astype(f32)).astype(bf16)
            du[:, cols] = (grad * du[:, cols].astype(f32)).astype(bf16)
            if j > 0:
                ring.pass_on()
        acts_load = copy(n2_hbm, acts)
        loads = [block_load(0, w_gate, w_up)]
        for j in range(chunks):
            if j + 1 < chunks:
                loads.append(block_load(j + 1, w_gate, w_up))
            for made in loads[j]:
                made.wait()
            value = mm_nt(dg[...], weight[j % 2, 0].reshape(256, units))
            hid_sum.put(j, value + mm_nt(du[...], weight[j % 2, 1].reshape(256, units)))
            if j % 2 == 1 or j == 4:
                ring.pass_on()
        acts_load.wait()
        for j in weight_grads(grad_gate, acts, dg):
            if j in (2, 5, 7):
                ring.pass_on()
        ring.start(2)
        inner_load = copy(inner_hbm, dg)
        copy(g_hbm.at[own_rows_at], rows_in).wait()
        hid_sum.finish()

        def put(i, rows, grad):
            gh[rows, :] = grad
            place = own_subs[i]
            dh[place, :] = grad.astype(bf16)
            spread.put(i, lambda: dh.at[place])

        gain_rows[1:2, :] = through_norm(hid_ref, gains[1], rows_in, put)
        for j in weight_grads(grad_up, acts, du):
            if j in (2, 5):
                ring.pass_on()
        ring.start(3)
        ring.order([2, 3])
        spread.arrive_near()
        inner_load.wait()
        loads = [block_load(0, w_down)]
        for j in range(chunks):
            if j + 1 < chunks:
                loads.append(block_load(j + 1, w_down))
            loads[j][0].wait()
            out_sum.put(j, mm_nt(dg[...], weight[j % 2, 0].reshape(256, units)))
            if j in (2, 6):
                ring.pass_on()

    pl.run_scoped(
        feed_forward,
        pltpu.VMEM((tok, width), bf16),
        pltpu.VMEM((tok, units), bf16),
        pltpu.VMEM((tok, units), bf16),
        pltpu.VMEM((2, 2, per, block, units), bf16),
        pltpu.VMEM((2, n, block, 256), bf16),
    )
    spread.forward()
    out_sum.send_far()
    ring.pass_on()
    spread.arrive()

    def attention(q, kv, ob, v_out, dob, ka, kb, va, vb, dk, dv):
        loads = [copy(q_hbm, q), copy(kv_hbm, kv), copy(ob_hbm, ob), copy(w_out, v_out)]
        for made in loads:
            made.wait()
        for i in (0, 1):
            rows = slice(2 * i * quarter, 2 * (i + 1) * quarter)
            total = 0.0
            for j in range(n):
                total = total + mm_nt(dh[rows, j * block : (j + 1) * block], v_out[j])
            dob[rows, :] = total.astype(bf16)
        attn_backward(
            q, kv, dob, lse_ref, cs_ref, sn_ref, start_ref, dqkv, ka, kb, va, vb, dk, dv,
            {2: ring.pass_on, 5: ring.pass_on, 8: ring.pass_on},
        )
        writes = []
        for j in range(n):
            if j >= 2:
                writes[j - 2].wait()
            stage_o[j % 2] = mm_tn(ob[...], dh[:, j * block : (j + 1) * block]).astype(bf16)
            writes.append(copy(stage_o.at[j % 2], grad_out.at[j]))
        writes[-2].wait()
        writes[-1].wait()

    pl.run_scoped(
        attention,
        pltpu.VMEM((tok, heads), bf16),
        pltpu.VMEM((tok, 128), bf16),
        pltpu.VMEM((tok, heads), bf16),
        pltpu.VMEM((n, heads, block), bf16),
        pltpu.VMEM((tok, heads), bf16),
        *[pltpu.VMEM((tok, 128), bf16)] * 4,
        *[pltpu.VMEM((tok, 128), f32)] * 2,
    )
    out_sum.finish()
    for i in (0, 1):
        rows = slice(i * sub, (i + 1) * sub)
        own_rows[rows, :] = (hid_ref[rows, :] + keep[rows, :]).astype(bf16)
        result.put(i, lambda i=i: own_rows.at[pl.ds(i * sub, sub)])
    owns = [copy(own_rows, output.at[own_rows_at])]
    for k, device in enumerate((mate, across)):
        pl.semaphore_signal(credit.at[k], inc=1, device_id={"tensor": device}, device_id_type=MESH)
    pl.semaphore_wait(credit.at[0], 1)
    pl.semaphore_wait(credit.at[1], 1)
    ring.pass_on()

    def projections(acts, v_qkv):
        loads = [copy(w_qkv, v_qkv), copy(n1_hbm, acts), copy(x_hbm.at[own_rows_at], rows_in)]
        loads[0].wait()
        for j in range(chunks):
            weight = v_qkv[j * per : (j + 1) * per, :block].reshape(256, heads + 128)
            x_sum.put(j, mm_nt(dqkv[...], weight))
        ring.pass_on()
        loads[1].wait()
        for j in weight_grads(grad_qkv, acts, dqkv):
            if j == 4:
                ring.pass_on()
        loads[2].wait()

    pl.run_scoped(
        projections,
        pltpu.VMEM((tok, width), bf16),
        pltpu.VMEM((n, block + 16, heads + 128), bf16),
    )
    x_sum.finish()

    def put(i, rows, grad):
        rows_in[rows, :] = grad.astype(bf16)
        last.put(i, lambda: rows_in.at[pl.ds(i * sub, sub)])

    gain_rows[0:1, :] = through_norm(rows_in, gains[0], gh, put)
    owns.append(copy(rows_in, grad_x.at[own_rows_at]))
    for k, device in enumerate((mate, across)):
        made = remote(gain_rows, gain_in.at[k], device)
        made.start()
        made.wait()
        gain_rows[...] += gain_in[k]
    for i in range(n):
        both = [gain_rows[k : k + 1, i * block : (i + 1) * block] for k in (0, 1)]
        both = jnp.concatenate(both + [jnp.zeros((1, heads + 128 - 2 * block), f32)], axis=1)
        gain_tile[i] = jnp.broadcast_to(both, (16, heads + 128)).astype(bf16)
    copy(gain_tile, grad_qkv.at[:, pl.ds(block, 16)]).wait()
    result.forward()
    ring.pass_on(len(ring.events) - 2)
    ring.start(4)
    ring.start(5)
    ring.order([4, 5])
    ring.pass_on(2)
    last.forward()
    ring.pass_on(len(ring.events))
    for spreading in (result, last):
        spreading.arrive_near()
        spreading.arrive()
    for spreading in (spread, result, last):
        spreading.close()
    ring.finish()
    for made in owns:
        made.wait()
    for writes in written:
        for made in writes[-2:]:
            made.wait()


def backward(n, g, n2, n1, x, to_gate, to_up, inner, grad_down, w_qkv, w_out, w_gate, w_up, w_down, q, kv, ob, hid, lse, cs, sn, start):
    tok, width = x.shape
    block = width // n
    h = block // 2
    heads, units = ob.shape[1], inner.shape[1]
    quarter = tok // 4
    per, chunks = 256 // block, width // 256
    vm = pl.BlockSpec(memory_space=pltpu.VMEM)
    anywhere = pl.BlockSpec(memory_space=pl.ANY)
    hbm = jax.ShapeDtypeStruct
    qkv = heads + 128
    return pl.pallas_call(
        functools.partial(backward_kernel, n),
        out_shape=(
            hbm((tok, width), bf16),
            hbm((tok, width), bf16),
            hbm((block, units), f32),
            hbm((block, units), f32),
            hbm((block, units), f32),
            hbm((heads, block), f32),
            hbm((block + 16, qkv), f32),
            hbm((n, block, units), bf16),
            hbm((n, block, units), bf16),
            hbm((n, heads, block), bf16),
            hbm((n, block + 16, qkv), bf16),
            hbm((2, n - 1, 2, h // 2, units), bf16),
            hbm((n - 1, 2, h, units), bf16),
            hbm((n - 1, 2, h, units), bf16),
            hbm((n - 1, 2, heads // 2, block), bf16),
            hbm((n - 1, 2, h + 16, qkv), bf16),
        ),
        in_specs=[anywhere] * 16 + [vm] * 5,
        out_specs=(anywhere,) * 16,
        scratch_shapes=[
            pltpu.VMEM((2, tok, 256), f32),
            pltpu.VMEM((chunks, 2 * quarter, 256), bf16),
            pltpu.VMEM((chunks, 2 * quarter, 256), bf16),
            pltpu.VMEM((chunks, quarter, 256), bf16),
            pltpu.VMEM((chunks, quarter, 256), bf16),
            pltpu.VMEM((quarter, width), f32),
            pltpu.VMEM((tok, width), bf16),
            pltpu.VMEM((quarter, width), f32),
            pltpu.VMEM((quarter, width), bf16),
            pltpu.VMEM((quarter, width), bf16),
            pltpu.VMEM((tok, qkv), bf16),
            pltpu.VMEM((2, per, block, units), bf16),
            pltpu.VMEM((2, heads, block), bf16),
            pltpu.VMEM((2, h, units), f32),
            pltpu.VMEM((2, heads // 2, block), f32),
            pltpu.VMEM((2, h + 16, qkv), f32),
            pltpu.VMEM((3, 2, h, units), bf16),
            pltpu.VMEM((3, 2, h, units), bf16),
            pltpu.VMEM((2, 2, heads // 2, block), bf16),
            pltpu.VMEM((2, 2, heads // 2, block), bf16),
            pltpu.VMEM((2, 2, h + 16, qkv), bf16),
            pltpu.VMEM((2, 2, h + 16, qkv), bf16),
            pltpu.VMEM((8, width), f32),
            pltpu.VMEM((2, 8, width), f32),
            pltpu.VMEM((n, 16, qkv), bf16),
            pltpu.SemaphoreType.DMA((6, 2, n - 1)),
            pltpu.SemaphoreType.DMA((6, 2, n - 1)),
            pltpu.SemaphoreType.DMA((3, 3, 2)),
            pltpu.SemaphoreType.DMA((3, 3, 2)),
            pltpu.SemaphoreType.DMA((80,)),
            pltpu.SemaphoreType.DMA((80,)),
            pltpu.SemaphoreType.REGULAR((2,)),
            pltpu.SemaphoreType.DMA((160,)),
        ],
        compiler_params=pltpu.CompilerParams(collective_id=2, has_side_effects=True, vmem_limit_bytes=62 * 2**20),
    )(g, n2, n1, x, to_gate, to_up, inner, grad_down, w_qkv, w_out, w_gate, w_up, w_down, q, kv, ob, hid, lse, cs, sn, start)


def prep_kernel(q_ref, k_ref, v_ref, d_ref, g1_ref, g2_ref, qkv_ref, dt_ref):
    rows, cols = q_ref.shape
    qkv_ref[:rows, :cols] = q_ref[...]
    qkv_ref[:rows, cols:] = jnp.concatenate([k_ref[...], v_ref[...]], axis=1)
    qkv_ref[rows:, :] = jnp.zeros((16, qkv_ref.shape[1]), bf16)
    gains = jnp.concatenate([g1_ref[...], g2_ref[...]], axis=1).astype(f32)
    qkv_ref[rows:, : 2 * rows] = jnp.broadcast_to(gains, (16, 2 * rows)).astype(bf16)
    dt_ref[...] = jnp.transpose(d_ref[...].astype(f32)).astype(bf16)


def prep(w_query, w_key, w_value, w_down, gain_attn, gain_mlp):
    rows, cols = w_query.shape
    vm = pl.BlockSpec(memory_space=pltpu.VMEM)
    return pl.pallas_call(
        prep_kernel,
        out_shape=(
            jax.ShapeDtypeStruct((rows + 16, cols + 128), bf16),
            jax.ShapeDtypeStruct(w_down.shape[::-1], bf16),
        ),
        in_specs=[vm] * 6,
        out_specs=(vm,) * 2,
        compiler_params=pltpu.CompilerParams(vmem_limit_bytes=32 * 2**20),
    )(w_query, w_key, w_value, w_down, gain_attn.reshape(1, -1), gain_mlp.reshape(1, -1))


def per_device(
    n_dp,
    tokens,
    gain_attn,
    w_query,
    w_key,
    w_value,
    w_out,
    gain_mlp,
    w_gate,
    w_up,
    w_down,
    lengths,
    cotangent,
):
    tok, width = tokens.shape
    line = n_dp // 2
    block = width // n_dp
    cols = w_query.shape[1]
    ends = jnp.cumsum(lengths[0], dtype=jnp.int32)
    starts = ends - lengths[0]
    places = jnp.arange(tok, dtype=jnp.int32)
    inside = (places[:, None] >= starts[None, :]) & (places[:, None] < ends[None, :])
    start = jnp.sum(jnp.where(inside, starts[None, :], 0), axis=1, dtype=jnp.int32)
    freqs = rope_base ** (-jnp.arange(HD // 2, dtype=f32) * 2.0 / HD)
    angles = (places - start).astype(f32)[:, None] * freqs[None, :]
    cosine, sine = jnp.cos(angles), jnp.sin(angles)
    cs = jnp.concatenate([cosine] * 4, axis=1)
    sn = jnp.concatenate([-sine, sine, -sine, sine], axis=1)

    p_qkv, p_down = prep(w_query, w_key, w_value, w_down, gain_attn, gain_mlp)
    w_qkv, w_out_all, w_g, w_u, w_d, n1, q, kv, ob, lse, hidden, n2, to_gate, to_up, inner, grad_down = forward(
        n_dp, p_qkv, w_out, w_gate, w_up, p_down, tokens, cotangent, cs, sn, start[:, None]
    )
    output, grad_tokens, s_down, s_gate, s_up, s_out, s_qkv = backward(
        n_dp, cotangent, n2, n1, tokens, to_gate, to_up, inner, grad_down, w_qkv, w_out_all, w_g, w_u, w_d,
        q, kv, ob, hidden, lse, cs, sn, start[None, :]
    )[:7]
    return (
        output,
        grad_tokens.astype(f32),
        s_qkv[:block, :cols],
        s_qkv[:block, cols : cols + HD],
        s_qkv[:block, cols + HD :],
        s_out,
        s_gate,
        s_up,
        s_down.T,
        s_qkv[block, :block],
        s_qkv[block, block : 2 * block],
    )


def solution(mesh):
    placed = (
        P("dp", None),
        P("dp"),
        P("dp", "tensor"),
        P("dp", "tensor"),
        P("dp", "tensor"),
        P("tensor", "dp"),
        P("dp"),
        P("dp", "tensor"),
        P("dp", "tensor"),
        P("tensor", "dp"),
        P("dp", None),
        P("dp", None),
    )
    return jax.shard_map(
        functools.partial(per_device, mesh.shape["dp"]),
        mesh=mesh,
        in_specs=placed,
        out_specs=(
            P("dp", None),
            P("dp", None),
            P("dp", "tensor"),
            P("dp", "tensor"),
            P("dp", "tensor"),
            P("tensor", "dp"),
            P("dp", "tensor"),
            P("dp", "tensor"),
            P("tensor", "dp"),
            P("dp"),
            P("dp"),
        ),
        check_vma=False,
    )
```

```python
import functools

import jax
import jax.numpy as jnp
from jax import lax
from jax.experimental import pallas as pl
from jax.experimental.pallas import tpu as pltpu
from jax.sharding import PartitionSpec as P

HD = 64
QB = 128


def swap_halves(z):
    lane = lax.broadcasted_iota(jnp.int32, z.shape, 1)
    return jnp.where(lane % HD < HD // 2, pltpu.roll(z, 128 - HD // 2, 1), pltpu.roll(z, HD // 2, 1))


def nt(a, b):
    return lax.dot_general(a, b, (((1,), (1,)), ((), ())), preferred_element_type=jnp.float32)


def attn_forward(qkv_ref, cs_ref, sn_ref, start_ref, q_ref, kv_ref, ob_ref, lse_ref, ka, kb, va, vb, between=()):
    tok = qkv_ref.shape[0]
    width = q_ref.shape[1]
    pairs = width // 128
    lane = lax.broadcasted_iota(jnp.int32, (tok, 128), 1)
    cs = cs_ref[...]
    sn = sn_ref[...]
    kv = qkv_ref[:, width:]
    krot = kv * cs + swap_halves(kv) * sn
    kvr = jnp.where(lane < HD, krot, kv).astype(jnp.bfloat16)
    kv_ref[...] = kvr
    kvf = kvr.astype(jnp.float32)
    rolled = pltpu.roll(kvf, HD, 1)
    ka[...] = jnp.where(lane < HD, kvf, 0.0).astype(jnp.bfloat16)
    kb[...] = jnp.where(lane < HD, 0.0, rolled).astype(jnp.bfloat16)
    va[...] = jnp.where(lane < HD, rolled, 0.0).astype(jnp.bfloat16)
    vb[...] = jnp.where(lane < HD, 0.0, kvf).astype(jnp.bfloat16)
    for i in range(tok // QB):
        rows = pl.ds(i * QB, QB)
        kp = (i + 1) * QB
        qs = []
        for p in range(pairs):
            z = qkv_ref[rows, p * 128:(p + 1) * 128]
            r = (z * cs_ref[rows, :] + swap_halves(z) * sn_ref[rows, :]).astype(jnp.bfloat16)
            r = (r.astype(jnp.float32) * 0.125).astype(jnp.bfloat16)
            q_ref[rows, p * 128:(p + 1) * 128] = r
            qs.append(r)
        qe = jnp.concatenate(qs, axis=0)
        col = lax.broadcasted_iota(jnp.int32, (QB, kp), 1)
        row = lax.broadcasted_iota(jnp.int32, (QB, kp), 0) + i * QB
        seen = (col <= row) & (col >= start_ref[rows, :])
        bias = jnp.where(seen, 0.0, -1e30)
        total = 0.0
        lse_tile = jnp.zeros((QB, 128), jnp.float32)
        lane_b = lax.broadcasted_iota(jnp.int32, (QB, 128), 1)
        for odd, (k2, v2) in enumerate(((ka, va), (kb, vb))):
            s = nt(qe, k2[:kp, :]).reshape(pairs, QB, kp) + bias[None]
            m = jnp.max(s, axis=-1, keepdims=True)
            e = jnp.exp(s - m)
            l = jnp.sum(e, axis=-1, keepdims=True)
            o = jnp.dot(e.astype(jnp.bfloat16).reshape(pairs * QB, kp), v2[:kp, :], preferred_element_type=jnp.float32)
            total = total + o.reshape(pairs, QB, 128) / l
            lse = m + jnp.log(l)
            for p in range(pairs):
                lse_tile = jnp.where(lane_b == 2 * p + odd, lse[p], lse_tile)
        for p in range(pairs):
            ob_ref[rows, p * 128:(p + 1) * 128] = total[p].astype(jnp.bfloat16)
        lse_ref[:, i * QB:(i + 1) * QB] = jnp.transpose(lse_tile)[: 2 * pairs]
        if i in between:
            between[i]()


def attn_backward(q_ref, kv_ref, dob_ref, lse_ref, cs_ref, sn_ref, start_ref, out_ref, ka, kb, va, vb, dk, dv, between=()):
    tok, width = q_ref.shape
    pairs = width // 128
    lane = lax.broadcasted_iota(jnp.int32, (tok, 128), 1)
    kvf = kv_ref[...].astype(jnp.float32)
    rolled = pltpu.roll(kvf, HD, 1)
    ka[...] = jnp.where(lane < HD, kvf, 0.0).astype(jnp.bfloat16)
    kb[...] = jnp.where(lane < HD, 0.0, rolled).astype(jnp.bfloat16)
    va[...] = jnp.where(lane < HD, rolled, 0.0).astype(jnp.bfloat16)
    vb[...] = jnp.where(lane < HD, 0.0, kvf).astype(jnp.bfloat16)
    dk[...] = jnp.zeros_like(dk)
    dv[...] = jnp.zeros_like(dv)
    for i in range(tok // QB):
        rows = pl.ds(i * QB, QB)
        kp = (i + 1) * QB
        qe = jnp.concatenate([q_ref[rows, p * 128:(p + 1) * 128] for p in range(pairs)], axis=0)
        de = jnp.concatenate([dob_ref[rows, p * 128:(p + 1) * 128] for p in range(pairs)], axis=0)
        key = lax.broadcasted_iota(jnp.int32, (kp, QB), 0)
        query = lax.broadcasted_iota(jnp.int32, (kp, QB), 1) + i * QB
        seen = (key <= query) & (key >= start_ref[:, i * QB:(i + 1) * QB])
        bias = jnp.where(seen, 0.0, -1e30)
        bias = jnp.concatenate([bias] * pairs, axis=1)
        dq = 0.0
        parts = []
        for odd, (k2, v2) in enumerate(((ka, va), (kb, vb))):
            lse = jnp.concatenate([lse_ref[2 * p + odd:2 * p + odd + 1, i * QB:(i + 1) * QB] for p in range(pairs)], axis=1)
            s = nt(k2[:kp, :], qe)
            pt = jnp.exp(s + bias - lse)
            dp = nt(v2[:kp, :], de)
            delta = jnp.sum(pt * dp, axis=0, keepdims=True)
            ds = (pt * (dp - delta)).astype(jnp.bfloat16)
            dvo = jnp.dot(pt.astype(jnp.bfloat16), de, preferred_element_type=jnp.float32)
            dko = jnp.dot(ds, qe, preferred_element_type=jnp.float32)
            parts.append((dko, dvo))
            dq = dq + lax.dot_general(ds, k2[:kp, :], (((0,), (0,)), ((), ())), preferred_element_type=jnp.float32)
        lk = lane[:kp]
        dk[:kp, :] += jnp.where(lk < HD, parts[0][0], parts[1][0])
        dv[:kp, :] += jnp.where(lk < HD, parts[0][1], parts[1][1])
        cs = cs_ref[rows, :]
        sn = sn_ref[rows, :]
        for p in range(pairs):
            y = dq[p * QB:(p + 1) * QB] * 0.125
            out_ref[rows, p * 128:(p + 1) * 128] = (y * cs - swap_halves(y) * sn).astype(jnp.bfloat16)
        if i in between:
            between[i]()
    dkf = dk[...]
    dkf = dkf + pltpu.roll(dkf, HD, 1)
    dkf = dkf * cs_ref[...] - swap_halves(dkf) * sn_ref[...]
    dvf = dv[...]
    dvf = dvf + pltpu.roll(dvf, HD, 1)
    out_ref[:, width:] = jnp.where(lane < HD, dkf, dvf).astype(jnp.bfloat16)


norm_eps = 1e-05
rope_base = 10000.0
bf16 = jnp.bfloat16
f32 = jnp.float32


def mm(a, b):
    return jnp.dot(a, b, preferred_element_type=f32)


def mm_nt(a, b):
    return lax.dot_general(a, b, (((1,), (1,)), ((), ())), preferred_element_type=f32)


def mm_tn(a, b):
    return lax.dot_general(a, b, (((0,), (0,)), ((), ())), preferred_element_type=f32)


MESH = pl.DeviceIdType.MESH


def ring_place(n, index):
    odd = index % 2
    return (1 - odd) * (index // 2) + odd * (n - 1 - index // 2)


def ring_index(n, place):
    place = (place + 2 * n) % n
    far = place // (n // 2)
    return (1 - far) * 2 * place + far * (2 * (n - 1 - place) + 1)


class Gather:
    def __init__(self, n, chains, send, recv):
        self.n, self.chains, self.send_sem, self.recv_sem = n, chains, send, recv
        self.place = ring_place(n, lax.axis_index("dp"))
        self.up = ring_index(n, self.place + 1)
        self.down = ring_index(n, self.place - 1)
        self.sent, self.events, self.groups = [], [], []

    def copy(self, chain, step, way):
        first, whole, cols, *rows = self.chains[chain]
        rows = pl.ds(*rows[way])
        cols = () if cols is None else (pl.ds(*cols),)
        origin = ring_index(self.n, self.place - step if way == 0 else self.place + step)
        place = whole.at[(origin, rows) + cols]
        return pltpu.make_async_remote_copy(
            src_ref=first.at[(rows,) + cols] if step == 0 else place,
            dst_ref=place,
            send_sem=self.send_sem.at[chain, way, step],
            recv_sem=self.recv_sem.at[chain, way, step],
            device_id={"dp": self.up if way == 0 else self.down},
            device_id_type=MESH,
        )

    def start(self, chain, step):
        for way in (0, 1):
            self.copy(chain, step, way).start()
        self.sent.append((chain, step))

    def queue(self, chains):
        self.groups.append(chains)
        self.begin()

    def begin(self):
        if self.groups and len(self.events) <= 1:
            chains = self.groups.pop(0)
            for chain in chains:
                self.start(chain, 0)
            self.events += [(chain, step) for step in range(self.n - 1) for chain in chains]

    def pass_on(self, count=1):
        for _ in range(count):
            if not self.events:
                return
            chain, step = self.events.pop(0)
            for way in (0, 1):
                self.copy(chain, step, way).wait_recv()
            if step + 1 < self.n - 1:
                self.start(chain, step + 1)
            self.begin()

    def through(self, chains):
        while any(chain in chains for chain, _ in self.events) or any(set(g) & set(chains) for g in self.groups):
            self.pass_on()

    def finish(self):
        for chain, step in self.sent:
            for way in (0, 1):
                self.copy(chain, step, way).wait_send()


def forward_kernel(
    n,
    s_qkv, s_out, s_gate, s_up, s_down, tokens, cotangent, cs_ref, sn_ref, start_ref,
    w_qkv, w_out, w_gate, w_up, w_down, n1_out, q_ref, kv_ref, ob_ref, lse_ref, hid_ref,
    n2_out, to_gate_out, to_up_out, inner_out, grad_down, dg_out, du_out, dn2_out,
    v_qkv, v_out, n1, n2, part, near, keep, far_part, far, own_n2, ring_send, ring_recv, tp_send, tp_recv, local,
):
    tok, width = n1.shape
    block = width // n
    quarter = tok // 4
    sub = quarter // 2
    units = s_gate.shape[1]
    early = to_early(units)
    index = lax.axis_index("dp")
    t = lax.axis_index("tensor")
    c, y = t % 2, t // 2
    mate = y * 2 + (1 - c)
    across = (1 - y) * 2 + c
    h = block // 2
    ho = s_out.shape[0] // 2
    chains = [(s_qkv, v_qkv, None, (0, h + 16), (h + 16, h)), (s_out, v_out, None, (0, ho), (ho, ho))]
    for cols in ((0, early), (early, units - early)):
        for shard, whole in ((s_gate, w_gate), (s_up, w_up), (s_down, w_down)):
            chains.append((shard, whole, cols, (0, h), (h, h)))
    chains[-1:] = [
        (s_down, w_down, (early, units - early), (0, h // 2), (h, h // 2)),
        (s_down, w_down, (early, units - early), (h // 2, h // 2), (h + h // 2, h // 2)),
    ]
    ring = Gather(n, chains, ring_send, ring_recv)
    barrier = pltpu.get_barrier_semaphore()
    for device in ({"dp": ring.up}, {"dp": ring.down}, {"tensor": mate}, {"tensor": across}):
        pl.semaphore_signal(barrier, inc=1, device_id=device, device_id_type=MESH)

    used = []

    def copy(source, target):
        made = pltpu.make_async_copy(source, target, local.at[len(used)])
        made.start()
        used.append(made)
        return made

    whole = copy(tokens, n2)
    pairs = ((s_qkv, v_qkv), (s_out, v_out), (s_gate, w_gate), (s_up, w_up), (s_down, w_down))
    own = [copy(source, target.at[index]) for source, target in pairs]
    pl.semaphore_wait(barrier, 4)
    ring.queue([0, 1])
    ring.queue([2, 3, 4])
    ring.queue([5, 6])
    ring.queue([7, 8])
    whole.wait()
    ring.through([0, 1])
    own[0].wait()
    own[1].wait()

    gain_one = v_qkv[:, block : block + 16, :block]
    gain_two = v_qkv[:, block : block + 16, block : 2 * block]
    gains = [[g[i, :1].astype(f32) for i in range(n)] for g in (gain_one, gain_two)]
    gain_one, gain_two = (jnp.concatenate(g, axis=1) for g in gains)

    def attention(qkv, ka, kb, va, vb):
        steps = 4
        rows_each = tok // steps
        for i in range(steps):
            rows = pl.ds(i * rows_each, rows_each)
            z = n2[rows, :].astype(f32)
            inverse = lax.rsqrt(jnp.mean(z * z, axis=-1, keepdims=True) + norm_eps)
            n1[rows, :] = (z * inverse * gain_one).astype(bf16)
            qkv[rows, :] = mm(n1[rows, :], v_qkv[:, :block].reshape(width, qkv.shape[1]))
            if i in (1, 3):
                ring.pass_on()
        attn_forward(
            qkv, cs_ref, sn_ref, start_ref, q_ref, kv_ref, ob_ref, lse_ref, ka, kb, va, vb,
            {i: ring.pass_on for i in (2, 4, 6, 8)},
        )

    pl.run_scoped(
        attention, pltpu.VMEM((tok, v_qkv.shape[2]), f32), *[pltpu.VMEM((tok, 128), bf16)] * 4
    )
    saved = [copy(n1, n1_out), copy(v_qkv, w_qkv), copy(v_out, w_out)]

    def remote(k, source, target, device):
        made = pltpu.make_async_remote_copy(
            src_ref=source, dst_ref=target, send_sem=tp_send.at[k], recv_sem=tp_recv.at[k],
            device_id={"tensor": device}, device_id_type=MESH,
        )
        made.start()
        return made

    def projected(first):
        rows = pl.ds(pl.multiple_of(first, 16), sub)
        return jnp.concatenate([mm(ob_ref[rows, :], v_out[j]) for j in range(n)], axis=1)

    pieces = [((1 - y) * quarter + i * sub) for i in (0, 1)] + [(y * quarter + i * sub) for i in (0, 1)]
    tp = []
    for i, first in enumerate(pieces):
        part[i * sub : (i + 1) * sub, :] = projected((1 - c) * 2 * quarter + first).astype(bf16)
        tp.append(remote(i, part.at[pl.ds(i * sub, sub)], near.at[pl.ds(i * sub, sub)], mate))
    for i, first in enumerate(pieces):
        mine = projected(c * 2 * quarter + first)
        tp[i].wait_recv()
        total = mine + near[i * sub : (i + 1) * sub, :].astype(f32)
        if i < 2:
            far_part[i * sub : (i + 1) * sub, :] = total.astype(bf16)
            tp.append(remote(4 + i, far_part.at[pl.ds(i * sub, sub)], far.at[pl.ds(i * sub, sub)], across))
        else:
            keep[(i - 2) * sub : (i - 1) * sub, :] = total
        if i == 1:
            ring.pass_on()

    first_row = (2 * c + y) * quarter
    token_rows = copy(tokens.at[pl.ds(pl.multiple_of(first_row, 16), quarter)], own_n2)
    token_rows.wait()
    sent = []
    for i in (0, 1):
        rows = pl.ds(i * sub, sub)
        ring.pass_on(3)
        tp[4 + i].wait_recv()
        hidden = own_n2[rows, :].astype(f32) + keep[rows, :] + far[rows, :].astype(f32)
        hid_ref[rows, :] = hidden
        inverse = lax.rsqrt(jnp.mean(hidden * hidden, axis=-1, keepdims=True) + norm_eps)
        place = pl.ds(pl.multiple_of(first_row + i * sub, 16), sub)
        n2[place, :] = (hidden * inverse * gain_two).astype(bf16)
        sent.append(remote(6 + i, n2.at[place], n2.at[place], across))
        sent.append(remote(8 + i, n2.at[place], n2.at[place], mate))
    saved[0].wait()
    cot_load = copy(cotangent, n1)
    other_row = (2 * c + 1 - y) * quarter
    for i in (0, 1):
        ring.pass_on(3)
        sent[2 * i].wait_recv()
        place = pl.ds(pl.multiple_of(other_row + i * sub, 16), sub)
        sent.append(remote(10 + i, n2.at[place], n2.at[place], mate))
    for made in (sent[1], sent[3], sent[4], sent[5]):
        made.wait_recv()
    saved.append(copy(n2, n2_out))
    ring.through([2, 3, 4])
    cot_load.wait()
    for made in own[2:]:
        made.wait()
    per = 256 // block
    chunks = width // 256

    def feed_forward(weight, stage, inner, dg, du, blocks, sums, grads):
        tiles = [(first, min(256, units - first)) for first in range(0, units, 256)]
        before = early // 256

        def load(j):
            first, wide = tiles[j]
            sources = (w_gate, w_up, w_down) if j < before else (w_gate, w_up)
            return [
                copy(source.at[:, :, pl.ds(first, wide)], weight.at[j % 2, k, :, :, pl.ds(0, wide)])
                for k, source in enumerate(sources)
            ]

        def tile(j, k, rows):
            wide = tiles[j][1]
            return mm(rows[...], weight[j % 2, k, :, :, :wide].reshape(width, wide))

        def gated(j):
            first, wide = tiles[j]
            gate, up = tile(j, 0, n2), tile(j, 1, n2)
            sig = jax.nn.sigmoid(gate)
            silu = gate * sig
            inner[:, first : first + wide] = (silu * up).astype(bf16)
            return up * (sig * (1.0 + gate * (1.0 - sig))), silu

        def weight_grads(target, rows, right, calls):
            cols = right.shape[1]
            writes = []
            for j in range(chunks):
                if j >= 2:
                    writes[j - 2].wait()
                grad = mm_tn(rows[:, j * 256 : (j + 1) * 256], right[...]).astype(bf16)
                grads[j % 2, :, :, :cols] = grad.reshape(per, block, cols)
                writes.append(copy(grads.at[j % 2, :, :, pl.ds(0, cols)], target.at[pl.ds(j * per, per)]))
                if j in calls:
                    ring.pass_on()
            writes[-2].wait()
            writes[-1].wait()

        loads = [load(0)]
        for j in range(before):
            if j + 1 < before:
                loads.append(load(j + 1))
            for made in loads[j]:
                made.wait()
            to_gate, to_up = gated(j)
            ring.pass_on()
            first, wide = tiles[j]
            grad = tile(j, 2, n1)
            dg[:, first : first + wide] = (grad * to_gate).astype(bf16)
            du[:, first : first + wide] = (grad * to_up).astype(bf16)
            ring.pass_on()

        def block_load(j):
            return [
                copy(s.at[pl.ds(j * per, per), :, pl.ds(0, early)], blocks.at[j % 2, k])
                for k, s in enumerate((w_gate, w_up))
            ]

        loads = [block_load(0)]
        writes = []
        for j in range(chunks):
            if j + 1 < chunks:
                loads.append(block_load(j + 1))
            for made in loads[j]:
                made.wait()
            if j >= 2:
                writes[j - 2].wait()
            value = mm_nt(dg[...], blocks[j % 2, 0].reshape(256, early))
            sums[j % 2] = value + mm_nt(du[...], blocks[j % 2, 1].reshape(256, early))
            writes.append(copy(sums.at[j % 2], dn2_out.at[j]))
            if j % 2 == 1:
                ring.pass_on()
        for made in writes[-2:]:
            made.wait()
        early_writes = [copy(dg, dg_out), copy(du, du_out)]
        ring.through([5, 6])
        loads = {before: load(before)}
        writes = []
        for j in range(before, len(tiles)):
            if j + 1 < len(tiles):
                loads[j + 1] = load(j + 1)
            for made in loads[j]:
                made.wait()
            first, wide = tiles[j]
            for k, value in enumerate(gated(j)):
                if len(writes) >= 4:
                    writes[-4].wait()
                stage[j % 2, k, :, :wide] = value.astype(bf16)
                target = (to_gate_out, to_up_out)[k]
                writes.append(copy(stage.at[j % 2, k, :, pl.ds(0, wide)], target.at[:, pl.ds(first - early, wide)]))
            ring.pass_on(2)
        for made in writes[-4:]:
            made.wait()
        inner_write = copy(inner, inner_out)
        weight_grads(grad_down, n1, inner, range(chunks))
        inner_write.wait()
        for made in early_writes:
            made.wait()

    pl.run_scoped(
        feed_forward,
        pltpu.VMEM((2, 3, n, block, 256), bf16),
        pltpu.VMEM((2, 2, tok, 256), bf16),
        pltpu.VMEM((tok, units), bf16),
        pltpu.VMEM((tok, early), bf16),
        pltpu.VMEM((tok, early), bf16),
        pltpu.VMEM((2, 2, per, block, early), bf16),
        pltpu.VMEM((2, tok, 256), f32),
        pltpu.VMEM((2, per, block, units), bf16),
    )
    ring.pass_on(len(ring.events))
    for made in sent:
        made.wait_send()
    for made in tp:
        made.wait_send()
    ring.finish()
    for made in saved[1:]:
        made.wait()


def to_early(units):
    return (units // 256 + 1) // 2 * 256


def forward(n, s_qkv, s_out, s_gate, s_up, s_down, tokens, cotangent, cs, sn, start):
    tok, width = tokens.shape
    heads = s_qkv.shape[1] - 128
    units = s_gate.shape[1]
    early = to_early(units)
    quarter = tok // 4
    vm = pl.BlockSpec(memory_space=pltpu.VMEM)
    anywhere = pl.BlockSpec(memory_space=pl.ANY)
    shards = (s_qkv, s_out, s_gate, s_up, s_down)
    return pl.pallas_call(
        functools.partial(forward_kernel, n),
        out_shape=tuple(jax.ShapeDtypeStruct((n,) + s.shape, bf16) for s in shards)
        + (
            jax.ShapeDtypeStruct((tok, width), bf16),
            jax.ShapeDtypeStruct((tok, heads), bf16),
            jax.ShapeDtypeStruct((tok, 128), bf16),
            jax.ShapeDtypeStruct((tok, heads), bf16),
            jax.ShapeDtypeStruct((heads // HD, tok), f32),
            jax.ShapeDtypeStruct((quarter, width), f32),
            jax.ShapeDtypeStruct((tok, width), bf16),
            jax.ShapeDtypeStruct((tok, units - early), bf16),
            jax.ShapeDtypeStruct((tok, units - early), bf16),
            jax.ShapeDtypeStruct((tok, units), bf16),
            jax.ShapeDtypeStruct((n, width // n, units), bf16),
            jax.ShapeDtypeStruct((tok, early), bf16),
            jax.ShapeDtypeStruct((tok, early), bf16),
            jax.ShapeDtypeStruct((width // 256, tok, 256), f32),
        ),
        in_specs=[anywhere] * 7 + [vm] * 3,
        out_specs=(anywhere,) * 6 + (vm,) * 5 + (anywhere,) * 8,
        scratch_shapes=[
            pltpu.VMEM((n,) + s_qkv.shape, bf16),
            pltpu.VMEM((n,) + s_out.shape, bf16),
            pltpu.VMEM((tok, width), bf16),
            pltpu.VMEM((tok, width), bf16),
            pltpu.VMEM((2 * quarter, width), bf16),
            pltpu.VMEM((2 * quarter, width), bf16),
            pltpu.VMEM((quarter, width), f32),
            pltpu.VMEM((quarter, width), bf16),
            pltpu.VMEM((quarter, width), bf16),
            pltpu.VMEM((quarter, width), bf16),
            pltpu.SemaphoreType.DMA((9, 2, n - 1)),
            pltpu.SemaphoreType.DMA((9, 2, n - 1)),
            pltpu.SemaphoreType.DMA((12,)),
            pltpu.SemaphoreType.DMA((12,)),
            pltpu.SemaphoreType.DMA((128,)),
        ],
        compiler_params=pltpu.CompilerParams(collective_id=1, has_side_effects=True, vmem_limit_bytes=62 * 2**20),
    )(*shards, tokens, cotangent, cs, sn, start)


class Later:
    def __init__(self, make):
        self.make = make

    def start(self):
        self.make().start()

    def wait(self):
        self.make().wait()

    def wait_send(self):
        self.make().wait_send()

    def wait_recv(self):
        self.make().wait_recv()


class Reduce:
    def __init__(self, n, chains, pools, send, recv, slot_sem, term_sem):
        self.n, self.chains, self.pools = n, chains, pools
        self.send_sem, self.recv_sem = send, recv
        self.slot_sem, self.term_sem = slot_sem, term_sem
        self.place = ring_place(n, lax.axis_index("dp"))
        self.up = ring_index(n, self.place + 1)
        self.down = ring_index(n, self.place - 1)
        self.origin = [
            [ring_index(n, self.place - 1 - step), ring_index(n, self.place + 1 + step)] for step in range(n)
        ]
        self.events, self.groups, self.waiting, self.used = [], [], [], [0] * len(pools)
        self.busy = [{} for _ in pools]
        self.ready = self.pending = None

    def send(self, chain, step, way, source):
        return Later(
            lambda: pltpu.make_async_remote_copy(
                src_ref=source(),
                dst_ref=self.landing(chain, step, way),
                send_sem=self.send_sem.at[chain, way, step],
                recv_sem=self.recv_sem.at[chain, way, step],
                device_id={"dp": self.up if way == 0 else self.down},
                device_id_type=MESH,
            )
        )

    def landing(self, chain, step, way):
        (slots, first), rows = self.chains[chain][2], self.chains[chain][3 + way]
        return slots.at[first + (step, way, pl.ds(0, rows[1]))]

    def term(self, chain, step, way):
        terms, cols = self.chains[chain][:2]
        rows = pl.ds(*self.chains[chain][3 + way])
        cols = () if cols is None else (pl.ds(*cols),)
        return terms.at[(self.origin[step][way], rows) + cols]

    def part(self, chain, way):
        cols = self.chains[chain][1]
        return (pl.ds(0, self.chains[chain][3 + way][1]),) + (() if cols is None else (pl.ds(0, cols[1]),))

    def start(self, chain):
        for way in (0, 1):
            made = self.send(chain, 0, way, functools.partial(self.term, chain, 0, way))
            made.start()
            self.waiting.append(made)

    def queue(self, chains):
        self.groups.append(chains)
        self.begin()

    def add(self, chain, events=None):
        self.start(chain)
        if events is None:
            before, after, self.events = self.events, [(chain, step) for step in range(self.n - 1)], []
            while before:
                self.events += before[:1] + after[:1]
                before, after = before[1:], after[1:]
            events = after
        self.events += events
        self.fetch()

    def begin(self):
        if self.groups and len(self.events) <= 4:
            chains = self.groups.pop(0)
            for chain in chains:
                self.start(chain)
            self.events += [(chain, step) for step in range(self.n - 1) for chain in chains]
            self.fetch()

    def fetch(self):
        if self.ready is not None or not self.events:
            return
        chain, step = self.events[0]
        pool = self.chains[chain][5]
        arrived, terms = self.pools[pool]
        slot = self.used[pool] % arrived.shape[0]
        self.used[pool] += 1
        for made in self.busy[pool].pop(slot, ()):
            made.wait_send()
        copies = []
        for way in (0, 1):
            copies.append(
                Later(
                    lambda way=way: pltpu.make_async_copy(
                        self.term(chain, step + 1, way),
                        terms.at[(slot, way) + self.part(chain, way)],
                        self.term_sem.at[pool, slot, way],
                    )
                )
            )
            copies[-1].start()
        self.ready = (slot, copies)

    def held(self, chain, way, slot):
        return self.pools[self.chains[chain][5]][0].at[(slot, way) + self.part(chain, way)]

    def pass_on(self, count=1):
        for _ in range(count):
            if not self.events:
                return
            self.flush()
            chain, step = self.events.pop(0)
            pool = self.chains[chain][5]
            slot, copies = self.ready
            self.ready = None
            loads = []
            for way in (0, 1):
                self.send(chain, step, way, functools.partial(self.landing, chain, step, way)).wait_recv()
                loads.append(self.load(chain, step, way, pool, slot))
                loads[-1].start()
            self.pending = (chain, step, slot, copies, loads)
            self.fetch()
            self.begin()

    def load(self, chain, step, way, pool, slot):
        return Later(
            lambda: pltpu.make_async_copy(
                self.landing(chain, step, way), self.held(chain, way, slot), self.slot_sem.at[pool, slot, way]
            )
        )

    def flush(self):
        if self.pending is None:
            return
        chain, step, slot, copies, loads = self.pending
        self.pending = None
        pool, result = self.chains[chain][5:]
        arrived, terms = self.pools[pool]
        sent = []
        for way in (0, 1):
            loads[way].wait()
            copies[way].wait()
            place = (slot, way) + self.part(chain, way)
            total = arrived[place].astype(f32) + terms[place].astype(f32)
            if step + 1 < self.n - 1:
                arrived[place] = total.astype(arrived.dtype)
                sent.append(self.send(chain, step + 1, way, functools.partial(self.held, chain, way, slot)))
                sent[-1].start()
            else:
                result(way, total)
        self.busy[pool][slot] = sent

    def turn(self, due):
        if due:
            self.pass_on()
        else:
            self.flush()

    def hop(self, due=True):
        if due:
            self.pass_on()
            self.flush()

    def drain(self):
        while self.events or self.groups:
            self.pass_on()
        self.flush()

    def finish(self):
        for busy in self.busy:
            for sent in busy.values():
                for made in sent:
                    made.wait_send()
        for made in self.waiting:
            made.wait_send()


def backward_kernel(
    n,
    g_hbm, n2_hbm, n1_hbm, x_hbm, to_gate, to_up, inner_hbm, grad_down, early_dg, early_du, early_dn2,
    w_qkv, w_out, w_gate, w_up, w_down, q_hbm, kv_hbm, ob_hbm, hid_ref, lse_ref, cs_ref, sn_ref, start_ref,
    output, grad_x, r_down, r_gate, r_up, r_out, r_qkv, r_gain,
    grad_gate, grad_up, grad_out, grad_qkv, grad_gain, l_down, l_gate, l_up, l_out, l_qkv, l_gain,
    tile, part, near, far_part, far, keep, dh, gh, rows_in, own_rows, dqkv, stage, stage_o, fin, fin_o, fin_q, gain_sum,
    pool_a, pool_b, pool_c, pool_d, pool_e, pool_f, pool_g, pool_h, gain_rows, gain_in, gain_tile, gain_out,
    ring_send, ring_recv, slot_sem, term_sem, tp_send, tp_recv, credit, local,
):
    tok, width = dh.shape
    block = width // n
    per = 256 // block
    chunks = width // 256
    units = w_gate.shape[2]
    heads = ob_hbm.shape[1]
    quarter = tok // 4
    sub = quarter // 2
    h = block // 2
    ho = heads // 2
    t = lax.axis_index("tensor")
    c, y = t % 2, t // 2
    mate = y * 2 + (1 - c)
    across = (1 - y) * 2 + c
    diagonal = (1 - y) * 2 + (1 - c)
    first_row = (2 * c + y) * quarter
    other_row = (2 * c + 1 - y) * quarter
    count = [0, 0]

    def rows_at(first, rows):
        return pl.ds(pl.multiple_of(first, 16), rows)

    own_rows_at = rows_at(first_row, quarter)
    own_subs = [rows_at(first_row + i * sub, sub) for i in (0, 1)]
    other_subs = [rows_at(other_row + i * sub, sub) for i in (0, 1)]
    sent_half = rows_at((1 - c) * 2 * quarter, 2 * quarter)
    sent_tile, kept_tile = (rows_at((2 * c + at) * quarter, quarter) for at in (1 - y, y))
    sent_quarter, kept_quarter = rows_at((1 - y) * quarter, quarter), rows_at(y * quarter, quarter)

    def now(place):
        return place() if callable(place) else place

    def copy(source, target):
        k = count[0]
        count[0] += 1
        made = Later(lambda: pltpu.make_async_copy(now(source), now(target), local.at[k]))
        made.start()
        return made

    def remote(source, target, device):
        k = count[1]
        count[1] += 1
        return Later(
            lambda: pltpu.make_async_remote_copy(
                src_ref=now(source), dst_ref=now(target), send_sem=tp_send.at[k], recv_sem=tp_recv.at[k],
                device_id={"tensor": device}, device_id_type=MESH,
            )
        )

    def to(result, buffer, writes, firsts, cols=None):
        def write(way, total):
            if len(writes) >= 2:
                writes[-2].wait()
            rows = pl.ds(0, total.shape[0])
            slot = len(writes) % 2
            lanes = () if cols is None else (pl.ds(0, cols[1]),)
            buffer[(slot, rows) + lanes] = total
            target = (pl.ds(firsts[way], total.shape[0]),) + (() if cols is None else (pl.ds(*cols),))
            writes.append(copy(lambda: buffer.at[(slot, rows) + lanes], lambda: result.at[target]))

        return write

    early = to_early(units)
    def gain_done(way, total):
        if way == 0:
            gain_sum[...] = total

    written = [[], [], []]
    chains = [
        (grad_down, None, (l_down, (0,)), (0, h // 2), (h, h // 2), 0, to(r_down, fin, written[0], (0, h))),
        (
            grad_down, None, (l_down, (1,)), (h // 2, h // 2), (h + h // 2, h // 2), 0,
            to(r_down, fin, written[0], (h // 2, h + h // 2)),
        ),
        (grad_gate, None, (l_gate, ()), (0, h), (h, h), 0, to(r_gate, fin, written[0], (0, h))),
        (grad_up, None, (l_up, ()), (0, h), (h, h), 0, to(r_up, fin, written[0], (0, h))),
        (grad_out, None, (l_out, ()), (0, ho), (ho, ho), 1, to(r_out, fin_o, written[1], (0, ho))),
        (grad_qkv, None, (l_qkv, ()), (0, h), (h, h), 2, to(r_qkv, fin_q, written[2], (0, h))),
        (grad_gain, None, (l_gain, ()), (0, 8), (8, 8), 3, gain_done),
    ]
    pools = [(pool_a, pool_b), (pool_c, pool_d), (pool_e, pool_f), (pool_g, pool_h)]
    ring = Reduce(n, chains, pools, ring_send, ring_recv, slot_sem, term_sem)
    barrier = pltpu.get_barrier_semaphore()
    for device in ({"dp": ring.up}, {"dp": ring.down}, {"tensor": mate}, {"tensor": across}, {"tensor": diagonal}):
        pl.semaphore_signal(barrier, inc=1, device_id=device, device_id_type=MESH)
    gain_load = copy(w_qkv.at[:, pl.ds(block, 16)], gain_tile)

    def gain(k):
        parts = [gain_tile[i, :1, k * block : (k + 1) * block].astype(f32) for i in range(n)]
        return jnp.concatenate(parts, axis=1)

    class Sum:
        def __init__(self, at_once=True):
            self.near, self.far, self.at_once = [], [], at_once

        def put(self, j, value):
            tile[j % 2] = value
            part[j] = tile[j % 2, sent_half, :].astype(bf16)
            self.near.append(remote(lambda: part.at[j], lambda: near.at[j], mate))
            self.near[j].start()
            if j > 0:
                self.absorb(j - 1)
            if j == chunks - 1:
                self.absorb(j)

        def absorb(self, j):
            self.near[j].wait_recv()
            far_part[j] = (tile[j % 2, sent_tile, :] + near[j, sent_quarter, :].astype(f32)).astype(bf16)
            keep[:, j * 256 : (j + 1) * 256] = tile[j % 2, kept_tile, :] + near[j, kept_quarter, :].astype(f32)
            self.far.append(remote(lambda: far_part.at[j], lambda: far.at[j], across))
            if self.at_once:
                self.far[j].start()

        def send_far(self):
            for made in self.far:
                made.start()
            self.at_once = True

        def finish(self, due=()):
            for j in range(chunks):
                ring.turn(j in due)
                self.far[j].wait_recv()
                keep[:, j * 256 : (j + 1) * 256] += far[j].astype(f32)
            for made in self.near + self.far:
                made.wait_send()

    class Spread:
        def __init__(self, whole):
            self.whole, self.far, self.near, self.last = whole, [], [], []

        def put(self, i, source):
            place = lambda: self.whole.at[own_subs[i]]
            self.far.append(remote(source, place, across))
            self.far[i].start()
            self.near.append(remote(source, place, mate))
            self.near[i].start()

        def forward(self, calls):
            for i in (0, 1):
                ring.pass_on(calls[i])
                ring.flush()
                self.far[i].wait_recv()
                place = lambda i=i: self.whole.at[other_subs[i]]
                self.last.append(remote(place, place, mate))
                self.last[i].start()

        def arrive_near(self):
            for made in self.near:
                made.wait_recv()

        def arrive(self):
            for made in self.last:
                made.wait_recv()

        def close(self):
            for made in self.far + self.near + self.last:
                made.wait_send()

    def through_norm(values, gain, base, put):
        gain_grad = 0.0
        for i in (0, 1):
            rows = slice(i * sub, (i + 1) * sub)
            z = values[rows, :].astype(f32)
            inverse = lax.rsqrt(jnp.mean(z * z, axis=-1, keepdims=True) + norm_eps)
            scaled = z * inverse
            grad = keep[rows, :]
            gain_grad = gain_grad + jnp.sum(grad * scaled, axis=0, keepdims=True)
            grad = grad * gain
            grad = inverse * (grad - scaled * jnp.mean(grad * scaled, axis=-1, keepdims=True))
            put(i, rows, base[rows, :].astype(f32) + grad)
        return gain_grad

    def weight_grads(target, left, right):
        writes = []
        cols = right.shape[1]
        for j in range(chunks):
            if j >= 2:
                writes[j - 2].wait()
            grad = mm_tn(left[:, j * 256 : (j + 1) * 256], right[...]).astype(bf16)
            stage[j % 2, :, :, :cols] = grad.reshape(per, block, cols)
            writes.append(copy(stage.at[j % 2, :, :, pl.ds(0, cols)], target.at[pl.ds(j * per, per)]))
            yield j
        writes[-2].wait()
        writes[-1].wait()

    hid_sum, out_sum, x_sum = Sum(), Sum(False), Sum()
    spread, result, last = Spread(dh), Spread(output), Spread(grad_x)
    gain_rows[...] = jnp.zeros_like(gain_rows)

    def feed_forward(acts, dg, du, weight, sums, wtile):
        late = units - early
        tiles = [(first, min(256, units - first)) for first in range(early, units, 256)]

        def tile_load(j):
            first, wide = tiles[j]
            return copy(w_down.at[:, :, pl.ds(first, wide)], wtile.at[j % 2, :, :, pl.ds(0, wide)])

        def late_load(j):
            made = [
                copy(s.at[pl.ds(j * per, per), :, pl.ds(early, late)], weight.at[j % 2, k, :, :, pl.ds(0, late)])
                for k, s in enumerate((w_gate, w_up))
            ]
            return made + [copy(early_dn2.at[j], sums.at[j % 2])]

        def block_load(j):
            return copy(w_down.at[pl.ds(j * per, per)], weight.at[j % 2, 0])

        acts_load = copy(g_hbm, acts)
        tile_loads = [tile_load(0)]
        factors = [copy(to_gate, dg.at[:, pl.ds(early, late)]), copy(to_up, du.at[:, pl.ds(early, late)])]
        loads = [late_load(0)]
        row_load = copy(g_hbm.at[own_rows_at], rows_in)
        firsts = [copy(early_dg, dg.at[:, pl.ds(0, early)]), copy(early_du, du.at[:, pl.ds(0, early)])]
        pl.semaphore_wait(barrier, 5)
        ring.queue([0, 1])
        acts_load.wait()
        for j, (first, wide) in enumerate(tiles):
            if j + 1 < len(tiles):
                tile_loads.append(tile_load(j + 1))
            tile_loads[j].wait()
            grad = mm(acts[...], wtile[j % 2, :, :, :wide].reshape(width, wide))
            if j == 0:
                for made in factors:
                    made.wait()
            cols = slice(first, first + wide)
            dg[:, cols] = (grad * dg[:, cols].astype(f32)).astype(bf16)
            du[:, cols] = (grad * du[:, cols].astype(f32)).astype(bf16)
            ring.hop(j > 0)
        for j in range(chunks):
            if j + 1 < chunks:
                loads.append(late_load(j + 1))
            if j == 0:
                acts_load = copy(n2_hbm, acts)
            for made in loads[j]:
                made.wait()

            value = mm_nt(dg[:, early:], weight[j % 2, 0, :, :, :late].reshape(256, late))
            value = value + mm_nt(du[:, early:], weight[j % 2, 1, :, :, :late].reshape(256, late))
            hid_sum.put(j, value + sums[j % 2])
            ring.hop(j % 3 != 2)
        loads = [block_load(0)]
        acts_load.wait()
        for made in firsts:
            made.wait()
        def put(i, rows, grad):
            gh[rows, :] = grad
            place = own_subs[i]
            dh[place, :] = grad.astype(bf16)
            spread.put(i, lambda: dh.at[place])

        for j in weight_grads(grad_gate, acts, dg):
            ring.hop(j in (1, 4, 6))
            if j == 3:
                gain_load.wait()
                row_load.wait()
                hid_sum.finish()
                gain_rows[1:2, :] = through_norm(hid_ref, gain(1), rows_in, put)
                ring.hop()
        inner_load = copy(inner_hbm, dg)
        ring.add(2, [(2, 0), (2, 1)])
        for j in weight_grads(grad_up, acts, du):
            ring.turn(j in (1, 3, 6))
        steps = n - 1
        ring.add(3, [pair for s in range(steps) for pair in ((3, s), (2, s + 2)) if pair[1] < steps])
        spread.arrive_near()
        inner_load.wait()
        for j in range(chunks):
            if j + 1 < chunks:
                loads.append(block_load(j + 1))
            loads[j].wait()
            out_sum.put(j, mm_nt(dg[...], weight[j % 2, 0].reshape(256, units)))
            ring.turn(j in (1, 3, 5))
            if j == 6:
                spread.forward((1, 0))
                out_sum.send_far()

    pl.run_scoped(
        feed_forward,
        pltpu.VMEM((tok, width), bf16),
        pltpu.VMEM((tok, units), bf16),
        pltpu.VMEM((tok, units), bf16),
        pltpu.VMEM((2, 2, per, block, units), bf16),
        pltpu.VMEM((2, tok, 256), f32),
        pltpu.VMEM((2, n, block, 256), bf16),
    )
    ring.turn(True)
    spread.arrive()
    ring.turn(False)

    def attention(q, kv, ob, v_out, v_qkv, dob, ka, kb, va, vb, dk, dv):
        pairs = ((w_out, v_out), (q_hbm, q), (kv_hbm, kv), (w_qkv, v_qkv), (ob_hbm, ob))
        loads = [copy(source, target) for source, target in pairs]
        loads[0].wait()
        for i in (0, 1):
            rows = slice(2 * i * quarter, 2 * (i + 1) * quarter)
            total = 0.0
            for j in range(n):
                total = total + mm_nt(dh[rows, j * block : (j + 1) * block], v_out[j])
            dob[rows, :] = total.astype(bf16)
        loads[1].wait()
        loads[2].wait()
        attn_backward(
            q, kv, dob, lse_ref, cs_ref, sn_ref, start_ref, dqkv, ka, kb, va, vb, dk, dv,
            {i: functools.partial(ring.turn, i in (1, 3, 6, 8)) for i in range(tok // QB)},
        )
        out_sum.finish()
        own_rows[...] = (hid_ref[...] + keep[...]).astype(bf16)
        for k, device in enumerate((mate, across)):
            pl.semaphore_signal(credit.at[k], inc=1, device_id={"tensor": device}, device_id_type=MESH)
        loads[3].wait()
        loads[4].wait()
        pl.semaphore_wait(credit.at[0], 1)
        pl.semaphore_wait(credit.at[1], 1)
        for j in range(chunks):
            weight = v_qkv[j * per : (j + 1) * per, :block].reshape(256, heads + 128)
            x_sum.put(j, mm_nt(dqkv[...], weight))
            ring.turn(j in (2, 6))
        writes = []
        for j in range(n):
            if j >= 2:
                writes[j - 2].wait()
            stage_o[j % 2] = mm_tn(ob[...], dh[:, j * block : (j + 1) * block]).astype(bf16)
            writes.append(copy(stage_o.at[j % 2], grad_out.at[j]))
            ring.turn(j in (2, n - 2))
        writes[-2].wait()
        writes[-1].wait()

    row_load = copy(x_hbm.at[own_rows_at], rows_in)
    pl.run_scoped(
        attention,
        pltpu.VMEM((tok, heads), bf16),
        pltpu.VMEM((tok, 128), bf16),
        pltpu.VMEM((tok, heads), bf16),
        pltpu.VMEM((n, heads, block), bf16),
        pltpu.VMEM((n, block + 16, heads + 128), bf16),
        pltpu.VMEM((tok, heads), bf16),
        *[pltpu.VMEM((tok, 128), bf16)] * 4,
        *[pltpu.VMEM((tok, 128), f32)] * 2,
    )
    owns = [copy(own_rows, output.at[own_rows_at])]

    def projections(acts):
        copy(n1_hbm, acts).wait()
        for j in weight_grads(grad_qkv, acts, dqkv):
            ring.turn(j in (2, 6))
            if j == 2:
                for i in (0, 1):
                    result.put(i, lambda i=i: own_rows.at[pl.ds(i * sub, sub)])

    pl.run_scoped(projections, pltpu.VMEM((tok, width), bf16))
    ring.queue([4, 5])
    row_load.wait()
    x_sum.finish((1, 4, 7))

    def put(i, rows, grad):
        rows_in[rows, :] = grad.astype(bf16)
        last.put(i, lambda: rows_in.at[pl.ds(i * sub, sub)])

    gain_rows[0:1, :] = through_norm(rows_in, gain(0), gh, put)
    owns.append(copy(rows_in, grad_x.at[own_rows_at]))
    for i in range(n):
        both = [gain_rows[k : k + 1, i * block : (i + 1) * block] for k in (0, 1)]
        gain_out[i] = jnp.broadcast_to(jnp.concatenate(both, axis=1), (16, 2 * block))
    copy(gain_out, grad_gain).wait()
    ring.turn(True)
    ring.add(6)
    result.forward((1, 3))
    last.forward((4, 4))
    ring.drain()
    gain_in[t] = gain_sum[...]
    shares = [remote(gain_sum, gain_in.at[t], device) for device in (mate, across, diagonal)]
    for made in shares:
        made.start()
    for made in shares:
        made.wait()
    gain_sum[...] = (gain_in[0] + gain_in[1]) + (gain_in[2] + gain_in[3])
    owns.append(copy(gain_sum, r_gain))
    for spreading in (result, last):
        spreading.arrive_near()
        spreading.arrive()
    for spreading in (spread, result, last):
        spreading.close()
    ring.finish()
    for made in owns:
        made.wait()
    for writes in written:
        for made in writes[-2:]:
            made.wait()


def backward(n, g, n2, n1, x, to_gate, to_up, inner, grads, w_qkv, w_out, w_gate, w_up, w_down, q, kv, ob, hid, lse, cs, sn, start):
    tok, width = x.shape
    block = width // n
    h = block // 2
    heads, units = ob.shape[1], inner.shape[1]
    quarter = tok // 4
    per, chunks = 256 // block, width // 256
    vm = pl.BlockSpec(memory_space=pltpu.VMEM)
    anywhere = pl.BlockSpec(memory_space=pl.ANY)
    hbm = jax.ShapeDtypeStruct
    qkv = heads + 128
    return pl.pallas_call(
        functools.partial(backward_kernel, n),
        out_shape=(
            hbm((tok, width), bf16),
            hbm((tok, width), bf16),
            hbm((block, units), f32),
            hbm((block, units), f32),
            hbm((block, units), f32),
            hbm((heads, block), f32),
            hbm((block, qkv), f32),
            hbm((8, 2 * block), f32),
            hbm((n, block, units), bf16),
            hbm((n, block, units), bf16),
            hbm((n, heads, block), bf16),
            hbm((n, block, qkv), bf16),
            hbm((n, 16, 2 * block), f32),
            hbm((2, n - 1, 2, h // 2, units), bf16),
            hbm((n - 1, 2, h, units), bf16),
            hbm((n - 1, 2, h, units), bf16),
            hbm((n - 1, 2, heads // 2, block), bf16),
            hbm((n - 1, 2, h, qkv), bf16),
            hbm((n - 1, 2, 8, 2 * block), f32),
        ),
        in_specs=[anywhere] * 19 + [vm] * 5,
        out_specs=(anywhere,) * 19,
        scratch_shapes=[
            pltpu.VMEM((2, tok, 256), f32),
            pltpu.VMEM((chunks, 2 * quarter, 256), bf16),
            pltpu.VMEM((chunks, 2 * quarter, 256), bf16),
            pltpu.VMEM((chunks, quarter, 256), bf16),
            pltpu.VMEM((chunks, quarter, 256), bf16),
            pltpu.VMEM((quarter, width), f32),
            pltpu.VMEM((tok, width), bf16),
            pltpu.VMEM((quarter, width), f32),
            pltpu.VMEM((quarter, width), bf16),
            pltpu.VMEM((quarter, width), bf16),
            pltpu.VMEM((tok, qkv), bf16),
            pltpu.VMEM((2, per, block, units), bf16),
            pltpu.VMEM((2, heads, block), bf16),
            pltpu.VMEM((2, h, units), f32),
            pltpu.VMEM((2, heads // 2, block), f32),
            pltpu.VMEM((2, h, qkv), f32),
            pltpu.VMEM((8, 2 * block), f32),
            pltpu.VMEM((3, 2, h, units), bf16),
            pltpu.VMEM((3, 2, h, units), bf16),
            pltpu.VMEM((2, 2, heads // 2, block), bf16),
            pltpu.VMEM((2, 2, heads // 2, block), bf16),
            pltpu.VMEM((2, 2, h, qkv), bf16),
            pltpu.VMEM((2, 2, h, qkv), bf16),
            pltpu.VMEM((2, 2, 8, 2 * block), f32),
            pltpu.VMEM((2, 2, 8, 2 * block), f32),
            pltpu.VMEM((8, width), f32),
            pltpu.VMEM((4, 8, 2 * block), f32),
            pltpu.VMEM((n, 16, qkv), bf16),
            pltpu.VMEM((n, 16, 2 * block), f32),
            pltpu.SemaphoreType.DMA((7, 2, n - 1)),
            pltpu.SemaphoreType.DMA((7, 2, n - 1)),
            pltpu.SemaphoreType.DMA((4, 4, 2)),
            pltpu.SemaphoreType.DMA((4, 4, 2)),
            pltpu.SemaphoreType.DMA((80,)),
            pltpu.SemaphoreType.DMA((80,)),
            pltpu.SemaphoreType.REGULAR((2,)),
            pltpu.SemaphoreType.DMA((160,)),
        ],
        compiler_params=pltpu.CompilerParams(collective_id=2, has_side_effects=True, vmem_limit_bytes=62 * 2**20),
    )(g, n2, n1, x, to_gate, to_up, inner, *grads, w_qkv, w_out, w_gate, w_up, w_down, q, kv, ob, hid, lse, cs, sn, start)


def prep_kernel(q_ref, k_ref, v_ref, d_ref, g1_ref, g2_ref, qkv_ref, dt_ref):
    rows, cols = q_ref.shape
    qkv_ref[:rows, :cols] = q_ref[...]
    qkv_ref[:rows, cols:] = jnp.concatenate([k_ref[...], v_ref[...]], axis=1)
    qkv_ref[rows:, :] = jnp.zeros((16, qkv_ref.shape[1]), bf16)
    gains = jnp.concatenate([g1_ref[...], g2_ref[...]], axis=1).astype(f32)
    qkv_ref[rows:, : 2 * rows] = jnp.broadcast_to(gains, (16, 2 * rows)).astype(bf16)
    dt_ref[...] = jnp.transpose(d_ref[...].astype(f32)).astype(bf16)


def prep(w_query, w_key, w_value, w_down, gain_attn, gain_mlp):
    rows, cols = w_query.shape
    vm = pl.BlockSpec(memory_space=pltpu.VMEM)
    return pl.pallas_call(
        prep_kernel,
        out_shape=(
            jax.ShapeDtypeStruct((rows + 16, cols + 128), bf16),
            jax.ShapeDtypeStruct(w_down.shape[::-1], bf16),
        ),
        in_specs=[vm] * 6,
        out_specs=(vm,) * 2,
        compiler_params=pltpu.CompilerParams(vmem_limit_bytes=32 * 2**20),
    )(w_query, w_key, w_value, w_down, gain_attn.reshape(1, -1), gain_mlp.reshape(1, -1))


def per_device(
    n_dp,
    tokens,
    gain_attn,
    w_query,
    w_key,
    w_value,
    w_out,
    gain_mlp,
    w_gate,
    w_up,
    w_down,
    lengths,
    cotangent,
):
    tok, width = tokens.shape
    line = n_dp // 2
    block = width // n_dp
    cols = w_query.shape[1]
    ends = jnp.cumsum(lengths[0], dtype=jnp.int32)
    starts = ends - lengths[0]
    places = jnp.arange(tok, dtype=jnp.int32)
    inside = (places[:, None] >= starts[None, :]) & (places[:, None] < ends[None, :])
    start = jnp.sum(jnp.where(inside, starts[None, :], 0), axis=1, dtype=jnp.int32)
    freqs = rope_base ** (-jnp.arange(HD // 2, dtype=f32) * 2.0 / HD)
    angles = (places - start).astype(f32)[:, None] * freqs[None, :]
    cosine, sine = jnp.cos(angles), jnp.sin(angles)
    cs = jnp.concatenate([cosine] * 4, axis=1)
    sn = jnp.concatenate([-sine, sine, -sine, sine], axis=1)

    p_qkv, p_down = prep(w_query, w_key, w_value, w_down, gain_attn, gain_mlp)
    w_qkv, w_out_all, w_g, w_u, w_d, n1, q, kv, ob, lse, hidden, n2, to_gate, to_up, inner, *grads = forward(
        n_dp, p_qkv, w_out, w_gate, w_up, p_down, tokens, cotangent, cs, sn, start[:, None]
    )
    output, grad_tokens, s_down, s_gate, s_up, s_out, s_qkv, s_gain = backward(
        n_dp, cotangent, n2, n1, tokens, to_gate, to_up, inner, grads, w_qkv, w_out_all, w_g, w_u, w_d,
        q, kv, ob, hidden, lse, cs, sn, start[None, :]
    )[:8]
    return (
        output,
        grad_tokens.astype(f32),
        s_qkv[:, :cols],
        s_qkv[:, cols : cols + HD],
        s_qkv[:, cols + HD :],
        s_out,
        s_gate,
        s_up,
        s_down.T,
        s_gain[0, :block],
        s_gain[0, block:],
    )


def solution(mesh):
    placed = (
        P("dp", None),
        P("dp"),
        P("dp", "tensor"),
        P("dp", "tensor"),
        P("dp", "tensor"),
        P("tensor", "dp"),
        P("dp"),
        P("dp", "tensor"),
        P("dp", "tensor"),
        P("tensor", "dp"),
        P("dp", None),
        P("dp", None),
    )
    return jax.shard_map(
        functools.partial(per_device, mesh.shape["dp"]),
        mesh=mesh,
        in_specs=placed,
        out_specs=(
            P("dp", None),
            P("dp", None),
            P("dp", "tensor"),
            P("dp", "tensor"),
            P("dp", "tensor"),
            P("tensor", "dp"),
            P("dp", "tensor"),
            P("dp", "tensor"),
            P("tensor", "dp"),
            P("dp"),
            P("dp"),
        ),
        check_vma=False,
    )
```

```python
import functools

import jax
import jax.numpy as jnp
from jax import lax
from jax.experimental import pallas as pl
from jax.experimental.pallas import tpu as pltpu
from jax.sharding import PartitionSpec as P

HD = 64
QB = 128


def swap_halves(z):
    lane = lax.broadcasted_iota(jnp.int32, z.shape, 1)
    return jnp.where(lane % HD < HD // 2, pltpu.roll(z, 128 - HD // 2, 1), pltpu.roll(z, HD // 2, 1))


def nt(a, b):
    return lax.dot_general(a, b, (((1,), (1,)), ((), ())), preferred_element_type=jnp.float32)


def attn_forward(qkv_ref, cs_ref, sn_ref, start_ref, q_ref, kv_ref, ob_ref, lse_ref, ka, kb, va, vb, between=()):
    tok = qkv_ref.shape[0]
    width = q_ref.shape[1]
    pairs = width // 128
    lane = lax.broadcasted_iota(jnp.int32, (tok, 128), 1)
    cs = cs_ref[...]
    sn = sn_ref[...]
    kv = qkv_ref[:, width:]
    krot = kv * cs + swap_halves(kv) * sn
    kvr = jnp.where(lane < HD, krot, kv).astype(jnp.bfloat16)
    kv_ref[...] = kvr
    kvf = kvr.astype(jnp.float32)
    rolled = pltpu.roll(kvf, HD, 1)
    ka[...] = jnp.where(lane < HD, kvf, 0.0).astype(jnp.bfloat16)
    kb[...] = jnp.where(lane < HD, 0.0, rolled).astype(jnp.bfloat16)
    va[...] = jnp.where(lane < HD, rolled, 0.0).astype(jnp.bfloat16)
    vb[...] = jnp.where(lane < HD, 0.0, kvf).astype(jnp.bfloat16)
    for i in range(tok // QB):
        rows = pl.ds(i * QB, QB)
        kp = (i + 1) * QB
        qs = []
        for p in range(pairs):
            z = qkv_ref[rows, p * 128:(p + 1) * 128]
            r = (z * cs_ref[rows, :] + swap_halves(z) * sn_ref[rows, :]).astype(jnp.bfloat16)
            r = (r.astype(jnp.float32) * 0.125).astype(jnp.bfloat16)
            q_ref[rows, p * 128:(p + 1) * 128] = r
            qs.append(r)
        qe = jnp.concatenate(qs, axis=0)
        col = lax.broadcasted_iota(jnp.int32, (QB, kp), 1)
        row = lax.broadcasted_iota(jnp.int32, (QB, kp), 0) + i * QB
        seen = (col <= row) & (col >= start_ref[rows, :])
        bias = jnp.where(seen, 0.0, -1e30)
        total = 0.0
        lse_tile = jnp.zeros((QB, 128), jnp.float32)
        lane_b = lax.broadcasted_iota(jnp.int32, (QB, 128), 1)
        for odd, (k2, v2) in enumerate(((ka, va), (kb, vb))):
            s = nt(qe, k2[:kp, :]).reshape(pairs, QB, kp) + bias[None]
            m = jnp.max(s, axis=-1, keepdims=True)
            e = jnp.exp(s - m)
            l = jnp.sum(e, axis=-1, keepdims=True)
            o = jnp.dot(e.astype(jnp.bfloat16).reshape(pairs * QB, kp), v2[:kp, :], preferred_element_type=jnp.float32)
            total = total + o.reshape(pairs, QB, 128) / l
            lse = m + jnp.log(l)
            for p in range(pairs):
                lse_tile = jnp.where(lane_b == 2 * p + odd, lse[p], lse_tile)
        for p in range(pairs):
            ob_ref[rows, p * 128:(p + 1) * 128] = total[p].astype(jnp.bfloat16)
        lse_ref[:, i * QB:(i + 1) * QB] = jnp.transpose(lse_tile)[: 2 * pairs]
        if i in between:
            between[i]()


def attn_backward(q_ref, kv_ref, dob_ref, lse_ref, cs_ref, sn_ref, start_ref, out_ref, ka, kb, va, vb, dk, dv, between=()):
    tok, width = q_ref.shape
    pairs = width // 128
    lane = lax.broadcasted_iota(jnp.int32, (tok, 128), 1)
    kvf = kv_ref[...].astype(jnp.float32)
    rolled = pltpu.roll(kvf, HD, 1)
    ka[...] = jnp.where(lane < HD, kvf, 0.0).astype(jnp.bfloat16)
    kb[...] = jnp.where(lane < HD, 0.0, rolled).astype(jnp.bfloat16)
    va[...] = jnp.where(lane < HD, rolled, 0.0).astype(jnp.bfloat16)
    vb[...] = jnp.where(lane < HD, 0.0, kvf).astype(jnp.bfloat16)
    dk[...] = jnp.zeros_like(dk)
    dv[...] = jnp.zeros_like(dv)
    for i in range(tok // QB):
        rows = pl.ds(i * QB, QB)
        kp = (i + 1) * QB
        qe = jnp.concatenate([q_ref[rows, p * 128:(p + 1) * 128] for p in range(pairs)], axis=0)
        de = jnp.concatenate([dob_ref[rows, p * 128:(p + 1) * 128] for p in range(pairs)], axis=0)
        key = lax.broadcasted_iota(jnp.int32, (kp, QB), 0)
        query = lax.broadcasted_iota(jnp.int32, (kp, QB), 1) + i * QB
        seen = (key <= query) & (key >= start_ref[:, i * QB:(i + 1) * QB])
        bias = jnp.where(seen, 0.0, -1e30)
        bias = jnp.concatenate([bias] * pairs, axis=1)
        dq = 0.0
        parts = []
        for odd, (k2, v2) in enumerate(((ka, va), (kb, vb))):
            lse = jnp.concatenate([lse_ref[2 * p + odd:2 * p + odd + 1, i * QB:(i + 1) * QB] for p in range(pairs)], axis=1)
            s = nt(k2[:kp, :], qe)
            pt = jnp.exp(s + bias - lse)
            dp = nt(v2[:kp, :], de)
            delta = jnp.sum(pt * dp, axis=0, keepdims=True)
            ds = (pt * (dp - delta)).astype(jnp.bfloat16)
            dvo = jnp.dot(pt.astype(jnp.bfloat16), de, preferred_element_type=jnp.float32)
            dko = jnp.dot(ds, qe, preferred_element_type=jnp.float32)
            parts.append((dko, dvo))
            dq = dq + lax.dot_general(ds, k2[:kp, :], (((0,), (0,)), ((), ())), preferred_element_type=jnp.float32)
        lk = lane[:kp]
        dk[:kp, :] += jnp.where(lk < HD, parts[0][0], parts[1][0])
        dv[:kp, :] += jnp.where(lk < HD, parts[0][1], parts[1][1])
        cs = cs_ref[rows, :]
        sn = sn_ref[rows, :]
        for p in range(pairs):
            y = dq[p * QB:(p + 1) * QB] * 0.125
            out_ref[rows, p * 128:(p + 1) * 128] = (y * cs - swap_halves(y) * sn).astype(jnp.bfloat16)
        if i in between:
            between[i]()
    dkf = dk[...]
    dkf = dkf + pltpu.roll(dkf, HD, 1)
    dkf = dkf * cs_ref[...] - swap_halves(dkf) * sn_ref[...]
    dvf = dv[...]
    dvf = dvf + pltpu.roll(dvf, HD, 1)
    out_ref[:, width:] = jnp.where(lane < HD, dkf, dvf).astype(jnp.bfloat16)


norm_eps = 1e-05
rope_base = 10000.0
bf16 = jnp.bfloat16
f32 = jnp.float32


def mm(a, b):
    return jnp.dot(a, b, preferred_element_type=f32)


def mm_nt(a, b):
    return lax.dot_general(a, b, (((1,), (1,)), ((), ())), preferred_element_type=f32)


def mm_tn(a, b):
    return lax.dot_general(a, b, (((0,), (0,)), ((), ())), preferred_element_type=f32)


MESH = pl.DeviceIdType.MESH


def ring_place(n, index):
    odd = index % 2
    return (1 - odd) * (index // 2) + odd * (n - 1 - index // 2)


def ring_index(n, place):
    place = (place + 2 * n) % n
    far = place // (n // 2)
    return (1 - far) * 2 * place + far * (2 * (n - 1 - place) + 1)


class Gather:
    def __init__(self, n, chains, send, recv):
        self.n, self.chains, self.send_sem, self.recv_sem = n, chains, send, recv
        self.place = ring_place(n, lax.axis_index("dp"))
        self.up = ring_index(n, self.place + 1)
        self.down = ring_index(n, self.place - 1)
        self.sent, self.events, self.groups = [], [], []

    def copy(self, chain, step, way):
        first, whole, cols, *rows = self.chains[chain]
        rows = pl.ds(*rows[way])
        cols = () if cols is None else (pl.ds(*cols),)
        origin = ring_index(self.n, self.place - step if way == 0 else self.place + step)
        place = whole.at[(origin, rows) + cols]
        return pltpu.make_async_remote_copy(
            src_ref=first.at[(rows,) + cols] if step == 0 else place,
            dst_ref=place,
            send_sem=self.send_sem.at[chain, way, step],
            recv_sem=self.recv_sem.at[chain, way, step],
            device_id={"dp": self.up if way == 0 else self.down},
            device_id_type=MESH,
        )

    def start(self, chain, step):
        for way in (0, 1):
            self.copy(chain, step, way).start()
        self.sent.append((chain, step))

    def queue(self, chains):
        self.groups.append(chains)
        self.begin()

    def begin(self):
        if self.groups and len(self.events) <= 1:
            chains = self.groups.pop(0)
            for chain in chains:
                self.start(chain, 0)
            self.events += [(chain, step) for step in range(self.n - 1) for chain in chains]

    def pass_on(self, count=1):
        for _ in range(count):
            if not self.events:
                return
            chain, step = self.events.pop(0)
            for way in (0, 1):
                self.copy(chain, step, way).wait_recv()
            if step + 1 < self.n - 1:
                self.start(chain, step + 1)
            self.begin()

    def through(self, chains):
        while any(chain in chains for chain, _ in self.events) or any(set(g) & set(chains) for g in self.groups):
            self.pass_on()

    def finish(self):
        for chain, step in self.sent:
            for way in (0, 1):
                self.copy(chain, step, way).wait_send()


def forward_kernel(
    n,
    s_qkv, s_out, s_gate, s_up, s_down, tokens, cotangent, cs_ref, sn_ref, start_ref,
    w_qkv, w_out, w_gate, w_up, w_down, n1_out, q_ref, kv_ref, ob_ref, lse_ref, hid_ref,
    n2_out, to_gate_out, to_up_out, inner_out, grad_down, dg_out, du_out, dn2_out,
    v_qkv, v_out, n1, n2, part, near, keep, far_part, far, own_n2, ring_send, ring_recv, tp_send, tp_recv, local,
):
    tok, width = n1.shape
    block = width // n
    quarter = tok // 4
    sub = quarter // 2
    units = s_gate.shape[1]
    early = to_early(units)
    index = lax.axis_index("dp")
    t = lax.axis_index("tensor")
    c, y = t % 2, t // 2
    mate = y * 2 + (1 - c)
    across = (1 - y) * 2 + c
    h = block // 2
    ho = s_out.shape[0] // 2
    chains = [(s_qkv, v_qkv, None, (0, h + 16), (h + 16, h)), (s_out, v_out, None, (0, ho), (ho, ho))]
    for cols in ((0, early), (early, units - early)):
        for shard, whole in ((s_gate, w_gate), (s_up, w_up), (s_down, w_down)):
            chains.append((shard, whole, cols, (0, h), (h, h)))
    chains[-1:] = [
        (s_down, w_down, (early, units - early), (0, h // 2), (h, h // 2)),
        (s_down, w_down, (early, units - early), (h // 2, h // 2), (h + h // 2, h // 2)),
    ]
    ring = Gather(n, chains, ring_send, ring_recv)
    barrier = pltpu.get_barrier_semaphore()
    for device in ({"dp": ring.up}, {"dp": ring.down}, {"tensor": mate}, {"tensor": across}):
        pl.semaphore_signal(barrier, inc=1, device_id=device, device_id_type=MESH)

    used = []

    def copy(source, target):
        made = pltpu.make_async_copy(source, target, local.at[len(used)])
        made.start()
        used.append(made)
        return made

    whole = copy(tokens, n2)
    pairs = ((s_qkv, v_qkv), (s_out, v_out), (s_gate, w_gate), (s_up, w_up), (s_down, w_down))
    own = [copy(source, target.at[index]) for source, target in pairs]
    pl.semaphore_wait(barrier, 4)
    ring.queue([0, 1])
    ring.queue([2, 3, 4])
    ring.queue([5, 6])
    ring.queue([7, 8])
    whole.wait()
    ring.through([0, 1])
    own[0].wait()
    own[1].wait()

    gain_one = v_qkv[:, block : block + 16, :block]
    gain_two = v_qkv[:, block : block + 16, block : 2 * block]
    gains = [[g[i, :1].astype(f32) for i in range(n)] for g in (gain_one, gain_two)]
    gain_one, gain_two = (jnp.concatenate(g, axis=1) for g in gains)

    def attention(qkv, ka, kb, va, vb):
        steps = 4
        rows_each = tok // steps
        for i in range(steps):
            rows = pl.ds(i * rows_each, rows_each)
            z = n2[rows, :].astype(f32)
            inverse = lax.rsqrt(jnp.mean(z * z, axis=-1, keepdims=True) + norm_eps)
            n1[rows, :] = (z * inverse * gain_one).astype(bf16)
            qkv[rows, :] = mm(n1[rows, :], v_qkv[:, :block].reshape(width, qkv.shape[1]))
            if i in (1, 3):
                ring.pass_on()
        attn_forward(
            qkv, cs_ref, sn_ref, start_ref, q_ref, kv_ref, ob_ref, lse_ref, ka, kb, va, vb,
            {i: ring.pass_on for i in (2, 4, 6, 8)},
        )

    pl.run_scoped(
        attention, pltpu.VMEM((tok, v_qkv.shape[2]), f32), *[pltpu.VMEM((tok, 128), bf16)] * 4
    )
    saved = [copy(n1, n1_out), copy(v_qkv, w_qkv), copy(v_out, w_out)]

    def remote(k, source, target, device):
        made = pltpu.make_async_remote_copy(
            src_ref=source, dst_ref=target, send_sem=tp_send.at[k], recv_sem=tp_recv.at[k],
            device_id={"tensor": device}, device_id_type=MESH,
        )
        made.start()
        return made

    def projected(first):
        rows = pl.ds(pl.multiple_of(first, 16), sub)
        return jnp.concatenate([mm(ob_ref[rows, :], v_out[j]) for j in range(n)], axis=1)

    pieces = [((1 - y) * quarter + i * sub) for i in (0, 1)] + [(y * quarter + i * sub) for i in (0, 1)]
    tp = []
    for i, first in enumerate(pieces):
        part[i * sub : (i + 1) * sub, :] = projected((1 - c) * 2 * quarter + first).astype(bf16)
        tp.append(remote(i, part.at[pl.ds(i * sub, sub)], near.at[pl.ds(i * sub, sub)], mate))
    for i, first in enumerate(pieces):
        mine = projected(c * 2 * quarter + first)
        tp[i].wait_recv()
        total = mine + near[i * sub : (i + 1) * sub, :].astype(f32)
        if i < 2:
            far_part[i * sub : (i + 1) * sub, :] = total.astype(bf16)
            tp.append(remote(4 + i, far_part.at[pl.ds(i * sub, sub)], far.at[pl.ds(i * sub, sub)], across))
        else:
            keep[(i - 2) * sub : (i - 1) * sub, :] = total
        if i == 1:
            ring.pass_on()

    first_row = (2 * c + y) * quarter
    token_rows = copy(tokens.at[pl.ds(pl.multiple_of(first_row, 16), quarter)], own_n2)
    token_rows.wait()
    sent = []
    for i in (0, 1):
        rows = pl.ds(i * sub, sub)
        ring.pass_on(3)
        tp[4 + i].wait_recv()
        hidden = own_n2[rows, :].astype(f32) + keep[rows, :] + far[rows, :].astype(f32)
        hid_ref[rows, :] = hidden
        inverse = lax.rsqrt(jnp.mean(hidden * hidden, axis=-1, keepdims=True) + norm_eps)
        place = pl.ds(pl.multiple_of(first_row + i * sub, 16), sub)
        n2[place, :] = (hidden * inverse * gain_two).astype(bf16)
        sent.append(remote(6 + i, n2.at[place], n2.at[place], across))
        sent.append(remote(8 + i, n2.at[place], n2.at[place], mate))
    saved[0].wait()
    cot_load = copy(cotangent, n1)
    other_row = (2 * c + 1 - y) * quarter
    for i in (0, 1):
        ring.pass_on(3)
        sent[2 * i].wait_recv()
        place = pl.ds(pl.multiple_of(other_row + i * sub, 16), sub)
        sent.append(remote(10 + i, n2.at[place], n2.at[place], mate))
    for made in (sent[1], sent[3], sent[4], sent[5]):
        made.wait_recv()
    saved.append(copy(n2, n2_out))
    ring.through([2, 3, 4])
    cot_load.wait()
    for made in own[2:]:
        made.wait()
    per = 256 // block
    chunks = width // 256

    def feed_forward(weight, stage, inner, dg, du, blocks, sums, grads):
        tiles = [(first, min(256, units - first)) for first in range(0, units, 256)]
        before = early // 256

        def load(j):
            first, wide = tiles[j]
            sources = (w_gate, w_up, w_down) if j < before else (w_gate, w_up)
            return [
                copy(source.at[:, :, pl.ds(first, wide)], weight.at[j % 2, k, :, :, pl.ds(0, wide)])
                for k, source in enumerate(sources)
            ]

        def tile(j, k, rows):
            wide = tiles[j][1]
            return mm(rows[...], weight[j % 2, k, :, :, :wide].reshape(width, wide))

        def gated(j):
            first, wide = tiles[j]
            gate, up = tile(j, 0, n2), tile(j, 1, n2)
            sig = jax.nn.sigmoid(gate)
            silu = gate * sig
            inner[:, first : first + wide] = (silu * up).astype(bf16)
            return up * (sig * (1.0 + gate * (1.0 - sig))), silu

        def weight_grads(target, rows, right, calls):
            cols = right.shape[1]
            writes = []
            for j in range(chunks):
                if j >= 2:
                    writes[j - 2].wait()
                grad = mm_tn(rows[:, j * 256 : (j + 1) * 256], right[...]).astype(bf16)
                grads[j % 2, :, :, :cols] = grad.reshape(per, block, cols)
                writes.append(copy(grads.at[j % 2, :, :, pl.ds(0, cols)], target.at[pl.ds(j * per, per)]))
                if j in calls:
                    ring.pass_on()
            writes[-2].wait()
            writes[-1].wait()

        loads = [load(0)]
        for j in range(before):
            if j + 1 < before:
                loads.append(load(j + 1))
            for made in loads[j]:
                made.wait()
            to_gate, to_up = gated(j)
            ring.pass_on()
            first, wide = tiles[j]
            grad = tile(j, 2, n1)
            dg[:, first : first + wide] = (grad * to_gate).astype(bf16)
            du[:, first : first + wide] = (grad * to_up).astype(bf16)
            ring.pass_on()

        def block_load(j):
            return [
                copy(s.at[pl.ds(j * per, per), :, pl.ds(0, early)], blocks.at[j % 2, k])
                for k, s in enumerate((w_gate, w_up))
            ]

        loads = [block_load(0)]
        writes = []
        for j in range(chunks):
            if j + 1 < chunks:
                loads.append(block_load(j + 1))
            for made in loads[j]:
                made.wait()
            if j >= 2:
                writes[j - 2].wait()
            value = mm_nt(dg[...], blocks[j % 2, 0].reshape(256, early))
            sums[j % 2] = value + mm_nt(du[...], blocks[j % 2, 1].reshape(256, early))
            writes.append(copy(sums.at[j % 2], dn2_out.at[j]))
            ring.pass_on()
        for made in writes[-2:]:
            made.wait()
        early_writes = [copy(dg, dg_out), copy(du, du_out)]
        ring.through([5, 6])
        loads = {before: load(before)}
        writes = []
        for j in range(before, len(tiles)):
            if j + 1 < len(tiles):
                loads[j + 1] = load(j + 1)
            for made in loads[j]:
                made.wait()
            first, wide = tiles[j]
            for k, value in enumerate(gated(j)):
                if len(writes) >= 4:
                    writes[-4].wait()
                stage[j % 2, k, :, :wide] = value.astype(bf16)
                target = (to_gate_out, to_up_out)[k]
                writes.append(copy(stage.at[j % 2, k, :, pl.ds(0, wide)], target.at[:, pl.ds(first - early, wide)]))
            ring.pass_on(2)
        for made in writes[-4:]:
            made.wait()
        inner_write = copy(inner, inner_out)
        weight_grads(grad_down, n1, inner, range(chunks))
        inner_write.wait()
        for made in early_writes:
            made.wait()

    pl.run_scoped(
        feed_forward,
        pltpu.VMEM((2, 3, n, block, 256), bf16),
        pltpu.VMEM((2, 2, tok, 256), bf16),
        pltpu.VMEM((tok, units), bf16),
        pltpu.VMEM((tok, early), bf16),
        pltpu.VMEM((tok, early), bf16),
        pltpu.VMEM((2, 2, per, block, early), bf16),
        pltpu.VMEM((2, tok, 256), f32),
        pltpu.VMEM((2, per, block, units), bf16),
    )
    ring.pass_on(len(ring.events))
    for made in sent:
        made.wait_send()
    for made in tp:
        made.wait_send()
    ring.finish()
    for made in saved[1:]:
        made.wait()


def to_early(units):
    return (units // 256 + 1) // 2 * 256


def forward(n, s_qkv, s_out, s_gate, s_up, s_down, tokens, cotangent, cs, sn, start):
    tok, width = tokens.shape
    heads = s_qkv.shape[1] - 128
    units = s_gate.shape[1]
    early = to_early(units)
    quarter = tok // 4
    vm = pl.BlockSpec(memory_space=pltpu.VMEM)
    anywhere = pl.BlockSpec(memory_space=pl.ANY)
    shards = (s_qkv, s_out, s_gate, s_up, s_down)
    return pl.pallas_call(
        functools.partial(forward_kernel, n),
        out_shape=tuple(jax.ShapeDtypeStruct((n,) + s.shape, bf16) for s in shards)
        + (
            jax.ShapeDtypeStruct((tok, width), bf16),
            jax.ShapeDtypeStruct((tok, heads), bf16),
            jax.ShapeDtypeStruct((tok, 128), bf16),
            jax.ShapeDtypeStruct((tok, heads), bf16),
            jax.ShapeDtypeStruct((heads // HD, tok), f32),
            jax.ShapeDtypeStruct((quarter, width), f32),
            jax.ShapeDtypeStruct((tok, width), bf16),
            jax.ShapeDtypeStruct((tok, units - early), bf16),
            jax.ShapeDtypeStruct((tok, units - early), bf16),
            jax.ShapeDtypeStruct((tok, units), bf16),
            jax.ShapeDtypeStruct((n, width // n, units), bf16),
            jax.ShapeDtypeStruct((tok, early), bf16),
            jax.ShapeDtypeStruct((tok, early), bf16),
            jax.ShapeDtypeStruct((width // 256, tok, 256), f32),
        ),
        in_specs=[anywhere] * 7 + [vm] * 3,
        out_specs=(anywhere,) * 6 + (vm,) * 5 + (anywhere,) * 8,
        scratch_shapes=[
            pltpu.VMEM((n,) + s_qkv.shape, bf16),
            pltpu.VMEM((n,) + s_out.shape, bf16),
            pltpu.VMEM((tok, width), bf16),
            pltpu.VMEM((tok, width), bf16),
            pltpu.VMEM((2 * quarter, width), bf16),
            pltpu.VMEM((2 * quarter, width), bf16),
            pltpu.VMEM((quarter, width), f32),
            pltpu.VMEM((quarter, width), bf16),
            pltpu.VMEM((quarter, width), bf16),
            pltpu.VMEM((quarter, width), bf16),
            pltpu.SemaphoreType.DMA((9, 2, n - 1)),
            pltpu.SemaphoreType.DMA((9, 2, n - 1)),
            pltpu.SemaphoreType.DMA((12,)),
            pltpu.SemaphoreType.DMA((12,)),
            pltpu.SemaphoreType.DMA((128,)),
        ],
        compiler_params=pltpu.CompilerParams(collective_id=1, has_side_effects=True, vmem_limit_bytes=62 * 2**20),
    )(*shards, tokens, cotangent, cs, sn, start)


class Later:
    def __init__(self, make):
        self.make = make

    def start(self):
        self.make().start()

    def wait(self):
        self.make().wait()

    def wait_send(self):
        self.make().wait_send()

    def wait_recv(self):
        self.make().wait_recv()


class Reduce:
    def __init__(self, n, chains, pools, send, recv, slot_sem, term_sem):
        self.n, self.chains, self.pools = n, chains, pools
        self.send_sem, self.recv_sem = send, recv
        self.slot_sem, self.term_sem = slot_sem, term_sem
        self.place = ring_place(n, lax.axis_index("dp"))
        self.up = ring_index(n, self.place + 1)
        self.down = ring_index(n, self.place - 1)
        self.origin = [
            [ring_index(n, self.place - 1 - step), ring_index(n, self.place + 1 + step)] for step in range(n)
        ]
        self.events, self.groups, self.waiting, self.used = [], [], [], [0] * len(pools)
        self.busy = [{} for _ in pools]
        self.ready = self.pending = None

    def send(self, chain, step, way, source):
        return Later(
            lambda: pltpu.make_async_remote_copy(
                src_ref=source(),
                dst_ref=self.landing(chain, step, way),
                send_sem=self.send_sem.at[chain, way, step],
                recv_sem=self.recv_sem.at[chain, way, step],
                device_id={"dp": self.up if way == 0 else self.down},
                device_id_type=MESH,
            )
        )

    def landing(self, chain, step, way):
        (slots, first), rows = self.chains[chain][2], self.chains[chain][3 + way]
        return slots.at[first + (step, way, pl.ds(0, rows[1]))]

    def term(self, chain, step, way):
        terms, cols = self.chains[chain][:2]
        rows = pl.ds(*self.chains[chain][3 + way])
        cols = () if cols is None else (pl.ds(*cols),)
        return terms.at[(self.origin[step][way], rows) + cols]

    def part(self, chain, way):
        cols = self.chains[chain][1]
        return (pl.ds(0, self.chains[chain][3 + way][1]),) + (() if cols is None else (pl.ds(0, cols[1]),))

    def start(self, chain):
        for way in (0, 1):
            made = self.send(chain, 0, way, functools.partial(self.term, chain, 0, way))
            made.start()
            self.waiting.append(made)

    def queue(self, chains):
        self.groups.append(chains)
        self.begin()

    def add(self, chain, events=None):
        self.start(chain)
        if events is None:
            before, after, self.events = self.events, [(chain, step) for step in range(self.n - 1)], []
            while before:
                self.events += before[:1] + after[:1]
                before, after = before[1:], after[1:]
            events = after
        self.events += events
        self.fetch()

    def begin(self):
        if self.groups and len(self.events) <= 4:
            chains = self.groups.pop(0)
            for chain in chains:
                self.start(chain)
            self.events += [(chain, step) for step in range(self.n - 1) for chain in chains]
            self.fetch()

    def fetch(self):
        if self.ready is not None or not self.events:
            return
        chain, step = self.events[0]
        pool = self.chains[chain][5]
        arrived, terms = self.pools[pool]
        slot = self.used[pool] % arrived.shape[0]
        self.used[pool] += 1
        for made in self.busy[pool].pop(slot, ()):
            made.wait_send()
        copies = []
        for way in (0, 1):
            copies.append(
                Later(
                    lambda way=way: pltpu.make_async_copy(
                        self.term(chain, step + 1, way),
                        terms.at[(slot, way) + self.part(chain, way)],
                        self.term_sem.at[pool, slot, way],
                    )
                )
            )
            copies[-1].start()
        self.ready = (slot, copies)

    def held(self, chain, way, slot):
        return self.pools[self.chains[chain][5]][0].at[(slot, way) + self.part(chain, way)]

    def pass_on(self, count=1):
        for _ in range(count):
            if not self.events:
                return
            self.flush()
            chain, step = self.events.pop(0)
            pool = self.chains[chain][5]
            slot, copies = self.ready
            self.ready = None
            loads = []
            for way in (0, 1):
                self.send(chain, step, way, functools.partial(self.landing, chain, step, way)).wait_recv()
                loads.append(self.load(chain, step, way, pool, slot))
                loads[-1].start()
            self.pending = (chain, step, slot, copies, loads)
            self.fetch()
            self.begin()

    def load(self, chain, step, way, pool, slot):
        return Later(
            lambda: pltpu.make_async_copy(
                self.landing(chain, step, way), self.held(chain, way, slot), self.slot_sem.at[pool, slot, way]
            )
        )

    def flush(self):
        if self.pending is None:
            return
        chain, step, slot, copies, loads = self.pending
        self.pending = None
        pool, result = self.chains[chain][5:]
        arrived, terms = self.pools[pool]
        sent = []
        for way in (0, 1):
            loads[way].wait()
            copies[way].wait()
            place = (slot, way) + self.part(chain, way)
            total = arrived[place].astype(f32) + terms[place].astype(f32)
            if step + 1 < self.n - 1:
                arrived[place] = total.astype(arrived.dtype)
                sent.append(self.send(chain, step + 1, way, functools.partial(self.held, chain, way, slot)))
                sent[-1].start()
            else:
                result(way, total)
        self.busy[pool][slot] = sent

    def turn(self, due):
        if due:
            self.pass_on()
        else:
            self.flush()

    def hop(self, due=True):
        if due:
            self.pass_on()
            self.flush()

    def drain(self):
        while self.events or self.groups:
            self.pass_on()
        self.flush()

    def finish(self):
        for busy in self.busy:
            for sent in busy.values():
                for made in sent:
                    made.wait_send()
        for made in self.waiting:
            made.wait_send()


def backward_kernel(
    n,
    g_hbm, n2_hbm, n1_hbm, x_hbm, to_gate, to_up, inner_hbm, grad_down, early_dg, early_du, early_dn2,
    w_qkv, w_out, w_gate, w_up, w_down, q_hbm, kv_hbm, ob_hbm, hid_ref, lse_ref, cs_ref, sn_ref, start_ref,
    output, grad_x, r_down, r_gate, r_up, r_out, r_qkv, r_gain,
    grad_gate, grad_up, grad_out, grad_qkv, grad_gain, l_down, l_gate, l_up, l_out, l_qkv, l_gain,
    tile, part, near, far_part, far, keep, dh, gh, rows_in, own_rows, dqkv, stage, stage_o, fin, fin_o, fin_q, gain_sum,
    pool_a, pool_b, pool_c, pool_d, pool_e, pool_f, pool_g, pool_h, gain_rows, gain_in, gain_tile, gain_out,
    ring_send, ring_recv, slot_sem, term_sem, tp_send, tp_recv, credit, local,
):
    tok, width = dh.shape
    block = width // n
    per = 256 // block
    chunks = width // 256
    units = w_gate.shape[2]
    heads = ob_hbm.shape[1]
    quarter = tok // 4
    sub = quarter // 2
    h = block // 2
    ho = heads // 2
    t = lax.axis_index("tensor")
    c, y = t % 2, t // 2
    mate = y * 2 + (1 - c)
    across = (1 - y) * 2 + c
    diagonal = (1 - y) * 2 + (1 - c)
    first_row = (2 * c + y) * quarter
    other_row = (2 * c + 1 - y) * quarter
    count = [0, 0]

    def rows_at(first, rows):
        return pl.ds(pl.multiple_of(first, 16), rows)

    own_rows_at = rows_at(first_row, quarter)
    own_subs = [rows_at(first_row + i * sub, sub) for i in (0, 1)]
    other_subs = [rows_at(other_row + i * sub, sub) for i in (0, 1)]
    sent_half = rows_at((1 - c) * 2 * quarter, 2 * quarter)
    sent_tile, kept_tile = (rows_at((2 * c + at) * quarter, quarter) for at in (1 - y, y))
    sent_quarter, kept_quarter = rows_at((1 - y) * quarter, quarter), rows_at(y * quarter, quarter)

    def now(place):
        return place() if callable(place) else place

    def copy(source, target):
        k = count[0]
        count[0] += 1
        made = Later(lambda: pltpu.make_async_copy(now(source), now(target), local.at[k]))
        made.start()
        return made

    def remote(source, target, device):
        k = count[1]
        count[1] += 1
        return Later(
            lambda: pltpu.make_async_remote_copy(
                src_ref=now(source), dst_ref=now(target), send_sem=tp_send.at[k], recv_sem=tp_recv.at[k],
                device_id={"tensor": device}, device_id_type=MESH,
            )
        )

    def to(result, buffer, writes, firsts, cols=None):
        def write(way, total):
            if len(writes) >= 2:
                writes[-2].wait()
            rows = pl.ds(0, total.shape[0])
            slot = len(writes) % 2
            lanes = () if cols is None else (pl.ds(0, cols[1]),)
            buffer[(slot, rows) + lanes] = total
            target = (pl.ds(firsts[way], total.shape[0]),) + (() if cols is None else (pl.ds(*cols),))
            writes.append(copy(lambda: buffer.at[(slot, rows) + lanes], lambda: result.at[target]))

        return write

    early = to_early(units)
    def gain_done(way, total):
        if way == 0:
            gain_sum[...] = total

    written = [[], [], []]
    chains = [
        (grad_down, None, (l_down, (0,)), (0, h // 2), (h, h // 2), 0, to(r_down, fin, written[0], (0, h))),
        (
            grad_down, None, (l_down, (1,)), (h // 2, h // 2), (h + h // 2, h // 2), 0,
            to(r_down, fin, written[0], (h // 2, h + h // 2)),
        ),
        (grad_gate, None, (l_gate, ()), (0, h), (h, h), 0, to(r_gate, fin, written[0], (0, h))),
        (grad_up, None, (l_up, ()), (0, h), (h, h), 0, to(r_up, fin, written[0], (0, h))),
        (grad_out, None, (l_out, ()), (0, ho), (ho, ho), 1, to(r_out, fin_o, written[1], (0, ho))),
        (grad_qkv, None, (l_qkv, ()), (0, h), (h, h), 2, to(r_qkv, fin_q, written[2], (0, h))),
        (grad_gain, None, (l_gain, ()), (0, 8), (8, 8), 3, gain_done),
    ]
    pools = [(pool_a, pool_b), (pool_c, pool_d), (pool_e, pool_f), (pool_g, pool_h)]
    ring = Reduce(n, chains, pools, ring_send, ring_recv, slot_sem, term_sem)
    barrier = pltpu.get_barrier_semaphore()
    for device in ({"dp": ring.up}, {"dp": ring.down}, {"tensor": mate}, {"tensor": across}, {"tensor": diagonal}):
        pl.semaphore_signal(barrier, inc=1, device_id=device, device_id_type=MESH)
    gain_load = copy(w_qkv.at[:, pl.ds(block, 16)], gain_tile)

    def gain(k):
        parts = [gain_tile[i, :1, k * block : (k + 1) * block].astype(f32) for i in range(n)]
        return jnp.concatenate(parts, axis=1)

    class Sum:
        def __init__(self, at_once=True):
            self.near, self.far, self.at_once = [], [], at_once

        def put(self, j, value):
            tile[j % 2] = value
            part[j] = tile[j % 2, sent_half, :].astype(bf16)
            self.near.append(remote(lambda: part.at[j], lambda: near.at[j], mate))
            self.near[j].start()
            if j > 0:
                self.absorb(j - 1)
            if j == chunks - 1:
                self.absorb(j)

        def absorb(self, j):
            self.near[j].wait_recv()
            far_part[j] = (tile[j % 2, sent_tile, :] + near[j, sent_quarter, :].astype(f32)).astype(bf16)
            keep[:, j * 256 : (j + 1) * 256] = tile[j % 2, kept_tile, :] + near[j, kept_quarter, :].astype(f32)
            self.far.append(remote(lambda: far_part.at[j], lambda: far.at[j], across))
            if self.at_once:
                self.far[j].start()

        def send_far(self):
            for made in self.far:
                made.start()
            self.at_once = True

        def finish(self, due=()):
            for j in range(chunks):
                ring.turn(j in due)
                self.far[j].wait_recv()
                keep[:, j * 256 : (j + 1) * 256] += far[j].astype(f32)
            for made in self.near + self.far:
                made.wait_send()

    class Spread:
        def __init__(self, whole):
            self.whole, self.far, self.near, self.last = whole, [], [], []

        def put(self, i, source):
            place = lambda: self.whole.at[own_subs[i]]
            self.far.append(remote(source, place, across))
            self.far[i].start()
            self.near.append(remote(source, place, mate))
            self.near[i].start()

        def forward(self, calls):
            for i in (0, 1):
                ring.pass_on(calls[i])
                ring.flush()
                self.far[i].wait_recv()
                place = lambda i=i: self.whole.at[other_subs[i]]
                self.last.append(remote(place, place, mate))
                self.last[i].start()

        def arrive_near(self):
            for made in self.near:
                made.wait_recv()

        def arrive(self):
            for made in self.last:
                made.wait_recv()

        def close(self):
            for made in self.far + self.near + self.last:
                made.wait_send()

    def through_norm(values, gain, base, put):
        gain_grad = 0.0
        for i in (0, 1):
            rows = slice(i * sub, (i + 1) * sub)
            z = values[rows, :].astype(f32)
            inverse = lax.rsqrt(jnp.mean(z * z, axis=-1, keepdims=True) + norm_eps)
            scaled = z * inverse
            grad = keep[rows, :]
            gain_grad = gain_grad + jnp.sum(grad * scaled, axis=0, keepdims=True)
            grad = grad * gain
            grad = inverse * (grad - scaled * jnp.mean(grad * scaled, axis=-1, keepdims=True))
            put(i, rows, base[rows, :].astype(f32) + grad)
        return gain_grad

    def weight_grads(target, left, right):
        writes = []
        cols = right.shape[1]
        for j in range(chunks):
            if j >= 2:
                writes[j - 2].wait()
            grad = mm_tn(left[:, j * 256 : (j + 1) * 256], right[...]).astype(bf16)
            stage[j % 2, :, :, :cols] = grad.reshape(per, block, cols)
            writes.append(copy(stage.at[j % 2, :, :, pl.ds(0, cols)], target.at[pl.ds(j * per, per)]))
            yield j
        writes[-2].wait()
        writes[-1].wait()

    hid_sum, out_sum, x_sum = Sum(), Sum(False), Sum()
    spread, result, last = Spread(dh), Spread(output), Spread(grad_x)
    gain_rows[...] = jnp.zeros_like(gain_rows)

    def feed_forward(acts, dg, du, weight, sums, wtile):
        late = units - early
        tiles = [(first, min(256, units - first)) for first in range(early, units, 256)]

        def tile_load(j):
            first, wide = tiles[j]
            return copy(w_down.at[:, :, pl.ds(first, wide)], wtile.at[j % 2, :, :, pl.ds(0, wide)])

        def late_load(j):
            made = [
                copy(s.at[pl.ds(j * per, per), :, pl.ds(early, late)], weight.at[j % 2, k, :, :, pl.ds(0, late)])
                for k, s in enumerate((w_gate, w_up))
            ]
            return made + [copy(early_dn2.at[j], sums.at[j % 2])]

        def block_load(j):
            return copy(w_down.at[pl.ds(j * per, per)], weight.at[j % 2, 0])

        acts_load = copy(g_hbm, acts)
        tile_loads = [tile_load(0)]
        factors = [copy(to_gate, dg.at[:, pl.ds(early, late)]), copy(to_up, du.at[:, pl.ds(early, late)])]
        loads = [late_load(0)]
        row_load = copy(g_hbm.at[own_rows_at], rows_in)
        firsts = [copy(early_dg, dg.at[:, pl.ds(0, early)]), copy(early_du, du.at[:, pl.ds(0, early)])]
        pl.semaphore_wait(barrier, 5)
        ring.queue([0, 1])
        acts_load.wait()
        for j, (first, wide) in enumerate(tiles):
            if j + 1 < len(tiles):
                tile_loads.append(tile_load(j + 1))
            tile_loads[j].wait()
            grad = mm(acts[...], wtile[j % 2, :, :, :wide].reshape(width, wide))
            if j == 0:
                for made in factors:
                    made.wait()
            cols = slice(first, first + wide)
            dg[:, cols] = (grad * dg[:, cols].astype(f32)).astype(bf16)
            du[:, cols] = (grad * du[:, cols].astype(f32)).astype(bf16)
            ring.hop(j > 0)
        for j in range(chunks):
            if j + 1 < chunks:
                loads.append(late_load(j + 1))
            if j == 0:
                acts_load = copy(n2_hbm, acts)
            for made in loads[j]:
                made.wait()

            value = mm_nt(dg[:, early:], weight[j % 2, 0, :, :, :late].reshape(256, late))
            value = value + mm_nt(du[:, early:], weight[j % 2, 1, :, :, :late].reshape(256, late))
            hid_sum.put(j, value + sums[j % 2])
            ring.hop(j % 3 != 2)
        loads = [block_load(0)]
        acts_load.wait()
        for made in firsts:
            made.wait()
        def put(i, rows, grad):
            gh[rows, :] = grad
            place = own_subs[i]
            dh[place, :] = grad.astype(bf16)
            spread.put(i, lambda: dh.at[place])

        for j in weight_grads(grad_gate, acts, dg):
            ring.hop(j in (1, 4, 6))
            if j == 3:
                gain_load.wait()
                row_load.wait()
                hid_sum.finish()
                gain_rows[1:2, :] = through_norm(hid_ref, gain(1), rows_in, put)
                ring.hop()
        inner_load = copy(inner_hbm, dg)
        ring.add(2, [(2, 0), (2, 1)])
        for j in weight_grads(grad_up, acts, du):
            ring.turn(j in (1, 3, 6))
        steps = n - 1
        ring.add(3, [pair for s in range(steps) for pair in ((3, s), (2, s + 2)) if pair[1] < steps])
        spread.arrive_near()
        inner_load.wait()
        for j in range(chunks):
            if j + 1 < chunks:
                loads.append(block_load(j + 1))
            loads[j].wait()
            out_sum.put(j, mm_nt(dg[...], weight[j % 2, 0].reshape(256, units)))
            ring.turn(j in (1, 3, 5))
            if j == 6:
                spread.forward((1, 0))
                out_sum.send_far()

    pl.run_scoped(
        feed_forward,
        pltpu.VMEM((tok, width), bf16),
        pltpu.VMEM((tok, units), bf16),
        pltpu.VMEM((tok, units), bf16),
        pltpu.VMEM((2, 2, per, block, units), bf16),
        pltpu.VMEM((2, tok, 256), f32),
        pltpu.VMEM((2, n, block, 256), bf16),
    )
    ring.turn(True)
    spread.arrive()
    ring.turn(False)

    def attention(q, kv, ob, v_out, v_qkv, dob, ka, kb, va, vb, dk, dv):
        pairs = ((w_out, v_out), (q_hbm, q), (kv_hbm, kv), (w_qkv, v_qkv), (ob_hbm, ob))
        loads = [copy(source, target) for source, target in pairs]
        loads[0].wait()
        for i in (0, 1):
            rows = slice(2 * i * quarter, 2 * (i + 1) * quarter)
            total = 0.0
            for j in range(n):
                total = total + mm_nt(dh[rows, j * block : (j + 1) * block], v_out[j])
            dob[rows, :] = total.astype(bf16)
        loads[1].wait()
        loads[2].wait()
        attn_backward(
            q, kv, dob, lse_ref, cs_ref, sn_ref, start_ref, dqkv, ka, kb, va, vb, dk, dv,
            {i: functools.partial(ring.turn, i in (1, 3, 6, 8)) for i in range(tok // QB)},
        )
        out_sum.finish()
        own_rows[...] = (hid_ref[...] + keep[...]).astype(bf16)
        for k, device in enumerate((mate, across)):
            pl.semaphore_signal(credit.at[k], inc=1, device_id={"tensor": device}, device_id_type=MESH)
        loads[3].wait()
        loads[4].wait()
        pl.semaphore_wait(credit.at[0], 1)
        pl.semaphore_wait(credit.at[1], 1)
        for j in range(chunks):
            weight = v_qkv[j * per : (j + 1) * per, :block].reshape(256, heads + 128)
            x_sum.put(j, mm_nt(dqkv[...], weight))
            ring.turn(j in (2, 6))
        writes = []
        for j in range(n):
            if j >= 2:
                writes[j - 2].wait()
            stage_o[j % 2] = mm_tn(ob[...], dh[:, j * block : (j + 1) * block]).astype(bf16)
            writes.append(copy(stage_o.at[j % 2], grad_out.at[j]))
            ring.turn(j in (2, n - 2))
        writes[-2].wait()
        writes[-1].wait()

    row_load = copy(x_hbm.at[own_rows_at], rows_in)
    pl.run_scoped(
        attention,
        pltpu.VMEM((tok, heads), bf16),
        pltpu.VMEM((tok, 128), bf16),
        pltpu.VMEM((tok, heads), bf16),
        pltpu.VMEM((n, heads, block), bf16),
        pltpu.VMEM((n, block + 16, heads + 128), bf16),
        pltpu.VMEM((tok, heads), bf16),
        *[pltpu.VMEM((tok, 128), bf16)] * 4,
        *[pltpu.VMEM((tok, 128), f32)] * 2,
    )
    owns = [copy(own_rows, output.at[own_rows_at])]

    def projections(acts):
        copy(n1_hbm, acts).wait()
        for j in weight_grads(grad_qkv, acts, dqkv):
            ring.turn(j in (2, 6))
            if j == 2:
                for i in (0, 1):
                    result.put(i, lambda i=i: own_rows.at[pl.ds(i * sub, sub)])

    pl.run_scoped(projections, pltpu.VMEM((tok, width), bf16))
    ring.queue([4, 5])
    row_load.wait()
    x_sum.finish((1, 4, 7))

    def put(i, rows, grad):
        rows_in[rows, :] = grad.astype(bf16)
        last.put(i, lambda: rows_in.at[pl.ds(i * sub, sub)])

    gain_rows[0:1, :] = through_norm(rows_in, gain(0), gh, put)
    owns.append(copy(rows_in, grad_x.at[own_rows_at]))
    for i in range(n):
        both = [gain_rows[k : k + 1, i * block : (i + 1) * block] for k in (0, 1)]
        gain_out[i] = jnp.broadcast_to(jnp.concatenate(both, axis=1), (16, 2 * block))
    copy(gain_out, grad_gain).wait()
    ring.turn(True)
    ring.add(6)
    result.forward((1, 3))
    last.forward((4, 4))
    ring.drain()
    gain_in[t] = gain_sum[...]
    shares = [remote(gain_sum, gain_in.at[t], device) for device in (mate, across, diagonal)]
    for made in shares:
        made.start()
    for made in shares:
        made.wait()
    gain_sum[...] = (gain_in[0] + gain_in[1]) + (gain_in[2] + gain_in[3])
    owns.append(copy(gain_sum, r_gain))
    for spreading in (result, last):
        spreading.arrive_near()
        spreading.arrive()
    for spreading in (spread, result, last):
        spreading.close()
    ring.finish()
    for made in owns:
        made.wait()
    for writes in written:
        for made in writes[-2:]:
            made.wait()


def backward(n, g, n2, n1, x, to_gate, to_up, inner, grads, w_qkv, w_out, w_gate, w_up, w_down, q, kv, ob, hid, lse, cs, sn, start):
    tok, width = x.shape
    block = width // n
    h = block // 2
    heads, units = ob.shape[1], inner.shape[1]
    quarter = tok // 4
    per, chunks = 256 // block, width // 256
    vm = pl.BlockSpec(memory_space=pltpu.VMEM)
    anywhere = pl.BlockSpec(memory_space=pl.ANY)
    hbm = jax.ShapeDtypeStruct
    qkv = heads + 128
    return pl.pallas_call(
        functools.partial(backward_kernel, n),
        out_shape=(
            hbm((tok, width), bf16),
            hbm((tok, width), bf16),
            hbm((block, units), f32),
            hbm((block, units), f32),
            hbm((block, units), f32),
            hbm((heads, block), f32),
            hbm((block, qkv), f32),
            hbm((8, 2 * block), f32),
            hbm((n, block, units), bf16),
            hbm((n, block, units), bf16),
            hbm((n, heads, block), bf16),
            hbm((n, block, qkv), bf16),
            hbm((n, 16, 2 * block), f32),
            hbm((2, n - 1, 2, h // 2, units), bf16),
            hbm((n - 1, 2, h, units), bf16),
            hbm((n - 1, 2, h, units), bf16),
            hbm((n - 1, 2, heads // 2, block), bf16),
            hbm((n - 1, 2, h, qkv), bf16),
            hbm((n - 1, 2, 8, 2 * block), f32),
        ),
        in_specs=[anywhere] * 19 + [vm] * 5,
        out_specs=(anywhere,) * 19,
        scratch_shapes=[
            pltpu.VMEM((2, tok, 256), f32),
            pltpu.VMEM((chunks, 2 * quarter, 256), bf16),
            pltpu.VMEM((chunks, 2 * quarter, 256), bf16),
            pltpu.VMEM((chunks, quarter, 256), bf16),
            pltpu.VMEM((chunks, quarter, 256), bf16),
            pltpu.VMEM((quarter, width), f32),
            pltpu.VMEM((tok, width), bf16),
            pltpu.VMEM((quarter, width), f32),
            pltpu.VMEM((quarter, width), bf16),
            pltpu.VMEM((quarter, width), bf16),
            pltpu.VMEM((tok, qkv), bf16),
            pltpu.VMEM((2, per, block, units), bf16),
            pltpu.VMEM((2, heads, block), bf16),
            pltpu.VMEM((2, h, units), f32),
            pltpu.VMEM((2, heads // 2, block), f32),
            pltpu.VMEM((2, h, qkv), f32),
            pltpu.VMEM((8, 2 * block), f32),
            pltpu.VMEM((3, 2, h, units), bf16),
            pltpu.VMEM((3, 2, h, units), bf16),
            pltpu.VMEM((2, 2, heads // 2, block), bf16),
            pltpu.VMEM((2, 2, heads // 2, block), bf16),
            pltpu.VMEM((2, 2, h, qkv), bf16),
            pltpu.VMEM((2, 2, h, qkv), bf16),
            pltpu.VMEM((2, 2, 8, 2 * block), f32),
            pltpu.VMEM((2, 2, 8, 2 * block), f32),
            pltpu.VMEM((8, width), f32),
            pltpu.VMEM((4, 8, 2 * block), f32),
            pltpu.VMEM((n, 16, qkv), bf16),
            pltpu.VMEM((n, 16, 2 * block), f32),
            pltpu.SemaphoreType.DMA((7, 2, n - 1)),
            pltpu.SemaphoreType.DMA((7, 2, n - 1)),
            pltpu.SemaphoreType.DMA((4, 4, 2)),
            pltpu.SemaphoreType.DMA((4, 4, 2)),
            pltpu.SemaphoreType.DMA((80,)),
            pltpu.SemaphoreType.DMA((80,)),
            pltpu.SemaphoreType.REGULAR((2,)),
            pltpu.SemaphoreType.DMA((160,)),
        ],
        compiler_params=pltpu.CompilerParams(collective_id=2, has_side_effects=True, vmem_limit_bytes=62 * 2**20),
    )(g, n2, n1, x, to_gate, to_up, inner, *grads, w_qkv, w_out, w_gate, w_up, w_down, q, kv, ob, hid, lse, cs, sn, start)


def prep_kernel(q_ref, k_ref, v_ref, d_ref, g1_ref, g2_ref, qkv_ref, dt_ref):
    rows, cols = q_ref.shape
    qkv_ref[:rows, :cols] = q_ref[...]
    qkv_ref[:rows, cols:] = jnp.concatenate([k_ref[...], v_ref[...]], axis=1)
    qkv_ref[rows:, :] = jnp.zeros((16, qkv_ref.shape[1]), bf16)
    gains = jnp.concatenate([g1_ref[...], g2_ref[...]], axis=1).astype(f32)
    qkv_ref[rows:, : 2 * rows] = jnp.broadcast_to(gains, (16, 2 * rows)).astype(bf16)
    dt_ref[...] = jnp.transpose(d_ref[...].astype(f32)).astype(bf16)


def prep(w_query, w_key, w_value, w_down, gain_attn, gain_mlp):
    rows, cols = w_query.shape
    vm = pl.BlockSpec(memory_space=pltpu.VMEM)
    return pl.pallas_call(
        prep_kernel,
        out_shape=(
            jax.ShapeDtypeStruct((rows + 16, cols + 128), bf16),
            jax.ShapeDtypeStruct(w_down.shape[::-1], bf16),
        ),
        in_specs=[vm] * 6,
        out_specs=(vm,) * 2,
        compiler_params=pltpu.CompilerParams(vmem_limit_bytes=32 * 2**20),
    )(w_query, w_key, w_value, w_down, gain_attn.reshape(1, -1), gain_mlp.reshape(1, -1))


def per_device(
    n_dp,
    tokens,
    gain_attn,
    w_query,
    w_key,
    w_value,
    w_out,
    gain_mlp,
    w_gate,
    w_up,
    w_down,
    lengths,
    cotangent,
):
    tok, width = tokens.shape
    line = n_dp // 2
    block = width // n_dp
    cols = w_query.shape[1]
    ends = jnp.cumsum(lengths[0], dtype=jnp.int32)
    starts = ends - lengths[0]
    places = jnp.arange(tok, dtype=jnp.int32)
    inside = (places[:, None] >= starts[None, :]) & (places[:, None] < ends[None, :])
    start = jnp.sum(jnp.where(inside, starts[None, :], 0), axis=1, dtype=jnp.int32)
    freqs = rope_base ** (-jnp.arange(HD // 2, dtype=f32) * 2.0 / HD)
    angles = (places - start).astype(f32)[:, None] * freqs[None, :]
    cosine, sine = jnp.cos(angles), jnp.sin(angles)
    cs = jnp.concatenate([cosine] * 4, axis=1)
    sn = jnp.concatenate([-sine, sine, -sine, sine], axis=1)

    p_qkv, p_down = prep(w_query, w_key, w_value, w_down, gain_attn, gain_mlp)
    w_qkv, w_out_all, w_g, w_u, w_d, n1, q, kv, ob, lse, hidden, n2, to_gate, to_up, inner, *grads = forward(
        n_dp, p_qkv, w_out, w_gate, w_up, p_down, tokens, cotangent, cs, sn, start[:, None]
    )
    output, grad_tokens, s_down, s_gate, s_up, s_out, s_qkv, s_gain = backward(
        n_dp, cotangent, n2, n1, tokens, to_gate, to_up, inner, grads, w_qkv, w_out_all, w_g, w_u, w_d,
        q, kv, ob, hidden, lse, cs, sn, start[None, :]
    )[:8]
    return (
        output,
        grad_tokens.astype(f32),
        s_qkv[:, :cols],
        s_qkv[:, cols : cols + HD],
        s_qkv[:, cols + HD :],
        s_out,
        s_gate,
        s_up,
        s_down.T,
        s_gain[0, :block],
        s_gain[0, block:],
    )


def solution(mesh):
    placed = (
        P("dp", None),
        P("dp"),
        P("dp", "tensor"),
        P("dp", "tensor"),
        P("dp", "tensor"),
        P("tensor", "dp"),
        P("dp"),
        P("dp", "tensor"),
        P("dp", "tensor"),
        P("tensor", "dp"),
        P("dp", None),
        P("dp", None),
    )
    return jax.shard_map(
        functools.partial(per_device, mesh.shape["dp"]),
        mesh=mesh,
        in_specs=placed,
        out_specs=(
            P("dp", None),
            P("dp", None),
            P("dp", "tensor"),
            P("dp", "tensor"),
            P("dp", "tensor"),
            P("tensor", "dp"),
            P("dp", "tensor"),
            P("dp", "tensor"),
            P("tensor", "dp"),
            P("dp"),
            P("dp"),
        ),
        check_vma=False,
    )
```
